32 devices in a mesh: dp: 8 (over z, core), expert: 4 (over y, x).
Axes of the slice: x: 2, y: 2, z: 4, core: 2. Of those that a mesh axis runs over, the one named last changes fastest.
Arguments:
- saved_input: bfloat16 [4096, 2048], P(('dp', 'expert')), parts along dimension 0, may hold values from -6 to 6
- grad_out: bfloat16 [4096, 2048], P(('dp', 'expert')), parts along dimension 0, may hold values from -6 to 6
- routes: int32 [4096, 8], P(('dp', 'expert')), parts along dimension 0, may hold values from 0 to 15, all different within a row
- route_gates: bfloat16 [4096, 8], P(('dp', 'expert')), parts along dimension 0, may hold values from 0.049804688 to 0.5
- gate_proj: bfloat16 [16, 2048, 768], P('expert'), may hold values from -0.125 to 0.125
- up_proj: bfloat16 [16, 2048, 768], P('expert'), may hold values from -0.125 to 0.125
- down_proj: bfloat16 [16, 768, 2048], P('expert'), may hold values from -0.21875 to 0.21875
Outputs:
- grad_in: bfloat16 [4096, 2048], P(('dp', 'expert')), parts along dimension 0
The draws below stay inside these ranges and needn't reach their ends.
There are 8 independent parts, one for each index of `dp`. The reference program is written for one: setup_inputs(seed, part) draws one part's arguments, and reference() takes and returns one part's arrays. A program takes and returns all parts, laid end to end along the dimension named above; an argument that names none is the same for every part. Nothing has to cross between parts.
Inputs may be any that keep to these rules, and one draw needn't show every extreme that they name: `routes`: each token names 8 different experts, and every expert is named by some token.
All inputs are finite; a program needn't handle non-finite values.
Results may differ from the reference program's by a relative error of at most 0.0057.
Values may be sent and summed in bfloat16 or wider, within the bound.
No kernel may reach another device: no remote copies, remote signals or barrier semaphores. Data moves between devices by JAX's collectives and lax.ppermute only.
A program may use at most 128 MiB of HBM per device.

```python
import jax
import jax.numpy as jnp
from jax import lax

D = 2048
FF = 768
EXPERTS = 16
TOP = 8
TOK_DEV = 128
CAP = 56
TOKENS = 512


def block_scale(key, shape, split, low, top_value):
    loudness = 1.0
    for axis_at, blocks in split:
        draws = jax.random.uniform(jax.random.fold_in(jax.random.fold_in(key, 6), axis_at), (blocks,), jnp.float32, low / len(split), top_value / len(split))
        loudness = loudness * jnp.repeat(jnp.exp(draws), shape[axis_at] // blocks).reshape((-1,) + (1,) * (len(shape) - 1 - axis_at))
    return loudness


def different_ones(key, rows, amount, top, lift):
    sequence = jax.random.permutation(jax.random.fold_in(key, 1), amount)
    favour = sequence
    for power in range(3):
        favour = favour * favour // amount
    favour = favour * lift // amount
    chance = jax.random.randint(jax.random.fold_in(key, 2), (rows, amount), 0, 4096) + favour
    fixed_rows = jax.random.permutation(jax.random.fold_in(key, 3), rows)[jnp.arange(amount) % rows]
    chance = jnp.where(jnp.arange(rows)[:, None] == fixed_rows[None, :], 1 << 14, chance)
    score = chance * amount + jnp.arange(amount)
    return lax.top_k(score.astype(jnp.int32), top)[1].astype(jnp.int32)


def centred(own_key, extent, spread, most, pieces=(), kind=jnp.bfloat16):
    result = jax.random.normal(own_key, extent, jnp.float32) * spread
    if len(pieces) > 0:
        result = block_scale(own_key, extent, pieces, -0.22, 0.18) * result
    return jnp.clip(result, min=-most, max=most).astype(kind)


def setup_inputs(seed: int = 0, part: int = 0) -> dict:
    splits = jax.random.split(jax.random.key(seed), 8)
    own_keys = jax.random.split(jax.random.fold_in(splits[7], part), 8)
    return {
        "saved_input": centred(own_keys[0], (TOKENS, D), 1.0, 6.0, ((0, 4),)),
        "grad_out": centred(own_keys[1], (TOKENS, D), 1.0, 6.0, ((0, 4),)),
        "routes": different_ones(own_keys[2], TOKENS, EXPERTS, TOP, 4096),
        "route_gates": jnp.clip(0.049804688 + 0.4501953 * jax.random.uniform(own_keys[3], (TOKENS, TOP), jnp.float32) ** block_scale(own_keys[3], (TOKENS, TOP), ((0, 4),), -0.2, 0.2), 0.049804688, 0.5).astype(jnp.bfloat16),
        "gate_proj": centred(splits[4], (EXPERTS, D, FF), D ** -0.5, 0.125, ((0, 4),)),
        "up_proj": centred(splits[5], (EXPERTS, D, FF), D ** -0.5, 0.125, ((0, 4),)),
        "down_proj": centred(splits[6], (EXPERTS, FF, D), FF ** -0.5, 0.21875, ((0, 4),)),
    }


def pair_ranks(routing):
    groups = routing.shape[0]
    ordered = jnp.swapaxes(routing, 1, 2).reshape(groups, -1)
    labels = jnp.arange(EXPERTS, dtype=jnp.int32)
    matches = (ordered[..., None] == labels).astype(jnp.int32)
    earlier = jnp.cumsum(matches, axis=1) - matches
    ranking = jnp.sum(earlier * matches, axis=-1)
    return ordered, ranking


def expert_rows(packed):
    input_rows, grad_rows, gate_rows, gate_weight, up_weight, down_weight = packed
    gate_pre = jnp.dot(input_rows, gate_weight, preferred_element_type=jnp.float32)
    up_pre = jnp.dot(input_rows, up_weight, preferred_element_type=jnp.float32)
    back_grad = jnp.dot(grad_rows, down_weight.T, preferred_element_type=jnp.float32)
    scaled = gate_rows.astype(jnp.float32)[:, None] * back_grad
    sigmoid_gate = jax.nn.sigmoid(gate_pre)
    gate_grad = (scaled * up_pre * sigmoid_gate * (1.0 + gate_pre * (1.0 - sigmoid_gate))).astype(jnp.bfloat16)
    up_grad = (scaled * gate_pre * sigmoid_gate).astype(jnp.bfloat16)
    summed = jnp.dot(gate_grad, gate_weight.T, preferred_element_type=jnp.float32)
    summed = summed + jnp.dot(up_grad, up_weight.T, preferred_element_type=jnp.float32)
    return summed.astype(jnp.bfloat16)


def reference(saved_input, grad_out, routes, route_gates, gate_proj, up_proj, down_proj):
    groups = TOKENS // TOK_DEV
    routing = routes.reshape(groups, TOK_DEV, TOP)
    ordered, ranking = pair_ranks(routing)
    pair_index = jnp.arange(TOP * TOK_DEV, dtype=jnp.int32)
    token_local = pair_index % TOK_DEV
    choice_index = pair_index // TOK_DEV
    group_index = jnp.arange(groups, dtype=jnp.int32)[:, None]
    token_global = group_index * TOK_DEV + token_local[None, :]
    slot_total = groups * CAP
    slot_of = jnp.where(ranking < CAP, ordered * slot_total + group_index * CAP + ranking, EXPERTS * slot_total)
    flat_slot = slot_of.reshape(-1).astype(jnp.int32)
    source_row = jnp.full((EXPERTS * slot_total,), TOKENS, jnp.int32)
    source_row = source_row.at[flat_slot].set(token_global.reshape(-1).astype(jnp.int32), mode="drop")
    gate_pairs = route_gates[token_global, choice_index[None, :]]
    gate_buffer = jnp.zeros((EXPERTS * slot_total,), jnp.bfloat16)
    gate_buffer = gate_buffer.at[flat_slot].set(gate_pairs.reshape(-1), mode="drop")
    zero_row = jnp.zeros((1, D), jnp.bfloat16)
    input_rows = jnp.concatenate([saved_input, zero_row], 0)[source_row].reshape(EXPERTS, slot_total, D)
    grad_rows = jnp.concatenate([grad_out, zero_row], 0)[source_row].reshape(EXPERTS, slot_total, D)
    gate_rows = gate_buffer.reshape(EXPERTS, slot_total)
    expert_out = lax.map(expert_rows, (input_rows, grad_rows, gate_rows, gate_proj, up_proj, down_proj))
    flat_rows = jnp.concatenate([expert_out.reshape(-1, D), zero_row], 0)
    picked = flat_rows[flat_slot].reshape(groups, TOP, TOK_DEV, D)
    summed = jnp.sum(picked.astype(jnp.float32), axis=1)
    return summed.reshape(TOKENS, D).astype(jnp.bfloat16)
```

```python
import functools

import jax
import jax.numpy as jnp
from jax import lax
from jax.experimental import pallas as pl
from jax.experimental.pallas import tpu as pltpu
from jax.sharding import PartitionSpec as P

CAP = 56
SLOT = 64
UNUSED = 200.0
MIB = 1 << 20
CHUNKS = 4

NT = (((1,), (1,)), ((), ()))
TN = (((0,), (0,)), ((), ()))


def dot(a, b, dims=(((1,), (0,)), ((), ()))):
    return lax.dot_general(a, b, dims, preferred_element_type=jnp.float32)


def params(limit):
    return pltpu.CompilerParams(vmem_limit_bytes=limit * MIB)


def whole(shape):
    return pl.BlockSpec(shape, lambda *_: (0,) * len(shape))


def rank_kernel(experts, routes_ref, gates_ref, out_ref):
    tokens, top = routes_ref.shape
    chosen = routes_ref[...].astype(jnp.float32).T
    gates = gates_ref[...].astype(jnp.float32).T
    label = lax.broadcasted_iota(jnp.int32, (experts, tokens), 0).astype(jnp.float32)
    hits = [(chosen[k : k + 1, :] == label).astype(jnp.float32) for k in range(top)]
    before = lax.broadcasted_iota(jnp.int32, (tokens, tokens), 0)
    after = lax.broadcasted_iota(jnp.int32, (tokens, tokens), 1)
    earlier = (before < after).astype(jnp.bfloat16)
    base = jnp.zeros((experts, 1), jnp.float32)
    rank = jnp.zeros((experts, tokens), jnp.float32)
    taken = jnp.zeros((experts, tokens), jnp.float32)
    gate = jnp.zeros((experts, tokens), jnp.float32)
    for k in range(top):
        inside = dot(hits[k].astype(jnp.bfloat16), earlier)
        rank += hits[k] * (inside + base)
        taken += hits[k]
        gate += hits[k] * gates[k : k + 1, :]
        base += jnp.sum(hits[k], axis=1, keepdims=True)
    rank = jnp.where((taken > 0.5) & (rank < CAP), rank, UNUSED)
    out_ref[:experts, :] = rank.astype(jnp.bfloat16)
    out_ref[experts:, :] = gate.astype(jnp.bfloat16)


def rank_table(routes, gates, experts):
    tokens = routes.shape[0]
    return pl.pallas_call(
        functools.partial(rank_kernel, experts),
        out_shape=jax.ShapeDtypeStruct((2 * experts, tokens), jnp.bfloat16),
    )(routes, gates)


def pre_kernel(axis, n, local, me_of, table_ref, x_ref, wg_ref, wu_ref, a_ref, b_ref, pick_ref, xs, gcol):
    experts = n * local
    tokens = x_ref.shape[1]

    @pl.when((pl.program_id(0) == 0) & (pl.program_id(1) == 0))
    def _():
        me = lax.axis_index(axis)
        row = lax.broadcasted_iota(jnp.int32, (2 * experts, tokens), 0)
        slot = lax.broadcasted_iota(jnp.int32, (SLOT, tokens), 0).astype(jnp.float32)
        for g in range(n):
            table = table_ref[g].astype(jnp.float32)
            picks = []
            for j in range(local):
                e = me * local + j
                rank = jnp.sum(jnp.where(row == e, table, 0.0), axis=0, keepdims=True)
                gate = jnp.sum(jnp.where(row == e + experts, table, 0.0), axis=0, keepdims=True)
                pick = (slot == rank).astype(jnp.float32)
                gcol[j, g * SLOT : (g + 1) * SLOT, :] = jnp.sum(pick * gate, axis=1, keepdims=True)
                picks.append(pick.astype(jnp.bfloat16))
            pick = jnp.concatenate(picks, axis=0)
            pick_ref[g] = pick
            rows = dot(pick, x_ref[g]).astype(jnp.bfloat16)
            for j in range(local):
                xs[j, g * SLOT : (g + 1) * SLOT, :] = rows[j * SLOT : (j + 1) * SLOT, :]

    e = pl.program_id(0)
    gate_pre = dot(xs[e], wg_ref[0])
    up_pre = dot(xs[e], wu_ref[0])
    sig = jax.nn.sigmoid(gate_pre)
    weighted = gcol[e] * sig
    a_ref[0] = weighted * up_pre * (1.0 + gate_pre * (1.0 - sig))
    b_ref[0] = weighted * gate_pre


def pre(axis, n, table, x_all, wg, wu):
    local, features, hidden = wg.shape
    tokens = x_all.shape[1]
    rows = n * SLOT
    cols = hidden // 2
    weight = pl.BlockSpec((1, features, cols), lambda e, f: (e, 0, f))
    result = pl.BlockSpec((1, rows, cols), lambda e, f: (e, 0, f))
    return pl.pallas_call(
        functools.partial(pre_kernel, axis, n, local, None),
        grid=(local, hidden // cols),
        in_specs=[whole(table.shape), whole(x_all.shape), weight, weight],
        out_specs=[result, result, whole((n, local * SLOT, tokens))],
        out_shape=[
            jax.ShapeDtypeStruct((local, rows, hidden), jnp.float32),
            jax.ShapeDtypeStruct((local, rows, hidden), jnp.float32),
            jax.ShapeDtypeStruct((n, local * SLOT, tokens), jnp.bfloat16),
        ],
        scratch_shapes=[
            pltpu.VMEM((local, rows, features), jnp.bfloat16),
            pltpu.VMEM((local, rows, 1), jnp.float32),
        ],
        compiler_params=params(48),
        cost_estimate=pl.CostEstimate(
            flops=4 * local * rows * features * hidden,
            bytes_accessed=4 * local * features * hidden + 8 * local * rows * hidden,
            transcendentals=local * rows * hidden,
        ),
    )(table, x_all, wg, wu)


def back_kernel(n, local, pick_ref, g_ref, wd_ref, a_ref, b_ref, hg_ref, hu_ref, gs):
    @pl.when((pl.program_id(0) == 0) & (pl.program_id(1) == 0))
    def _():
        for g in range(n):
            rows = dot(pick_ref[g], g_ref[g]).astype(jnp.bfloat16)
            for j in range(local):
                gs[j, g * SLOT : (g + 1) * SLOT, :] = rows[j * SLOT : (j + 1) * SLOT, :]

    back = dot(gs[pl.program_id(0)], wd_ref[0], NT)
    hg_ref[0] = (back * a_ref[0]).astype(jnp.bfloat16)
    hu_ref[0] = (back * b_ref[0]).astype(jnp.bfloat16)


def back(n, pick, g_all, wd, a, b):
    local, hidden, features = wd.shape
    rows = n * SLOT
    cols = hidden // 2
    block = pl.BlockSpec((1, rows, cols), lambda e, f: (e, 0, f))
    shape = jax.ShapeDtypeStruct((local, rows, hidden), jnp.bfloat16)
    return pl.pallas_call(
        functools.partial(back_kernel, n, local),
        grid=(local, hidden // cols),
        in_specs=[
            whole(pick.shape),
            whole(g_all.shape),
            pl.BlockSpec((1, cols, features), lambda e, f: (e, f, 0)),
            block,
            block,
        ],
        out_specs=[block, block],
        out_shape=[shape, shape],
        scratch_shapes=[pltpu.VMEM((local, rows, features), jnp.bfloat16)],
        compiler_params=params(40),
        cost_estimate=pl.CostEstimate(
            flops=2 * local * rows * features * hidden,
            bytes_accessed=2 * local * features * hidden + 12 * local * rows * hidden,
            transcendentals=0,
        ),
    )(pick, g_all, wd, a, b)


def out_kernel(axis, n, local, orders, pick_ref, hg_ref, hu_ref, wg_ref, wu_ref, *rest):
    outs, rows_ref = rest[:-1], rest[-1]
    e = pl.program_id(0)
    rows = (dot(hg_ref[0], wg_ref[0], NT) + dot(hu_ref[0], wu_ref[0], NT)).astype(jnp.bfloat16)
    for g in range(n):
        rows_ref[g, e] = rows[g * SLOT : (g + 1) * SLOT, :]

    @pl.when(e == local - 1)
    def _():
        me = lax.axis_index(axis)
        for out_ref, order in zip(outs, orders):
            for i, k in enumerate(order):
                g = lax.bitwise_xor(me, k)
                part = rows_ref[g].reshape(local * SLOT, -1)
                out_ref[i] = dot(pick_ref[g], part, TN).astype(out_ref.dtype)


def partial_sums(axis, n, orders, chunk, pick, hg, hu, wg, wu):
    local, features, hidden = wg.shape
    tokens = pick.shape[2]
    rows = n * SLOT
    cols = features // CHUNKS
    act = pl.BlockSpec((1, rows, hidden), lambda e: (e, 0, 0))
    weight = pl.BlockSpec((1, cols, hidden), lambda e: (e, chunk, 0))
    shapes = [(len(order), tokens, cols) for order in orders]
    types = [jnp.float32] + [jnp.bfloat16] * (len(orders) - 1)
    return pl.pallas_call(
        functools.partial(out_kernel, axis, n, local, orders),
        grid=(local,),
        in_specs=[whole(pick.shape), act, act, weight, weight],
        out_specs=[whole(s) for s in shapes],
        out_shape=[jax.ShapeDtypeStruct(s, t) for s, t in zip(shapes, types)],
        scratch_shapes=[pltpu.VMEM((n, local, SLOT, cols), jnp.bfloat16)],
        compiler_params=params(32),
        cost_estimate=pl.CostEstimate(
            flops=4 * local * rows * cols * hidden,
            bytes_accessed=4 * local * (cols + rows) * hidden,
            transcendentals=0,
        ),
    )(pick, hg, hu, wg, wu)


def sum_kernel(*refs):
    parts, out_ref = refs[:-1], refs[-1]
    each = len(parts) // CHUNKS
    cols = out_ref.shape[1] // CHUNKS
    for c in range(CHUNKS):
        own, *others = parts[c * each : (c + 1) * each]
        total = own[0]
        for other in others:
            total += other[0].astype(jnp.float32)
        out_ref[:, c * cols : (c + 1) * cols] = total.astype(jnp.bfloat16)


def body(axis, saved_input, grad_out, routes, route_gates, gate_proj, up_proj, down_proj):
    n = lax.axis_size(axis)
    local = gate_proj.shape[0]
    experts = n * local
    tokens, features = saved_input.shape

    def swap(array, k):
        return lax.ppermute(array, axis, [(i, i ^ k) for i in range(n)])

    table = lax.all_gather(rank_table(routes, route_gates, experts), axis)
    x_all = lax.all_gather(saved_input, axis)
    g_all = lax.all_gather(grad_out, axis)
    a, b, pick = pre(axis, n, table, x_all, gate_proj, up_proj)
    hg, hu = back(n, pick, g_all, down_proj, a, b)
    parts = []
    for chunk in range(CHUNKS):
        if n == 4:
            near, far = (1, 2) if chunk % 2 == 0 else (2, 1)
            orders = ((0,), (near, 3), (far,))
            own, two, one = partial_sums(axis, n, orders, chunk, pick, hg, hu, gate_proj, up_proj)
            two = swap(two, near)
            relay = (two[1:2].astype(jnp.float32) + one.astype(jnp.float32)).astype(jnp.bfloat16)
            parts += [own, two[:1], swap(relay, far)]
        else:
            orders = tuple((k,) for k in range(n))
            own, *others = partial_sums(axis, n, orders, chunk, pick, hg, hu, gate_proj, up_proj)
            parts += [own] + [swap(other, k + 1) for k, other in enumerate(others)]
    return pl.pallas_call(
        sum_kernel,
        out_shape=jax.ShapeDtypeStruct((tokens, features), jnp.bfloat16),
        compiler_params=params(48),
    )(*parts)


def solution(mesh):
    tokens = P(("dp", "expert"), None)
    weights = P("expert", None, None)
    return jax.shard_map(
        functools.partial(body, "expert"),
        mesh=mesh,
        in_specs=(tokens, tokens, tokens, tokens, weights, weights, weights),
        out_specs=tokens,
        check_vma=False,
    )
```

```python
import functools

import jax
import jax.numpy as jnp
from jax import lax
from jax.experimental import pallas as pl
from jax.experimental.pallas import tpu as pltpu
from jax.sharding import PartitionSpec as P

CAP = 56
SLOT = 64
UNUSED = 200.0
MIB = 1 << 20
CHUNKS = 4

NT = (((1,), (1,)), ((), ()))
TN = (((0,), (0,)), ((), ()))


def dot(a, b, dims=(((1,), (0,)), ((), ()))):
    return lax.dot_general(a, b, dims, preferred_element_type=jnp.float32)


def params(limit):
    return pltpu.CompilerParams(vmem_limit_bytes=limit * MIB)


def whole(shape):
    return pl.BlockSpec(shape, lambda *_: (0,) * len(shape))


def rank_kernel(experts, routes_ref, gates_ref, out_ref):
    top, tokens = routes_ref.shape
    chosen = routes_ref[...].astype(jnp.float32)
    gates = gates_ref[...].astype(jnp.float32)
    label = lax.broadcasted_iota(jnp.int32, (experts, tokens), 0).astype(jnp.float32)
    hits = [(chosen[k : k + 1, :] == label).astype(jnp.float32) for k in range(top)]
    before = lax.broadcasted_iota(jnp.int32, (tokens, tokens), 0)
    after = lax.broadcasted_iota(jnp.int32, (tokens, tokens), 1)
    earlier = (before < after).astype(jnp.bfloat16)
    base = jnp.zeros((experts, 1), jnp.float32)
    rank = jnp.zeros((experts, tokens), jnp.float32)
    taken = jnp.zeros((experts, tokens), jnp.float32)
    gate = jnp.zeros((experts, tokens), jnp.float32)
    for k in range(top):
        inside = dot(hits[k].astype(jnp.bfloat16), earlier)
        rank += hits[k] * (inside + base)
        taken += hits[k]
        gate += hits[k] * gates[k : k + 1, :]
        base += jnp.sum(hits[k], axis=1, keepdims=True)
    rank = jnp.where((taken > 0.5) & (rank < CAP), rank, UNUSED)
    out_ref[:experts, :] = rank.astype(jnp.bfloat16)
    out_ref[experts:, :] = gate.astype(jnp.bfloat16)


def rank_table(routes, gates, experts):
    tokens = routes.shape[1]
    return pl.pallas_call(
        functools.partial(rank_kernel, experts),
        out_shape=jax.ShapeDtypeStruct((2 * experts, tokens), jnp.bfloat16),
    )(routes, gates)


def gather_rows(pick, refs, first, count, out, group, local):
    blocks = [refs[first + i][...] for i in range(count)]
    tokens = blocks[0] if count == 1 else jnp.concatenate(blocks, axis=0)
    rows = dot(pick, tokens).astype(jnp.bfloat16)
    for j in range(local):
        out[j, group * SLOT : (group + 1) * SLOT, :] = rows[j * SLOT : (j + 1) * SLOT, :]


def pre_kernel(axis, n, local, counts, *refs):
    table_refs, token_refs = refs[:n], refs[n : n + sum(counts)]
    wg_ref, wu_ref, a_ref, b_ref, pick_ref, xs, gcol = refs[n + sum(counts) :]
    experts = n * local
    tokens = table_refs[0].shape[1]

    @pl.when((pl.program_id(0) == 0) & (pl.program_id(1) == 0))
    def _():
        me = lax.axis_index(axis)
        row = lax.broadcasted_iota(jnp.int32, (2 * experts, tokens), 0)
        slot = lax.broadcasted_iota(jnp.int32, (SLOT, tokens), 0).astype(jnp.float32)
        first = 0
        for g in range(n):
            table = table_refs[g][...].astype(jnp.float32)
            picks = []
            for j in range(local):
                e = me * local + j
                rank = jnp.sum(jnp.where(row == e, table, 0.0), axis=0, keepdims=True)
                gate = jnp.sum(jnp.where(row == e + experts, table, 0.0), axis=0, keepdims=True)
                pick = (slot == rank).astype(jnp.float32)
                gcol[j, g * SLOT : (g + 1) * SLOT, :] = jnp.sum(pick * gate, axis=1, keepdims=True)
                picks.append(pick.astype(jnp.bfloat16))
            pick = jnp.concatenate(picks, axis=0)
            pick_ref[g] = pick
            gather_rows(pick, token_refs, first, counts[g], xs, g, local)
            first += counts[g]

    e = pl.program_id(0)
    gate_pre = dot(xs[e], wg_ref[0])
    up_pre = dot(xs[e], wu_ref[0])
    sig = jax.nn.sigmoid(gate_pre)
    weighted = gcol[e] * sig
    a_ref[0] = weighted * up_pre * (1.0 + gate_pre * (1.0 - sig))
    b_ref[0] = weighted * gate_pre


def pre(axis, n, tables, tokens, wg, wu):
    local, features, hidden = wg.shape
    rows = n * SLOT
    cols = hidden // 2
    counts = [len(t) for t in tokens]
    blocks = [block for t in tokens for block in t]
    weight = pl.BlockSpec((1, features, cols), lambda e, f: (e, 0, f))
    result = pl.BlockSpec((1, rows, cols), lambda e, f: (e, 0, f))
    picks = (n, local * SLOT, tables[0].shape[1])
    return pl.pallas_call(
        functools.partial(pre_kernel, axis, n, local, counts),
        grid=(local, hidden // cols),
        in_specs=[whole(t.shape) for t in [*tables, *blocks]] + [weight, weight],
        out_specs=[result, result, whole(picks)],
        out_shape=[
            jax.ShapeDtypeStruct((local, rows, hidden), jnp.float32),
            jax.ShapeDtypeStruct((local, rows, hidden), jnp.float32),
            jax.ShapeDtypeStruct(picks, jnp.bfloat16),
        ],
        scratch_shapes=[
            pltpu.VMEM((local, rows, features), jnp.bfloat16),
            pltpu.VMEM((local, rows, 1), jnp.float32),
        ],
        compiler_params=params(48),
        cost_estimate=pl.CostEstimate(
            flops=4 * local * rows * features * hidden,
            bytes_accessed=4 * local * features * hidden + 8 * local * rows * hidden,
            transcendentals=local * rows * hidden,
        ),
    )(*tables, *blocks, wg, wu)


def back_kernel(n, local, counts, pick_ref, *refs):
    token_refs = refs[: sum(counts)]
    wd_ref, a_ref, b_ref, hg_ref, hu_ref, gs = refs[sum(counts) :]

    @pl.when((pl.program_id(0) == 0) & (pl.program_id(1) == 0))
    def _():
        first = 0
        for g in range(n):
            gather_rows(pick_ref[g], token_refs, first, counts[g], gs, g, local)
            first += counts[g]

    back = dot(gs[pl.program_id(0)], wd_ref[0], NT)
    hg_ref[0] = (back * a_ref[0]).astype(jnp.bfloat16)
    hu_ref[0] = (back * b_ref[0]).astype(jnp.bfloat16)


def back(n, pick, tokens, wd, a, b):
    local, hidden, features = wd.shape
    rows = n * SLOT
    cols = hidden // 2
    counts = [len(t) for t in tokens]
    blocks = [block for t in tokens for block in t]
    block = pl.BlockSpec((1, rows, cols), lambda e, f: (e, 0, f))
    shape = jax.ShapeDtypeStruct((local, rows, hidden), jnp.bfloat16)
    return pl.pallas_call(
        functools.partial(back_kernel, n, local, counts),
        grid=(local, hidden // cols),
        in_specs=[
            whole(pick.shape),
            *[whole(t.shape) for t in blocks],
            pl.BlockSpec((1, cols, features), lambda e, f: (e, f, 0)),
            block,
            block,
        ],
        out_specs=[block, block],
        out_shape=[shape, shape],
        scratch_shapes=[pltpu.VMEM((local, rows, features), jnp.bfloat16)],
        compiler_params=params(40),
        cost_estimate=pl.CostEstimate(
            flops=2 * local * rows * features * hidden,
            bytes_accessed=2 * local * features * hidden + 12 * local * rows * hidden,
            transcendentals=0,
        ),
    )(pick, *blocks, wd, a, b)


def out_kernel(n, local, orders, pick_ref, hg_ref, hu_ref, wg_ref, wu_ref, *rest):
    outs, rows_ref = rest[:-1], rest[-1]
    e = pl.program_id(0)
    rows = (dot(hg_ref[0], wg_ref[0], NT) + dot(hu_ref[0], wu_ref[0], NT)).astype(jnp.bfloat16)
    for g in range(n):
        rows_ref[g, e] = rows[g * SLOT : (g + 1) * SLOT, :]

    @pl.when(e == local - 1)
    def _():
        for out_ref, order in zip(outs, orders):
            for i, g in enumerate(order):
                part = rows_ref[g].reshape(local * SLOT, -1)
                out_ref[i] = dot(pick_ref[g], part, TN).astype(out_ref.dtype)


def partial_sums(n, orders, chunk, pick, hg, hu, wg, wu):
    local, features, hidden = wg.shape
    tokens = pick.shape[2]
    rows = n * SLOT
    cols = features // CHUNKS
    act = pl.BlockSpec((1, rows, hidden), lambda e: (e, 0, 0))
    weight = pl.BlockSpec((1, cols, hidden), lambda e: (e, chunk, 0))
    shapes = [(len(order), tokens, cols) for order in orders]
    types = [jnp.float32] + [jnp.bfloat16] * (len(orders) - 1)
    return pl.pallas_call(
        functools.partial(out_kernel, n, local, orders),
        grid=(local,),
        in_specs=[whole(pick.shape), act, act, weight, weight],
        out_specs=[whole(s) for s in shapes],
        out_shape=[jax.ShapeDtypeStruct(s, t) for s, t in zip(shapes, types)],
        scratch_shapes=[pltpu.VMEM((n, local, SLOT, cols), jnp.bfloat16)],
        compiler_params=params(32),
        cost_estimate=pl.CostEstimate(
            flops=4 * local * rows * cols * hidden,
            bytes_accessed=4 * local * (cols + rows) * hidden,
            transcendentals=0,
        ),
    )(pick, hg, hu, wg, wu)


def sum_kernel(*refs):
    parts, out_ref = refs[:-1], refs[-1]
    each = len(parts) // CHUNKS
    cols = out_ref.shape[1] // CHUNKS
    for c in range(CHUNKS):
        own, *others = parts[c * each : (c + 1) * each]
        total = own[0]
        for other in others:
            total += other[0].astype(jnp.float32)
        out_ref[:, c * cols : (c + 1) * cols] = total.astype(jnp.bfloat16)


def body(axis, saved_input, grad_out, routes, route_gates, gate_proj, up_proj, down_proj):
    n = lax.axis_size(axis)
    local = gate_proj.shape[0]
    experts = n * local
    tokens, features = saved_input.shape

    def swap(array, k):
        return lax.ppermute(array, axis, [(i, i ^ k) for i in range(n)])

    table = rank_table(routes.T, route_gates.T, experts)
    tables = [table] + [swap(table, k) for k in range(1, n)]
    if n == 4:
        half = tokens // 2
        upper, lower = saved_input[:half], saved_input[half:]
        near = [[]] + [[swap(upper, k), swap(lower, k)] for k in (1, 2)]
        relayed = [swap(near[1][0], 2), swap(near[2][1], 1)]
        x_blocks = [[saved_input], near[1], near[2], relayed]
        grad_out, *_ = lax.optimization_barrier((grad_out, near[1], near[2]))
    else:
        x_blocks = [[saved_input]] + [[swap(saved_input, k)] for k in range(1, n)]
    g_blocks = [[grad_out]] + [[swap(grad_out, k)] for k in range(1, n)]
    a, b, pick = pre(axis, n, tables, x_blocks, gate_proj, up_proj)
    hg, hu = back(n, pick, g_blocks, down_proj, a, b)
    parts = []
    for chunk in range(CHUNKS):
        if n == 4:
            first, last = (1, 2) if chunk % 2 == 0 else (2, 1)
            orders = ((0,), (first, 3), (last,))
            own, two, one = partial_sums(n, orders, chunk, pick, hg, hu, gate_proj, up_proj)
            two = swap(two, first)
            relay = (two[1:2].astype(jnp.float32) + one.astype(jnp.float32)).astype(jnp.bfloat16)
            parts += [own, two[:1], swap(relay, last)]
        else:
            orders = tuple((k,) for k in range(n))
            own, *others = partial_sums(n, orders, chunk, pick, hg, hu, gate_proj, up_proj)
            parts += [own] + [swap(other, k + 1) for k, other in enumerate(others)]
    return pl.pallas_call(
        sum_kernel,
        out_shape=jax.ShapeDtypeStruct((tokens, features), jnp.bfloat16),
        compiler_params=params(48),
    )(*parts)


def solution(mesh):
    tokens = P(("dp", "expert"), None)
    weights = P("expert", None, None)
    return jax.shard_map(
        functools.partial(body, "expert"),
        mesh=mesh,
        in_specs=(tokens, tokens, tokens, tokens, weights, weights, weights),
        out_specs=tokens,
        check_vma=False,
    )
```

```python
import functools

import jax
import jax.numpy as jnp
from jax import lax
from jax.experimental import pallas as pl
from jax.experimental.pallas import tpu as pltpu
from jax.sharding import PartitionSpec as P

CAP = 56
SLOT = 64
UNUSED = 200.0
MIB = 1 << 20
CHUNKS = 4
PRE_MIB = 8
BACK_MIB = 12
OUT_MIB = 4

NT = (((1,), (1,)), ((), ()))


def dot(a, b, dims=(((1,), (0,)), ((), ()))):
    return lax.dot_general(a, b, dims, preferred_element_type=jnp.float32)


def params(limit):
    return pltpu.CompilerParams(vmem_limit_bytes=limit * MIB)


def rank_kernel(experts, routes_ref, gates_ref, out_ref):
    top, tokens = routes_ref.shape
    chosen = routes_ref[...].astype(jnp.float32)
    gates = gates_ref[...].astype(jnp.float32)
    label = lax.broadcasted_iota(jnp.int32, (experts, tokens), 0).astype(jnp.float32)
    hits = [(chosen[k : k + 1, :] == label).astype(jnp.float32) for k in range(top)]
    before = lax.broadcasted_iota(jnp.int32, (tokens, tokens), 0)
    after = lax.broadcasted_iota(jnp.int32, (tokens, tokens), 1)
    earlier = (before < after).astype(jnp.bfloat16)
    base = jnp.zeros((experts, 1), jnp.float32)
    rank = jnp.zeros((experts, tokens), jnp.float32)
    taken = jnp.zeros((experts, tokens), jnp.float32)
    gate = jnp.zeros((experts, tokens), jnp.float32)
    for k in range(top):
        inside = dot(hits[k].astype(jnp.bfloat16), earlier)
        rank += hits[k] * (inside + base)
        taken += hits[k]
        gate += hits[k] * gates[k : k + 1, :]
        base += jnp.sum(hits[k], axis=1, keepdims=True)
    rank = jnp.where((taken > 0.5) & (rank < CAP), rank, UNUSED)
    out_ref[:experts, :] = rank.astype(jnp.bfloat16)
    out_ref[experts:, :] = gate.astype(jnp.bfloat16)


def rank_table(routes, gates, experts):
    tokens = routes.shape[1]
    return pl.pallas_call(
        functools.partial(rank_kernel, experts),
        out_shape=jax.ShapeDtypeStruct((2 * experts, tokens), jnp.bfloat16),
    )(routes, gates)


def gather_rows(n, local, pick_ref, token_refs, out):
    wide = 2 * SLOT
    features = out.shape[2]
    cols = features // 4
    for p in range(n // 2):
        refs = [ref for pair in token_refs[2 * p : 2 * p + 2] for ref in pair]
        for d in range(0, features, cols):
            part = slice(d, d + cols)
            tokens = jnp.concatenate([ref[:, part] for ref in refs], axis=0)
            rows = dot(pick_ref[p], tokens).astype(jnp.bfloat16)
            for j in range(local):
                out[j, p * wide : (p + 1) * wide, part] = rows[j * wide : (j + 1) * wide, :]


def split(refs, counts):
    parts, first = [], 0
    for count in counts:
        parts.append(refs[first : first + count])
        first += count
    return parts, refs[first:]


def pre_kernel(axis, n, local, counts, *refs):
    table_refs, refs = refs[:n], refs[n:]
    token_refs, refs = split(refs, counts)
    wg_ref, wu_ref, a_ref, b_ref, pick_ref, place_ref, xs, gcol = refs
    experts = n * local
    tokens = table_refs[0].shape[1]
    wide = 2 * SLOT
    hidden = wg_ref.shape[2]
    cols = hidden // 2
    me = lax.axis_index(axis)
    row = lax.broadcasted_iota(jnp.int32, (2 * experts, tokens), 0)
    slot = lax.broadcasted_iota(jnp.int32, (wide, tokens), 0).astype(jnp.float32)
    for p in range(n // 2):
        for j in range(local):
            e = me * local + j
            gates = jnp.zeros((wide, 1), jnp.float32)
            for q in range(2):
                table = table_refs[2 * p + q][...].astype(jnp.float32)
                rank = jnp.sum(jnp.where(row == e, table, 0.0), axis=0, keepdims=True)
                gate = jnp.sum(jnp.where(row == e + experts, table, 0.0), axis=0, keepdims=True)
                pick = (slot == rank + q * SLOT).astype(jnp.float32)
                gates += jnp.sum(pick * gate, axis=1, keepdims=True)
                across = slice(q * tokens, (q + 1) * tokens)
                down = slice(j * wide, (j + 1) * wide)
                pick_ref[p, down, across] = pick.astype(jnp.bfloat16)
                place_ref[p, across, down] = pick.T.astype(jnp.bfloat16)
            gcol[j, p * wide : (p + 1) * wide, :] = gates
    gather_rows(n, local, pick_ref, token_refs, xs)

    @pl.loop(0, local)
    def _(e):
        for f in range(0, hidden, cols):
            part = slice(f, f + cols)
            gate_pre = dot(xs[e], wg_ref[e, :, part])
            up_pre = dot(xs[e], wu_ref[e, :, part])
            sig = jax.nn.sigmoid(gate_pre)
            weighted = gcol[e] * sig
            a_ref[e, part, :] = (weighted * up_pre * (1.0 + gate_pre * (1.0 - sig))).T
            b_ref[e, part, :] = (weighted * gate_pre).T


def vmem(array):
    return pltpu.with_memory_space_constraint(array, pltpu.VMEM)


def load_kernel(count, *refs):
    sources, results, sems = refs[:count], refs[-count - 1 : -1], refs[-1]
    copies = [
        pltpu.make_async_copy(source.at[e], result.at[e], sems.at[i, e])
        for i, (source, result) in enumerate(zip(sources, results))
        for e in range(source.shape[0])
    ]
    for copy in copies:
        copy.start()
    for copy in copies:
        copy.wait()


def load(arrays, after):
    count = len(arrays)
    return pl.pallas_call(
        functools.partial(load_kernel, count),
        in_specs=[pl.BlockSpec(memory_space=pltpu.HBM)] * count + [pl.BlockSpec(memory_space=pl.ANY)],
        out_specs=[pl.BlockSpec(memory_space=pltpu.VMEM)] * count,
        out_shape=[pltpu.VMEM(w.shape, w.dtype) for w in arrays],
        scratch_shapes=[pltpu.SemaphoreType.DMA((count, arrays[0].shape[0]))],
        compiler_params=params(1),
        cost_estimate=pl.CostEstimate(
            flops=0, bytes_accessed=4 * count * arrays[0].size, transcendentals=0
        ),
    )(*[pltpu.with_memory_space_constraint(w, pltpu.HBM) for w in arrays], after)


def pre(axis, n, tables, tokens, wg, wu):
    local, features, hidden = wg.shape
    rows = n * SLOT
    across, down = 2 * tables[0].shape[1], 2 * SLOT * local
    return pl.pallas_call(
        functools.partial(pre_kernel, axis, n, local, [len(t) for t in tokens]),
        out_shape=[
            jax.ShapeDtypeStruct((local, hidden, rows), jnp.float32),
            jax.ShapeDtypeStruct((local, hidden, rows), jnp.float32),
            jax.ShapeDtypeStruct((n // 2, down, across), jnp.bfloat16),
            jax.ShapeDtypeStruct((n // 2, across, down), jnp.bfloat16),
        ],
        scratch_shapes=[
            pltpu.VMEM((local, rows, features), jnp.bfloat16),
            pltpu.VMEM((local, rows, 1), jnp.float32),
        ],
        compiler_params=params(PRE_MIB * max(1, n // 4)),
        cost_estimate=pl.CostEstimate(
            flops=4 * local * rows * features * hidden,
            bytes_accessed=4 * local * features * hidden,
            transcendentals=local * rows * hidden,
        ),
    )(*tables, *[block for t in tokens for block in t], vmem(wg), vmem(wu))


def back_kernel(n, local, counts, pick_ref, *refs):
    token_refs, refs = split(refs, counts)
    wd_ref, a_ref, b_ref, _, _, hg_ref, hu_ref, gs, weight, sems = refs
    hidden = wd_ref.shape[1]
    held = weight.shape[0]
    cols = hidden // 2

    def fetch(e, i):
        part = pl.ds(i * cols, cols)
        slot = lax.rem(e, held)
        return pltpu.make_async_copy(wd_ref.at[e, part], weight.at[slot, part], sems.at[slot, i])

    for e in range(held):
        for i in range(2):
            fetch(e, i).start()
    gather_rows(n, local, pick_ref, token_refs, gs)

    @pl.loop(0, local)
    def _(e):
        for i in range(2):
            part = slice(i * cols, (i + 1) * cols)
            fetch(e, i).wait()
            back = dot(weight[lax.rem(e, held), part, :], gs[e], NT)
            hg_ref[e, part, :] = (back * a_ref[e, part, :]).astype(jnp.bfloat16)
            hu_ref[e, part, :] = (back * b_ref[e, part, :]).astype(jnp.bfloat16)

            @pl.when(e + held < local)
            def _():
                fetch(e + held, i).start()


def back(n, pick, tokens, wd, a, b, wg, wu):
    local, hidden, features = wd.shape
    rows = n * SLOT
    blocks = [block for t in tokens for block in t]
    shape = jax.ShapeDtypeStruct((local, hidden, rows), jnp.bfloat16)
    inside, outside = pl.BlockSpec(memory_space=pltpu.VMEM), pl.BlockSpec(memory_space=pltpu.HBM)
    return pl.pallas_call(
        functools.partial(back_kernel, n, local, [len(t) for t in tokens]),
        in_specs=[inside] * (1 + len(blocks)) + [outside] + [inside] * 4,
        out_shape=[shape, shape],
        scratch_shapes=[
            pltpu.VMEM((local, rows, features), jnp.bfloat16),
            pltpu.VMEM((min(local, 2), hidden, features), jnp.bfloat16),
            pltpu.SemaphoreType.DMA((min(local, 2), 2)),
        ],
        compiler_params=params(BACK_MIB * max(1, n // 8)),
        cost_estimate=pl.CostEstimate(
            flops=2 * local * rows * features * hidden,
            bytes_accessed=2 * local * features * hidden,
            transcendentals=0,
        ),
    )(pick, *blocks, pltpu.with_memory_space_constraint(wd, pltpu.HBM), a, b, vmem(wg), vmem(wu))


def out_kernel(n, local, orders, chunk, place_ref, hg_ref, hu_ref, wg_ref, wu_ref, *rest):
    outs, rows_ref = rest[:-1], rest[-1]
    wide = 2 * SLOT
    cols = wg_ref.shape[1] // CHUNKS
    part = slice(chunk * cols, (chunk + 1) * cols)
    for e in range(local):
        rows = dot(wg_ref[e, part, :], hg_ref[e]) + dot(wu_ref[e, part, :], hu_ref[e])
        rows = rows.astype(jnp.bfloat16)
        for p in range(n // 2):
            rows_ref[p, :, e * wide : (e + 1) * wide] = rows[:, p * wide : (p + 1) * wide]
    tokens = place_ref.shape[1] // 2
    for p in range(n // 2):
        total = dot(place_ref[p], rows_ref[p], NT)
        for out_ref, order in zip(outs, orders):
            for i, g in enumerate(order):
                if g // 2 == p:
                    mine = total[g % 2 * tokens : (g % 2 + 1) * tokens, :]
                    out_ref[i] = mine.astype(out_ref.dtype)


def partial_sums(n, orders, chunk, place, hg, hu, wg, wu):
    local, features, hidden = wg.shape
    tokens = place.shape[1] // 2
    rows = n * SLOT
    cols = features // CHUNKS
    shapes = [(len(order), tokens, cols) for order in orders]
    types = [jnp.float32] + [jnp.bfloat16] * (len(orders) - 1)
    return pl.pallas_call(
        functools.partial(out_kernel, n, local, orders, chunk),
        out_shape=[jax.ShapeDtypeStruct(s, t) for s, t in zip(shapes, types)],
        scratch_shapes=[pltpu.VMEM((n // 2, cols, 2 * SLOT * local), jnp.bfloat16)],
        compiler_params=params(OUT_MIB * max(1, n // 4)),
        cost_estimate=pl.CostEstimate(
            flops=local * rows * cols * hidden,
            bytes_accessed=local * cols * hidden,
            transcendentals=0,
        ),
    )(place, hg, hu, vmem(wg), vmem(wu))


def sum_kernel(*refs):
    parts, out_ref = refs[:-1], refs[-1]
    each = len(parts) // CHUNKS
    cols = out_ref.shape[1] // CHUNKS
    for c in range(CHUNKS):
        own, *others = parts[c * each : (c + 1) * each]
        total = own[0]
        for other in others:
            total += other[0].astype(jnp.float32)
        out_ref[:, c * cols : (c + 1) * cols] = total.astype(jnp.bfloat16)


def body(axis, saved_input, grad_out, routes, route_gates, gate_proj, up_proj, down_proj):
    n = lax.axis_size(axis)
    local = gate_proj.shape[0]
    experts = n * local
    tokens, features = saved_input.shape

    def swap(array, k):
        return lax.ppermute(array, axis, [(i, i ^ k) for i in range(n)])

    table = rank_table(routes.T, route_gates.T, experts)
    tables = [table] + [swap(table, k) for k in range(1, n)]
    if n == 4:
        half = tokens // 2
        upper, lower = saved_input[:half], saved_input[half:]
        near = [[]] + [[swap(upper, k), swap(lower, k)] for k in (1, 2)]
        gate_proj, up_proj = load((gate_proj, up_proj), table)
        relayed = [swap(near[1][0], 2), swap(near[2][1], 1)]
        x_blocks = [[saved_input], near[1], near[2], relayed]
        grad_out, *_ = lax.optimization_barrier((grad_out, near[1], near[2]))
    else:
        x_blocks = [[saved_input]] + [[swap(saved_input, k)] for k in range(1, n)]
        gate_proj, up_proj = load((gate_proj, up_proj), table)
    g_blocks = [[grad_out]] + [[swap(grad_out, k)] for k in range(1, n)]
    a, b, pick, place = pre(axis, n, tables, x_blocks, gate_proj, up_proj)
    hg, hu = back(n, pick, g_blocks, down_proj, a, b, gate_proj, up_proj)
    parts = []
    for chunk in range(CHUNKS):
        if n == 4:
            first, last = (1, 2) if chunk % 2 == 0 else (2, 1)
            orders = ((0,), (first, 3), (last,))
            own, two, one = partial_sums(n, orders, chunk, place, hg, hu, gate_proj, up_proj)
            two = swap(two, first)
            relay = (two[1:2].astype(jnp.float32) + one.astype(jnp.float32)).astype(jnp.bfloat16)
            parts += [own, two[:1], swap(relay, last)]
        else:
            orders = tuple((k,) for k in range(n))
            own, *others = partial_sums(n, orders, chunk, place, hg, hu, gate_proj, up_proj)
            parts += [own] + [swap(other, k + 1) for k, other in enumerate(others)]
    return pl.pallas_call(
        sum_kernel,
        out_shape=jax.ShapeDtypeStruct((tokens, features), jnp.bfloat16),
        compiler_params=params(8),
    )(*parts)


def solution(mesh):
    tokens = P(("dp", "expert"), None)
    weights = P("expert", None, None)
    return jax.shard_map(
        functools.partial(body, "expert"),
        mesh=mesh,
        in_specs=(tokens, tokens, tokens, tokens, weights, weights, weights),
        out_specs=tokens,
        check_vma=False,
    )
```

```python
import functools

import jax
import jax.numpy as jnp
from jax import lax
from jax.experimental import pallas as pl
from jax.experimental.pallas import tpu as pltpu
from jax.sharding import PartitionSpec as P

CAP = 56
SLOT = 64
UNUSED = 200.0
MIB = 1 << 20
CHUNKS = 4
PRE_MIB = 8
BACK_MIB = 12
OUT_MIB = 4

NT = (((1,), (1,)), ((), ()))


def dot(a, b, dims=(((1,), (0,)), ((), ()))):
    return lax.dot_general(a, b, dims, preferred_element_type=jnp.float32)


def params(limit):
    return pltpu.CompilerParams(vmem_limit_bytes=limit * MIB)


def rank_kernel(experts, routes_ref, gates_ref, out_ref):
    top, tokens = routes_ref.shape
    chosen = routes_ref[...].astype(jnp.float32)
    gates = gates_ref[...].astype(jnp.float32)
    label = lax.broadcasted_iota(jnp.int32, (experts, tokens), 0).astype(jnp.float32)
    hits = [(chosen[k : k + 1, :] == label).astype(jnp.float32) for k in range(top)]
    before = lax.broadcasted_iota(jnp.int32, (tokens, tokens), 0)
    after = lax.broadcasted_iota(jnp.int32, (tokens, tokens), 1)
    earlier = (before < after).astype(jnp.bfloat16)
    base = jnp.zeros((experts, 1), jnp.float32)
    rank = jnp.zeros((experts, tokens), jnp.float32)
    taken = jnp.zeros((experts, tokens), jnp.float32)
    gate = jnp.zeros((experts, tokens), jnp.float32)
    for k in range(top):
        inside = dot(hits[k].astype(jnp.bfloat16), earlier)
        rank += hits[k] * (inside + base)
        taken += hits[k]
        gate += hits[k] * gates[k : k + 1, :]
        base += jnp.sum(hits[k], axis=1, keepdims=True)
    rank = jnp.where((taken > 0.5) & (rank < CAP), rank, UNUSED)
    out_ref[:experts, :] = rank.astype(jnp.bfloat16)
    out_ref[experts:, :] = gate.astype(jnp.bfloat16)


def rank_table(routes, gates, experts):
    tokens = routes.shape[1]
    return pl.pallas_call(
        functools.partial(rank_kernel, experts),
        out_shape=jax.ShapeDtypeStruct((2 * experts, tokens), jnp.bfloat16),
    )(routes, gates)


def gather_rows(n, local, pick_ref, token_refs, out):
    wide = 2 * SLOT
    features = out.shape[2]
    cols = features // 4
    for p in range(n // 2):
        refs = [ref for pair in token_refs[2 * p : 2 * p + 2] for ref in pair]
        for d in range(0, features, cols):
            part = slice(d, d + cols)
            tokens = jnp.concatenate([ref[:, part] for ref in refs], axis=0)
            rows = dot(pick_ref[p], tokens).astype(jnp.bfloat16)
            for j in range(local):
                out[j, p * wide : (p + 1) * wide, part] = rows[j * wide : (j + 1) * wide, :]


def gather_columns(n, local, place_ref, token_refs, out):
    wide = 2 * SLOT
    features = out.shape[1]
    size = features // 4
    for p in range(n // 2):
        refs = [ref for pair in token_refs[2 * p : 2 * p + 2] for ref in pair]
        for d in range(0, features, size):
            part = slice(d, d + size)
            tokens = jnp.concatenate([ref[:, part] for ref in refs], axis=0)
            columns = dot(tokens.T, place_ref[p]).astype(jnp.bfloat16)
            for j in range(local):
                out[j, part, p * wide : (p + 1) * wide] = columns[:, j * wide : (j + 1) * wide]


def split(refs, counts):
    parts, first = [], 0
    for count in counts:
        parts.append(refs[first : first + count])
        first += count
    return parts, refs[first:]


def pre_kernel(axis, n, local, counts, *refs):
    table_refs, refs = refs[:n], refs[n:]
    token_refs, refs = split(refs, counts)
    wg_ref, wu_ref, a_ref, b_ref, place_ref, xs, gcol, pick_ref = refs
    experts = n * local
    tokens = table_refs[0].shape[1]
    wide = 2 * SLOT
    hidden = wg_ref.shape[2]
    cols = hidden // 2
    me = lax.axis_index(axis)
    row = lax.broadcasted_iota(jnp.int32, (2 * experts, tokens), 0)
    slot = lax.broadcasted_iota(jnp.int32, (wide, tokens), 0).astype(jnp.float32)
    for p in range(n // 2):
        for j in range(local):
            e = me * local + j
            gates = jnp.zeros((wide, 1), jnp.float32)
            for q in range(2):
                table = table_refs[2 * p + q][...].astype(jnp.float32)
                rank = jnp.sum(jnp.where(row == e, table, 0.0), axis=0, keepdims=True)
                gate = jnp.sum(jnp.where(row == e + experts, table, 0.0), axis=0, keepdims=True)
                pick = (slot == rank + q * SLOT).astype(jnp.float32)
                gates += jnp.sum(pick * gate, axis=1, keepdims=True)
                across = slice(q * tokens, (q + 1) * tokens)
                down = slice(j * wide, (j + 1) * wide)
                pick_ref[p, down, across] = pick.astype(jnp.bfloat16)
                place_ref[p, across, down] = pick.T.astype(jnp.bfloat16)
            gcol[j, p * wide : (p + 1) * wide, :] = gates
    gather_rows(n, local, pick_ref, token_refs, xs)

    @pl.loop(0, local)
    def _(e):
        for f in range(0, hidden, cols):
            part = slice(f, f + cols)
            gate_pre = dot(xs[e], wg_ref[e, :, part])
            up_pre = dot(xs[e], wu_ref[e, :, part])
            sig = jax.nn.sigmoid(gate_pre)
            weighted = gcol[e] * sig
            a_ref[e, part, :] = (weighted * up_pre * (1.0 + gate_pre * (1.0 - sig))).T
            b_ref[e, part, :] = (weighted * gate_pre).T


def vmem(array):
    return pltpu.with_memory_space_constraint(array, pltpu.VMEM)


def load_kernel(count, *refs):
    sources, (*results, done_ref, sems) = refs[:count], refs[count + 1 :]
    copies = [
        pltpu.make_async_copy(source.at[e], result.at[e], sems.at[i, e])
        for i, (source, result) in enumerate(zip(sources, results))
        for e in range(source.shape[0])
    ]
    for copy in copies:
        copy.start()
    for copy in copies:
        copy.wait()
    done_ref[...] = jnp.zeros_like(done_ref)


def load(arrays, after):
    count = len(arrays)
    return pl.pallas_call(
        functools.partial(load_kernel, count),
        in_specs=[pl.BlockSpec(memory_space=pltpu.HBM)] * count + [pl.BlockSpec(memory_space=pl.ANY)],
        out_specs=[pl.BlockSpec(memory_space=pltpu.VMEM)] * (count + 1),
        out_shape=[pltpu.VMEM(w.shape, w.dtype) for w in arrays]
        + [jax.ShapeDtypeStruct((8, 128), jnp.float32)],
        scratch_shapes=[pltpu.SemaphoreType.DMA((count, arrays[0].shape[0]))],
        compiler_params=params(1),
        cost_estimate=pl.CostEstimate(
            flops=0, bytes_accessed=4 * count * arrays[0].size, transcendentals=0
        ),
    )(*[pltpu.with_memory_space_constraint(w, pltpu.HBM) for w in arrays], after)


def relay_kernel(x_ref, y_ref, *refs):
    upper_ref, lower_ref = refs[-2:]
    half = upper_ref.shape[0]
    upper_ref[...] = x_ref[:half, :]
    lower_ref[...] = y_ref[half:, :]


def relay_parts(beside, after):
    tokens, features = beside[0].shape
    inside, anywhere = pl.BlockSpec(memory_space=pltpu.VMEM), pl.BlockSpec(memory_space=pl.ANY)
    half = jax.ShapeDtypeStruct((tokens // 2, features), beside[0].dtype)
    return pl.pallas_call(
        relay_kernel,
        in_specs=[inside] * 2 + [anywhere] * len(after),
        out_shape=[half, half],
        compiler_params=params(4),
    )(*beside, *after)


def pass_kernel(array_ref, _, copy_ref):
    copy_ref[...] = array_ref[...]


def passed(array, after):
    return pl.pallas_call(
        pass_kernel,
        in_specs=[pl.BlockSpec(memory_space=pltpu.VMEM), pl.BlockSpec(memory_space=pl.ANY)],
        out_shape=jax.ShapeDtypeStruct(array.shape, array.dtype),
        compiler_params=params(4),
    )(array, after)


def pre(axis, n, tables, tokens, wg, wu):
    local, features, hidden = wg.shape
    rows = n * SLOT
    across, down = 2 * tables[0].shape[1], 2 * SLOT * local
    return pl.pallas_call(
        functools.partial(pre_kernel, axis, n, local, [len(t) for t in tokens]),
        out_shape=[
            jax.ShapeDtypeStruct((local, hidden, rows), jnp.float32),
            jax.ShapeDtypeStruct((local, hidden, rows), jnp.float32),
            jax.ShapeDtypeStruct((n // 2, across, down), jnp.bfloat16),
        ],
        scratch_shapes=[
            pltpu.VMEM((local, rows, features), jnp.bfloat16),
            pltpu.VMEM((local, rows, 1), jnp.float32),
            pltpu.VMEM((n // 2, down, across), jnp.bfloat16),
        ],
        compiler_params=params(PRE_MIB * max(1, n // 4)),
        cost_estimate=pl.CostEstimate(
            flops=4 * local * rows * features * hidden,
            bytes_accessed=4 * local * features * hidden,
            transcendentals=local * rows * hidden,
        ),
    )(*tables, *[block for t in tokens for block in t], vmem(wg), vmem(wu))


def back_kernel(n, local, counts, place_ref, *refs):
    token_refs, refs = split(refs, counts)
    wd_ref, a_ref, b_ref, _, _, hg_ref, hu_ref, gs, weight, sems = refs
    hidden = wd_ref.shape[1]
    held = weight.shape[0]
    cols = hidden // 2

    def fetch(e, i):
        part = pl.ds(i * cols, cols)
        slot = lax.rem(e, held)
        return pltpu.make_async_copy(wd_ref.at[e, part], weight.at[slot, part], sems.at[slot, i])

    for e in range(held):
        for i in range(2):
            fetch(e, i).start()
    gather_columns(n, local, place_ref, token_refs, gs)

    @pl.loop(0, local)
    def _(e):
        for i in range(2):
            part = slice(i * cols, (i + 1) * cols)
            fetch(e, i).wait()
            back = dot(weight[lax.rem(e, held), part, :], gs[e])
            hg_ref[e, part, :] = (back * a_ref[e, part, :]).astype(jnp.bfloat16)
            hu_ref[e, part, :] = (back * b_ref[e, part, :]).astype(jnp.bfloat16)

            @pl.when(e + held < local)
            def _():
                fetch(e + held, i).start()


def back(n, place, tokens, wd, a, b, wg, wu):
    local, hidden, features = wd.shape
    rows = n * SLOT
    blocks = [block for t in tokens for block in t]
    shape = jax.ShapeDtypeStruct((local, hidden, rows), jnp.bfloat16)
    inside, outside = pl.BlockSpec(memory_space=pltpu.VMEM), pl.BlockSpec(memory_space=pltpu.HBM)
    return pl.pallas_call(
        functools.partial(back_kernel, n, local, [len(t) for t in tokens]),
        in_specs=[inside] * (1 + len(blocks)) + [outside] + [inside] * 4,
        out_shape=[shape, shape],
        scratch_shapes=[
            pltpu.VMEM((local, features, rows), jnp.bfloat16),
            pltpu.VMEM((min(local, 2), hidden, features), jnp.bfloat16),
            pltpu.SemaphoreType.DMA((min(local, 2), 2)),
        ],
        compiler_params=params(BACK_MIB * max(1, n // 8)),
        cost_estimate=pl.CostEstimate(
            flops=2 * local * rows * features * hidden,
            bytes_accessed=2 * local * features * hidden,
            transcendentals=0,
        ),
    )(place, *blocks, pltpu.with_memory_space_constraint(wd, pltpu.HBM), a, b, vmem(wg), vmem(wu))


def out_kernel(n, local, orders, chunk, place_ref, hg_ref, hu_ref, wg_ref, wu_ref, *rest):
    outs, rows_ref = rest[:-1], rest[-1]
    wide = 2 * SLOT
    cols = wg_ref.shape[1] // CHUNKS
    part = slice(chunk * cols, (chunk + 1) * cols)
    for e in range(local):
        rows = dot(wg_ref[e, part, :], hg_ref[e]) + dot(wu_ref[e, part, :], hu_ref[e])
        rows = rows.astype(jnp.bfloat16)
        for p in range(n // 2):
            rows_ref[p, :, e * wide : (e + 1) * wide] = rows[:, p * wide : (p + 1) * wide]
    tokens = place_ref.shape[1] // 2
    for p in range(n // 2):
        total = dot(place_ref[p], rows_ref[p], NT)
        for out_ref, order in zip(outs, orders):
            for i, g in enumerate(order):
                if g // 2 == p:
                    mine = total[g % 2 * tokens : (g % 2 + 1) * tokens, :]
                    out_ref[i] = mine.astype(out_ref.dtype)


def partial_sums(n, orders, chunk, place, hg, hu, wg, wu):
    local, features, hidden = wg.shape
    tokens = place.shape[1] // 2
    rows = n * SLOT
    cols = features // CHUNKS
    shapes = [(len(order), tokens, cols) for order in orders]
    types = [jnp.float32] + [jnp.bfloat16] * (len(orders) - 1)
    return pl.pallas_call(
        functools.partial(out_kernel, n, local, orders, chunk),
        out_shape=[jax.ShapeDtypeStruct(s, t) for s, t in zip(shapes, types)],
        scratch_shapes=[pltpu.VMEM((n // 2, cols, 2 * SLOT * local), jnp.bfloat16)],
        compiler_params=params(OUT_MIB * max(1, n // 4)),
        cost_estimate=pl.CostEstimate(
            flops=local * rows * cols * hidden,
            bytes_accessed=local * cols * hidden,
            transcendentals=0,
        ),
    )(place, hg, hu, vmem(wg), vmem(wu))


def sum_kernel(*refs):
    parts, out_ref = refs[:-1], refs[-1]
    each = len(parts) // CHUNKS
    cols = out_ref.shape[1] // CHUNKS
    for c in range(CHUNKS):
        own, *others = parts[c * each : (c + 1) * each]
        total = own[0]
        for other in others:
            total += other[0].astype(jnp.float32)
        out_ref[:, c * cols : (c + 1) * cols] = total.astype(jnp.bfloat16)


def body(axis, saved_input, grad_out, routes, route_gates, gate_proj, up_proj, down_proj):
    n = lax.axis_size(axis)
    local = gate_proj.shape[0]
    experts = n * local
    tokens, features = saved_input.shape

    def swap(array, k):
        return lax.ppermute(array, axis, [(i, i ^ k) for i in range(n)])

    table = rank_table(routes.T, route_gates.T, experts)
    tables = [table] + [swap(table, k) for k in range(1, n)]
    gate_proj, up_proj, done = load((gate_proj, up_proj), table)
    if n == 4:
        x_near = [swap(saved_input, 1), swap(saved_input, 2)]
        upper, lower = relay_parts(x_near, [done, *tables[1:]])
        sent = passed(grad_out, upper)
        x_blocks = [[saved_input], *[[x] for x in x_near], [swap(upper, 2), swap(lower, 1)]]
        g_near = [swap(sent, 1), swap(sent, 2)]
    else:
        x_blocks = [[saved_input]] + [[swap(saved_input, k)] for k in range(1, n)]
    a, b, place = pre(axis, n, tables, x_blocks, gate_proj, up_proj)
    if n == 4:
        upper, lower = relay_parts(g_near, [place])
        g_blocks = [[sent], *[[g] for g in g_near], [swap(upper, 2), swap(lower, 1)]]
    else:
        g_blocks = [[grad_out]] + [[swap(grad_out, k)] for k in range(1, n)]
    hg, hu = back(n, place, g_blocks, down_proj, a, b, gate_proj, up_proj)
    parts = []
    for chunk in range(CHUNKS):
        if n == 4:
            first, last = (1, 2) if chunk % 2 == 0 else (2, 1)
            orders = ((0,), (first, 3), (last,))
            own, two, one = partial_sums(n, orders, chunk, place, hg, hu, gate_proj, up_proj)
            two = swap(two, first)
            mixed = (two[1:2].astype(jnp.float32) + one.astype(jnp.float32)).astype(jnp.bfloat16)
            parts += [own, two[:1], swap(mixed, last)]
        else:
            orders = tuple((k,) for k in range(n))
            own, *others = partial_sums(n, orders, chunk, place, hg, hu, gate_proj, up_proj)
            parts += [own] + [swap(other, k + 1) for k, other in enumerate(others)]
    return pl.pallas_call(
        sum_kernel,
        out_shape=jax.ShapeDtypeStruct((tokens, features), jnp.bfloat16),
        compiler_params=params(8),
    )(*parts)


def solution(mesh):
    tokens = P(("dp", "expert"), None)
    weights = P("expert", None, None)
    return jax.shard_map(
        functools.partial(body, "expert"),
        mesh=mesh,
        in_specs=(tokens, tokens, tokens, tokens, weights, weights, weights),
        out_specs=tokens,
        check_vma=False,
    )
```

```python
import functools

import jax
import jax.numpy as jnp
from jax import lax
from jax.experimental import pallas as pl
from jax.experimental.pallas import tpu as pltpu
from jax.sharding import PartitionSpec as P

CAP = 56
SLOT = 64
UNUSED = 200.0
MIB = 1 << 20
CHUNKS = 4
PRE_MIB = 6
BACK_MIB = 10
OUT_MIB = 4

NT = (((1,), (1,)), ((), ()))


def dot(a, b, dims=(((1,), (0,)), ((), ()))):
    return lax.dot_general(a, b, dims, preferred_element_type=jnp.float32)


def params(limit):
    return pltpu.CompilerParams(vmem_limit_bytes=limit * MIB)


def rank_kernel(experts, routes_ref, gates_ref, out_ref):
    top, tokens = routes_ref.shape
    chosen = routes_ref[...].astype(jnp.float32)
    gates = gates_ref[...].astype(jnp.float32)
    label = lax.broadcasted_iota(jnp.int32, (experts, tokens), 0).astype(jnp.float32)
    hits = [(chosen[k : k + 1, :] == label).astype(jnp.float32) for k in range(top)]
    before = lax.broadcasted_iota(jnp.int32, (tokens, tokens), 0)
    after = lax.broadcasted_iota(jnp.int32, (tokens, tokens), 1)
    earlier = (before < after).astype(jnp.bfloat16)
    base = jnp.zeros((experts, 1), jnp.float32)
    rank = jnp.zeros((experts, tokens), jnp.float32)
    taken = jnp.zeros((experts, tokens), jnp.float32)
    gate = jnp.zeros((experts, tokens), jnp.float32)
    for k in range(top):
        inside = dot(hits[k].astype(jnp.bfloat16), earlier)
        rank += hits[k] * (inside + base)
        taken += hits[k]
        gate += hits[k] * gates[k : k + 1, :]
        base += jnp.sum(hits[k], axis=1, keepdims=True)
    rank = jnp.where((taken > 0.5) & (rank < CAP), rank, UNUSED)
    out_ref[:experts, :] = rank.astype(jnp.bfloat16)
    out_ref[experts:, :] = gate.astype(jnp.bfloat16)


def rank_table(routes, gates, experts):
    tokens = routes.shape[1]
    return pl.pallas_call(
        functools.partial(rank_kernel, experts),
        out_shape=jax.ShapeDtypeStruct((2 * experts, tokens), jnp.bfloat16),
    )(routes, gates)


def slots_kernel(axis, n, local, *refs):
    table_refs, (pick_ref, place_ref, gate_ref) = refs[:n], refs[n:]
    experts = n * local
    tokens = table_refs[0].shape[1]
    wide = 2 * SLOT
    me = lax.axis_index(axis)
    row = lax.broadcasted_iota(jnp.int32, (2 * experts, tokens), 0)
    slot = lax.broadcasted_iota(jnp.int32, (wide, tokens), 0).astype(jnp.float32)
    for p in range(n // 2):
        tables = [table_refs[2 * p + q][...].astype(jnp.float32) for q in range(2)]
        for j in range(local):
            e = me * local + j
            down = slice(j * wide, (j + 1) * wide)
            gates = jnp.zeros((8, wide), jnp.float32)
            for q in range(2):
                rank = jnp.sum(jnp.where(row == e, tables[q], 0.0), axis=0, keepdims=True)
                gate = jnp.sum(jnp.where(row == e + experts, tables[q], 0.0), axis=0, keepdims=True)
                pick = (slot == rank + q * SLOT).astype(jnp.float32)
                place = pick.T.astype(jnp.bfloat16)
                across = slice(q * tokens, (q + 1) * tokens)
                pick_ref[p, down, across] = pick.astype(jnp.bfloat16)
                place_ref[p, across, down] = place
                gates += dot(jnp.broadcast_to(gate, (8, tokens)).astype(jnp.bfloat16), place)
            gate_ref[j, :, p * wide : (p + 1) * wide] = gates


def slots(axis, n, local, tables):
    tokens = tables[0].shape[1]
    across, down = 2 * tokens, 2 * SLOT * local
    return pl.pallas_call(
        functools.partial(slots_kernel, axis, n, local),
        out_shape=[
            jax.ShapeDtypeStruct((n // 2, down, across), jnp.bfloat16),
            jax.ShapeDtypeStruct((n // 2, across, down), jnp.bfloat16),
            jax.ShapeDtypeStruct((local, 8, n * SLOT), jnp.float32),
        ],
        compiler_params=params(4 * max(1, n // 8)),
    )(*tables)


def gather_rows(local, pick_ref, token_refs, first, out):
    wide = 2 * SLOT
    features = out.shape[2]
    cols = features // 4
    for p in range(len(token_refs) // 2):
        refs = [ref for pair in token_refs[2 * p : 2 * p + 2] for ref in pair]
        for d in range(0, features, cols):
            part = slice(d, d + cols)
            tokens = jnp.concatenate([ref[:, part] for ref in refs], axis=0)
            rows = dot(pick_ref[first + p], tokens).astype(jnp.bfloat16)
            for j in range(local):
                out[j, p * wide : (p + 1) * wide, part] = rows[j * wide : (j + 1) * wide, :]


def gather_columns(local, place_ref, token_refs, first, out):
    wide = 2 * SLOT
    features = out.shape[1]
    size = features // 4
    for p in range(len(token_refs) // 2):
        refs = [ref for pair in token_refs[2 * p : 2 * p + 2] for ref in pair]
        for d in range(0, features, size):
            part = slice(d, d + size)
            tokens = jnp.concatenate([ref[:, part] for ref in refs], axis=0)
            columns = dot(tokens.T, place_ref[first + p]).astype(jnp.bfloat16)
            for j in range(local):
                out[j, part, p * wide : (p + 1) * wide] = columns[:, j * wide : (j + 1) * wide]


def split(refs, counts):
    parts, first = [], 0
    for count in counts:
        parts.append(refs[first : first + count])
        first += count
    return parts, refs[first:]


def flat(groups):
    return [block for blocks in groups for block in blocks]


def sizes(groups):
    return [len(blocks) for blocks in groups]


INSIDE = pl.BlockSpec(memory_space=pltpu.VMEM)
OUTSIDE = pl.BlockSpec(memory_space=pltpu.HBM)
ANYWHERE = pl.BlockSpec(memory_space=pl.ANY)


def vmem(array):
    return pltpu.with_memory_space_constraint(array, pltpu.VMEM)


def hbm(array):
    return pltpu.with_memory_space_constraint(array, pltpu.HBM)


def fetches(source, result, sems):
    return [pltpu.make_async_copy(source.at[e], result.at[e], sems.at[e]) for e in range(source.shape[0])]


def load_kernel(count, *refs):
    sources, (*results, done_ref, sems) = refs[:count], refs[count + 1 :]
    copies = [
        pltpu.make_async_copy(source.at[e], result.at[e], sems.at[i, e])
        for i, (source, result) in enumerate(zip(sources, results))
        for e in range(source.shape[0])
    ]
    for copy in copies:
        copy.start()
    for copy in copies:
        copy.wait()
    done_ref[...] = jnp.zeros_like(done_ref)


def load(arrays, after):
    count = len(arrays)
    return pl.pallas_call(
        functools.partial(load_kernel, count),
        in_specs=[OUTSIDE] * count + [pl.BlockSpec(memory_space=pl.ANY)],
        out_specs=[pl.BlockSpec(memory_space=pltpu.VMEM)] * (count + 1),
        out_shape=[pltpu.VMEM(w.shape, w.dtype) for w in arrays]
        + [jax.ShapeDtypeStruct((8, 128), jnp.float32)],
        scratch_shapes=[pltpu.SemaphoreType.DMA((count, arrays[0].shape[0]))],
        compiler_params=params(1),
        cost_estimate=pl.CostEstimate(
            flops=0, bytes_accessed=4 * count * arrays[0].size, transcendentals=0
        ),
    )(*[pltpu.with_memory_space_constraint(w, pltpu.HBM) for w in arrays], after)


def rows_kernel(local, counts, pick_ref, *refs):
    token_refs, (_, out_ref) = split(refs, counts)
    gather_rows(local, pick_ref, token_refs, 0, out_ref)


def early_rows(local, pick, tokens, after):
    features = tokens[0][0].shape[1]
    return pl.pallas_call(
        functools.partial(rows_kernel, local, sizes(tokens)),
        in_specs=[INSIDE] * (1 + len(flat(tokens))) + [ANYWHERE],
        out_shape=jax.ShapeDtypeStruct((local, 2 * SLOT, features), jnp.bfloat16),
        compiler_params=params(4),
    )(pick, *flat(tokens), after)


def columns_kernel(local, counts, place_ref, *refs):
    token_refs, (_, out_ref) = split(refs, counts)
    gather_columns(local, place_ref, token_refs, 0, out_ref)


def early_columns(local, place, tokens, after):
    features = tokens[0][0].shape[1]
    return pl.pallas_call(
        functools.partial(columns_kernel, local, sizes(tokens)),
        in_specs=[INSIDE] * (1 + len(flat(tokens))) + [ANYWHERE],
        out_shape=jax.ShapeDtypeStruct((local, features, 2 * SLOT), jnp.bfloat16),
        compiler_params=params(4),
    )(place, *flat(tokens), after)


def relay_kernel(x_ref, y_ref, *refs):
    upper_ref, lower_ref = refs[-2:]
    half = upper_ref.shape[0]
    upper_ref[...] = x_ref[:half, :]
    lower_ref[...] = y_ref[half:, :]


def relay_parts(beside, after):
    tokens, features = beside[0].shape
    inside, anywhere = pl.BlockSpec(memory_space=pltpu.VMEM), pl.BlockSpec(memory_space=pl.ANY)
    half = jax.ShapeDtypeStruct((tokens // 2, features), beside[0].dtype)
    return pl.pallas_call(
        relay_kernel,
        in_specs=[inside] * 2 + [anywhere] * len(after),
        out_shape=[half, half],
        compiler_params=params(4),
    )(*beside, *after)


def pass_kernel(array_ref, _, copy_ref):
    copy_ref[...] = array_ref[...]


def passed(array, after):
    return pl.pallas_call(
        pass_kernel,
        in_specs=[pl.BlockSpec(memory_space=pltpu.VMEM), pl.BlockSpec(memory_space=pl.ANY)],
        out_shape=jax.ShapeDtypeStruct(array.shape, array.dtype),
        compiler_params=params(4),
    )(array, after)


def pre_kernel(local, counts, pick_ref, gate_ref, first_ref, *refs):
    token_refs, refs = split(refs, counts)
    wg_ref, wu_ref, a_ref, b_ref, xs = refs
    hidden = wg_ref.shape[2]
    cols = hidden // 2
    gather_rows(local, pick_ref, token_refs, 1, xs)

    @pl.loop(0, local)
    def _(e):
        rows = jnp.concatenate([first_ref[e], xs[e]], axis=0)
        gates = gate_ref[e][:1, :]
        for f in range(0, hidden, cols):
            part = slice(f, f + cols)
            gate_pre = dot(rows, wg_ref[e, :, part])
            up_pre = dot(rows, wu_ref[e, :, part])
            sig = jax.nn.sigmoid(gate_pre)
            a_ref[e, part, :] = (sig * up_pre * (1.0 + gate_pre * (1.0 - sig))).T * gates
            b_ref[e, part, :] = (sig * gate_pre).T * gates


def pre(n, pick, gates, first, tokens, wg, wu):
    local, features, hidden = wg.shape
    rows = n * SLOT
    return pl.pallas_call(
        functools.partial(pre_kernel, local, sizes(tokens)),
        in_specs=[INSIDE] * (5 + len(flat(tokens))),
        out_shape=[
            jax.ShapeDtypeStruct((local, hidden, rows), jnp.float32),
            jax.ShapeDtypeStruct((local, hidden, rows), jnp.float32),
        ],
        scratch_shapes=[pltpu.VMEM((local, rows - 2 * SLOT, features), jnp.bfloat16)],
        compiler_params=params(PRE_MIB * max(1, n // 4)),
        cost_estimate=pl.CostEstimate(
            flops=4 * local * rows * features * hidden,
            bytes_accessed=4 * local * features * hidden,
            transcendentals=local * rows * hidden,
        ),
    )(pick, gates, first, *flat(tokens), vmem(wg), vmem(wu))


def back_kernel(local, counts, place_ref, first_ref, *refs):
    token_refs, refs = split(refs, counts)
    wd_ref, a_ref, b_ref, _, _, hg_ref, hu_ref, gs, weight, sems = refs
    hidden = wd_ref.shape[1]
    cols = hidden // 2
    held = weight.shape[0]

    def fetch(e, i):
        part = pl.ds(i * cols, cols)
        slot = lax.rem(e, held)
        return pltpu.make_async_copy(wd_ref.at[e, part], weight.at[slot, part], sems.at[slot, i])

    for e in range(held):
        for i in range(2):
            fetch(e, i).start()
    gather_columns(local, place_ref, token_refs, 1, gs)

    @pl.loop(0, local)
    def _(e):
        rows = jnp.concatenate([first_ref[e], gs[e]], axis=1)
        for i in range(2):
            part = slice(i * cols, (i + 1) * cols)
            fetch(e, i).wait()
            back = dot(weight[lax.rem(e, held), part, :], rows)
            hg_ref[e, part, :] = (back * a_ref[e, part, :]).astype(jnp.bfloat16)
            hu_ref[e, part, :] = (back * b_ref[e, part, :]).astype(jnp.bfloat16)

            @pl.when(e + held < local)
            def _():
                fetch(e + held, i).start()


def back(n, place, first, tokens, wd, a, b, wg, wu):
    local, hidden, features = wd.shape
    rows = n * SLOT
    shape = jax.ShapeDtypeStruct((local, hidden, rows), jnp.bfloat16)
    return pl.pallas_call(
        functools.partial(back_kernel, local, sizes(tokens)),
        in_specs=[INSIDE] * (2 + len(flat(tokens))) + [OUTSIDE] + [INSIDE] * 4,
        out_shape=[shape, shape],
        scratch_shapes=[
            pltpu.VMEM((local, features, rows - 2 * SLOT), jnp.bfloat16),
            pltpu.VMEM((min(local, 2), hidden, features), jnp.bfloat16),
            pltpu.SemaphoreType.DMA((min(local, 2), 2)),
        ],
        compiler_params=params(BACK_MIB * max(1, n // 4)),
        cost_estimate=pl.CostEstimate(
            flops=2 * local * rows * features * hidden,
            bytes_accessed=2 * local * features * hidden,
            transcendentals=0,
        ),
    )(place, first, *flat(tokens), hbm(wd), a, b, vmem(wg), vmem(wu))


def out_kernel(n, local, orders, chunk, place_ref, hg_ref, hu_ref, wg_ref, wu_ref, *rest):
    outs, rows_ref = rest[:-1], rest[-1]
    wide = 2 * SLOT
    cols = wg_ref.shape[1] // CHUNKS
    part = slice(chunk * cols, (chunk + 1) * cols)
    for e in range(local):
        rows = dot(wg_ref[e, part, :], hg_ref[e]) + dot(wu_ref[e, part, :], hu_ref[e])
        rows = rows.astype(jnp.bfloat16)
        for p in range(n // 2):
            rows_ref[p, :, e * wide : (e + 1) * wide] = rows[:, p * wide : (p + 1) * wide]
    tokens = place_ref.shape[1] // 2
    for p in range(n // 2):
        total = dot(place_ref[p], rows_ref[p], NT)
        for out_ref, order in zip(outs, orders):
            for i, g in enumerate(order):
                if g // 2 == p:
                    mine = total[g % 2 * tokens : (g % 2 + 1) * tokens, :]
                    out_ref[i] = mine.astype(out_ref.dtype)


def partial_sums(n, orders, chunk, place, hg, hu, wg, wu):
    local, features, hidden = wg.shape
    tokens = place.shape[1] // 2
    rows = n * SLOT
    cols = features // CHUNKS
    shapes = [(len(order), tokens, cols) for order in orders]
    types = [jnp.float32] + [jnp.bfloat16] * (len(orders) - 1)
    return pl.pallas_call(
        functools.partial(out_kernel, n, local, orders, chunk),
        out_shape=[jax.ShapeDtypeStruct(s, t) for s, t in zip(shapes, types)],
        scratch_shapes=[pltpu.VMEM((n // 2, cols, 2 * SLOT * local), jnp.bfloat16)],
        compiler_params=params(OUT_MIB * max(1, n // 4)),
        cost_estimate=pl.CostEstimate(
            flops=local * rows * cols * hidden,
            bytes_accessed=local * cols * hidden,
            transcendentals=0,
        ),
    )(place, hg, hu, vmem(wg), vmem(wu))


def sum_kernel(*refs):
    parts, out_ref = refs[:-1], refs[-1]
    each = len(parts) // CHUNKS
    cols = out_ref.shape[1] // CHUNKS
    for c in range(CHUNKS):
        own, *others = parts[c * each : (c + 1) * each]
        total = own[0]
        for other in others:
            total += other[0].astype(jnp.float32)
        out_ref[:, c * cols : (c + 1) * cols] = total.astype(jnp.bfloat16)


def body(axis, saved_input, grad_out, routes, route_gates, gate_proj, up_proj, down_proj):
    n = lax.axis_size(axis)
    local = gate_proj.shape[0]
    experts = n * local
    tokens, features = saved_input.shape

    def swap(array, k):
        return lax.ppermute(array, axis, [(i, i ^ k) for i in range(n)])

    table = rank_table(routes.T, route_gates.T, experts)
    tables = [table] + [swap(table, k) for k in range(1, n)]
    pick, place, gates = slots(axis, n, local, tables)
    gate_proj, up_proj, done = load((gate_proj, up_proj), table)
    if n == 4:
        x_near = [swap(saved_input, 1), swap(saved_input, 2)]
        upper, lower = relay_parts(x_near, [done, place])
        sent = passed(grad_out, upper)
        x_blocks = [[saved_input], *[[x] for x in x_near], [swap(upper, 2), swap(lower, 1)]]
        g_near = [swap(sent, 1), swap(sent, 2)]
    else:
        x_blocks = [[saved_input]] + [[swap(saved_input, k)] for k in range(1, n)]
        sent = grad_out
    x_first = early_rows(local, pick, x_blocks[:2], sent)
    a, b = pre(n, pick, gates, x_first, x_blocks[2:], gate_proj, up_proj)
    if n == 4:
        upper, lower = relay_parts(g_near, [a])
        g_blocks = [[sent], *[[g] for g in g_near], [swap(upper, 2), swap(lower, 1)]]
    else:
        g_blocks = [[grad_out]] + [[swap(grad_out, k)] for k in range(1, n)]
        upper = a
    g_first = early_columns(local, place, g_blocks[:2], upper)
    hg, hu = back(n, place, g_first, g_blocks[2:], down_proj, a, b, gate_proj, up_proj)
    parts = []
    for chunk in range(CHUNKS):
        if n == 4:
            first, last = (1, 2) if chunk % 2 == 0 else (2, 1)
            orders = ((0,), (first, 3), (last,))
            own, two, one = partial_sums(n, orders, chunk, place, hg, hu, gate_proj, up_proj)
            two = swap(two, first)
            mixed = (two[1:2].astype(jnp.float32) + one.astype(jnp.float32)).astype(jnp.bfloat16)
            parts += [own, two[:1], swap(mixed, last)]
        else:
            orders = tuple((k,) for k in range(n))
            own, *others = partial_sums(n, orders, chunk, place, hg, hu, gate_proj, up_proj)
            parts += [own] + [swap(other, k + 1) for k, other in enumerate(others)]
    return pl.pallas_call(
        sum_kernel,
        out_shape=jax.ShapeDtypeStruct((tokens, features), jnp.bfloat16),
        compiler_params=params(8),
    )(*parts)


def solution(mesh):
    tokens = P(("dp", "expert"), None)
    weights = P("expert", None, None)
    return jax.shard_map(
        functools.partial(body, "expert"),
        mesh=mesh,
        in_specs=(tokens, tokens, tokens, tokens, weights, weights, weights),
        out_specs=tokens,
        check_vma=False,
    )
```

```python
import functools

import jax
import jax.numpy as jnp
from jax import lax
from jax.experimental import pallas as pl
from jax.experimental.pallas import tpu as pltpu
from jax.sharding import PartitionSpec as P

CAP = 56
SLOT = 64
UNUSED = 200.0
MIB = 1 << 20
CHUNKS = 4
PRE_MIB = 6
BACK_MIB = 10
OUT_MIB = 4

NT = (((1,), (1,)), ((), ()))


def dot(a, b, dims=(((1,), (0,)), ((), ()))):
    return lax.dot_general(a, b, dims, preferred_element_type=jnp.float32)


def params(limit):
    return pltpu.CompilerParams(vmem_limit_bytes=limit * MIB)


def rank_kernel(experts, routes_ref, gates_ref, out_ref):
    top, tokens = routes_ref.shape
    chosen = routes_ref[...].astype(jnp.float32)
    gates = gates_ref[...].astype(jnp.float32)
    label = lax.broadcasted_iota(jnp.int32, (experts, tokens), 0).astype(jnp.float32)
    hits = [(chosen[k : k + 1, :] == label).astype(jnp.float32) for k in range(top)]
    before = lax.broadcasted_iota(jnp.int32, (tokens, tokens), 0)
    after = lax.broadcasted_iota(jnp.int32, (tokens, tokens), 1)
    earlier = (before < after).astype(jnp.bfloat16)
    base = jnp.zeros((experts, 1), jnp.float32)
    rank = jnp.zeros((experts, tokens), jnp.float32)
    taken = jnp.zeros((experts, tokens), jnp.float32)
    gate = jnp.zeros((experts, tokens), jnp.float32)
    for k in range(top):
        inside = dot(hits[k].astype(jnp.bfloat16), earlier)
        rank += hits[k] * (inside + base)
        taken += hits[k]
        gate += hits[k] * gates[k : k + 1, :]
        base += jnp.sum(hits[k], axis=1, keepdims=True)
    rank = jnp.where((taken > 0.5) & (rank < CAP), rank, UNUSED)
    out_ref[:experts, :] = rank.astype(jnp.bfloat16)
    out_ref[experts:, :] = gate.astype(jnp.bfloat16)


def rank_table(routes, gates, experts):
    tokens = routes.shape[1]
    return pl.pallas_call(
        functools.partial(rank_kernel, experts),
        out_shape=jax.ShapeDtypeStruct((2 * experts, tokens), jnp.bfloat16),
    )(routes, gates)


def slots_kernel(axis, n, local, *refs):
    table_refs, (pick_ref, place_ref, gate_ref) = refs[:n], refs[n:]
    experts = n * local
    tokens = table_refs[0].shape[1]
    wide = 2 * SLOT
    me = lax.axis_index(axis)
    row = lax.broadcasted_iota(jnp.int32, (2 * experts, tokens), 0)
    slot = lax.broadcasted_iota(jnp.int32, (wide, tokens), 0).astype(jnp.float32)
    for p in range(n // 2):
        tables = [table_refs[2 * p + q][...].astype(jnp.float32) for q in range(2)]
        for j in range(local):
            e = me * local + j
            down = slice(j * wide, (j + 1) * wide)
            gates = jnp.zeros((8, wide), jnp.float32)
            for q in range(2):
                rank = jnp.sum(jnp.where(row == e, tables[q], 0.0), axis=0, keepdims=True)
                gate = jnp.sum(jnp.where(row == e + experts, tables[q], 0.0), axis=0, keepdims=True)
                pick = (slot == rank + q * SLOT).astype(jnp.float32)
                place = pick.T.astype(jnp.bfloat16)
                across = slice(q * tokens, (q + 1) * tokens)
                pick_ref[p, down, across] = pick.astype(jnp.bfloat16)
                place_ref[p, across, down] = place
                gates += dot(jnp.broadcast_to(gate, (8, tokens)).astype(jnp.bfloat16), place)
            gate_ref[j, :, p * wide : (p + 1) * wide] = gates


def slots(axis, n, local, tables):
    tokens = tables[0].shape[1]
    across, down = 2 * tokens, 2 * SLOT * local
    return pl.pallas_call(
        functools.partial(slots_kernel, axis, n, local),
        out_shape=[
            jax.ShapeDtypeStruct((n // 2, down, across), jnp.bfloat16),
            jax.ShapeDtypeStruct((n // 2, across, down), jnp.bfloat16),
            jax.ShapeDtypeStruct((local, 8, n * SLOT), jnp.float32),
        ],
        compiler_params=params(4 * max(1, n // 8)),
    )(*tables)


def gather_rows(local, pick_ref, token_refs, first, out):
    wide = 2 * SLOT
    features = out.shape[2]
    cols = features // 4
    for p in range(len(token_refs) // 2):
        refs = [ref for pair in token_refs[2 * p : 2 * p + 2] for ref in pair]
        for d in range(0, features, cols):
            part = slice(d, d + cols)
            tokens = jnp.concatenate([ref[:, part] for ref in refs], axis=0)
            rows = dot(pick_ref[first + p], tokens).astype(jnp.bfloat16)
            for j in range(local):
                out[j, p * wide : (p + 1) * wide, part] = rows[j * wide : (j + 1) * wide, :]


def gather_columns(local, place_ref, token_refs, first, out):
    wide = 2 * SLOT
    features = out.shape[1]
    size = features // 4
    for p in range(len(token_refs) // 2):
        refs = [ref for pair in token_refs[2 * p : 2 * p + 2] for ref in pair]
        for d in range(0, features, size):
            part = slice(d, d + size)
            tokens = jnp.concatenate([ref[:, part] for ref in refs], axis=0)
            columns = dot(tokens.T, place_ref[first + p]).astype(jnp.bfloat16)
            for j in range(local):
                out[j, part, p * wide : (p + 1) * wide] = columns[:, j * wide : (j + 1) * wide]


def split(refs, counts):
    parts, first = [], 0
    for count in counts:
        parts.append(refs[first : first + count])
        first += count
    return parts, refs[first:]


def flat(groups):
    return [block for blocks in groups for block in blocks]


def sizes(groups):
    return [len(blocks) for blocks in groups]


INSIDE = pl.BlockSpec(memory_space=pltpu.VMEM)
OUTSIDE = pl.BlockSpec(memory_space=pltpu.HBM)
ANYWHERE = pl.BlockSpec(memory_space=pl.ANY)


def vmem(array):
    return pltpu.with_memory_space_constraint(array, pltpu.VMEM)


def hbm(array):
    return pltpu.with_memory_space_constraint(array, pltpu.HBM)


def fetches(source, result, sems):
    return [pltpu.make_async_copy(source.at[e], result.at[e], sems.at[e]) for e in range(source.shape[0])]


def load_kernel(count, *refs):
    sources, (*results, done_ref, sems) = refs[:count], refs[count + 1 :]
    copies = [
        pltpu.make_async_copy(source.at[e], result.at[e], sems.at[i, e])
        for i, (source, result) in enumerate(zip(sources, results))
        for e in range(source.shape[0])
    ]
    for copy in copies:
        copy.start()
    for copy in copies:
        copy.wait()
    done_ref[...] = jnp.zeros_like(done_ref)


def load(arrays, after):
    count = len(arrays)
    return pl.pallas_call(
        functools.partial(load_kernel, count),
        in_specs=[OUTSIDE] * count + [pl.BlockSpec(memory_space=pl.ANY)],
        out_specs=[pl.BlockSpec(memory_space=pltpu.VMEM)] * (count + 1),
        out_shape=[pltpu.VMEM(w.shape, w.dtype) for w in arrays]
        + [jax.ShapeDtypeStruct((8, 128), jnp.float32)],
        scratch_shapes=[pltpu.SemaphoreType.DMA((count, arrays[0].shape[0]))],
        compiler_params=params(1),
        cost_estimate=pl.CostEstimate(
            flops=0, bytes_accessed=4 * count * arrays[0].size, transcendentals=0
        ),
    )(*[pltpu.with_memory_space_constraint(w, pltpu.HBM) for w in arrays], after)


def rows_kernel(local, counts, first, pick_ref, *refs):
    token_refs, (_, out_ref) = split(refs, counts)
    gather_rows(local, pick_ref, token_refs, first, out_ref)


def slot_rows(local, pick, tokens, first, after):
    features = tokens[0][0].shape[1]
    return pl.pallas_call(
        functools.partial(rows_kernel, local, sizes(tokens), first),
        in_specs=[INSIDE] * (1 + len(flat(tokens))) + [ANYWHERE],
        out_shape=jax.ShapeDtypeStruct((local, len(tokens) * SLOT, features), jnp.bfloat16),
        compiler_params=params(4),
    )(pick, *flat(tokens), after)


def columns_kernel(local, counts, place_ref, *refs):
    token_refs, (_, out_ref) = split(refs, counts)
    gather_columns(local, place_ref, token_refs, 0, out_ref)


def early_columns(local, place, tokens, after):
    features = tokens[0][0].shape[1]
    return pl.pallas_call(
        functools.partial(columns_kernel, local, sizes(tokens)),
        in_specs=[INSIDE] * (1 + len(flat(tokens))) + [ANYWHERE],
        out_shape=jax.ShapeDtypeStruct((local, features, 2 * SLOT), jnp.bfloat16),
        compiler_params=params(4),
    )(place, *flat(tokens), after)


def relay_kernel(x_ref, y_ref, *refs):
    upper_ref, lower_ref = refs[-2:]
    half = upper_ref.shape[0]
    upper_ref[...] = x_ref[:half, :]
    lower_ref[...] = y_ref[half:, :]


def relay_parts(beside, after):
    tokens, features = beside[0].shape
    inside, anywhere = pl.BlockSpec(memory_space=pltpu.VMEM), pl.BlockSpec(memory_space=pl.ANY)
    half = jax.ShapeDtypeStruct((tokens // 2, features), beside[0].dtype)
    return pl.pallas_call(
        relay_kernel,
        in_specs=[inside] * 2 + [anywhere] * len(after),
        out_shape=[half, half],
        compiler_params=params(4),
    )(*beside, *after)


def pass_kernel(array_ref, _, copy_ref):
    copy_ref[...] = array_ref[...]


def passed(array, after):
    return pl.pallas_call(
        pass_kernel,
        in_specs=[pl.BlockSpec(memory_space=pltpu.VMEM), pl.BlockSpec(memory_space=pl.ANY)],
        out_shape=jax.ShapeDtypeStruct(array.shape, array.dtype),
        compiler_params=params(4),
    )(array, after)


def pre_kernel(experts, gate_ref, first_ref, rest_ref, wg_ref, wu_ref, _, a_ref, b_ref):
    hidden = wg_ref.shape[2]
    cols = hidden // 2
    for i, e in enumerate(experts):
        rows = jnp.concatenate([first_ref[e], rest_ref[e]], axis=0)
        gates = gate_ref[e][:1, :]
        for f in range(0, hidden, cols):
            part = slice(f, f + cols)
            gate_pre = dot(rows, wg_ref[e, :, part])
            up_pre = dot(rows, wu_ref[e, :, part])
            sig = jax.nn.sigmoid(gate_pre)
            a_ref[i, part, :] = ((sig * up_pre * (1.0 + gate_pre * (1.0 - sig))).T * gates).astype(jnp.bfloat16)
            b_ref[i, part, :] = ((sig * gate_pre).T * gates).astype(jnp.bfloat16)


def pre(n, experts, gates, first, rest, wg, wu, after):
    local, features, hidden = wg.shape
    rows, count = n * SLOT, len(experts)
    shape = jax.ShapeDtypeStruct((count, hidden, rows), jnp.bfloat16)
    return pl.pallas_call(
        functools.partial(pre_kernel, experts),
        in_specs=[INSIDE] * 5 + [ANYWHERE],
        out_shape=[shape, shape],
        compiler_params=params(PRE_MIB * max(1, n // 4)),
        cost_estimate=pl.CostEstimate(
            flops=4 * count * rows * features * hidden,
            bytes_accessed=4 * count * features * hidden,
            transcendentals=count * rows * hidden,
        ),
    )(gates, first, rest, vmem(wg), vmem(wu), after)


def back_kernel(local, counts, halves, place_ref, first_ref, *refs):
    token_refs, (wd_ref, *refs) = split(refs, counts)
    factor_refs, (_, _, hg_ref, hu_ref, gs, weight, sems) = refs[: 2 * halves], refs[2 * halves :]
    factors = [
        (a_ref, b_ref, i)
        for a_ref, b_ref in zip(factor_refs[::2], factor_refs[1::2])
        for i in range(a_ref.shape[0])
    ]
    hidden = wd_ref.shape[1]
    cols = hidden // 2
    held = weight.shape[0]

    def fetch(e, i):
        part = pl.ds(i * cols, cols)
        slot = e % held
        return pltpu.make_async_copy(wd_ref.at[e, part], weight.at[slot, part], sems.at[slot, i])

    for e in range(held):
        for i in range(2):
            fetch(e, i).start()
    gather_columns(local, place_ref, token_refs, 1, gs)

    for e, (a_ref, b_ref, at) in enumerate(factors):
        rows = jnp.concatenate([first_ref[e], gs[e]], axis=1)
        for i in range(2):
            part = slice(i * cols, (i + 1) * cols)
            fetch(e, i).wait()
            back = dot(weight[e % held, part, :], rows)
            hg_ref[e, part, :] = (back * a_ref[at, part, :]).astype(jnp.bfloat16)
            hu_ref[e, part, :] = (back * b_ref[at, part, :]).astype(jnp.bfloat16)
            if e + held < local:
                fetch(e + held, i).start()


def back(n, place, first, tokens, wd, factors, wg, wu):
    local, hidden, features = wd.shape
    rows = n * SLOT
    shape = jax.ShapeDtypeStruct((local, hidden, rows), jnp.bfloat16)
    return pl.pallas_call(
        functools.partial(back_kernel, local, sizes(tokens), len(factors)),
        in_specs=[INSIDE] * (2 + len(flat(tokens))) + [OUTSIDE] + [INSIDE] * (2 * len(factors) + 2),
        out_shape=[shape, shape],
        scratch_shapes=[
            pltpu.VMEM((local, features, rows - 2 * SLOT), jnp.bfloat16),
            pltpu.VMEM((min(local, 2), hidden, features), jnp.bfloat16),
            pltpu.SemaphoreType.DMA((min(local, 2), 2)),
        ],
        compiler_params=params(BACK_MIB * max(1, n // 4)),
        cost_estimate=pl.CostEstimate(
            flops=2 * local * rows * features * hidden,
            bytes_accessed=2 * local * features * hidden,
            transcendentals=0,
        ),
    )(place, first, *flat(tokens), hbm(wd), *flat(factors), vmem(wg), vmem(wu))


def out_kernel(n, local, orders, chunk, place_ref, hg_ref, hu_ref, wg_ref, wu_ref, *rest):
    outs, rows_ref = rest[:-1], rest[-1]
    wide = 2 * SLOT
    cols = wg_ref.shape[1] // CHUNKS
    part = slice(chunk * cols, (chunk + 1) * cols)
    for e in range(local):
        rows = dot(wg_ref[e, part, :], hg_ref[e]) + dot(wu_ref[e, part, :], hu_ref[e])
        rows = rows.astype(jnp.bfloat16)
        for p in range(n // 2):
            rows_ref[p, :, e * wide : (e + 1) * wide] = rows[:, p * wide : (p + 1) * wide]
    tokens = place_ref.shape[1] // 2
    for p in range(n // 2):
        total = dot(place_ref[p], rows_ref[p], NT)
        for out_ref, order in zip(outs, orders):
            for i, g in enumerate(order):
                if g // 2 == p:
                    mine = total[g % 2 * tokens : (g % 2 + 1) * tokens, :]
                    out_ref[i] = mine.astype(out_ref.dtype)


def partial_sums(n, orders, chunk, place, hg, hu, wg, wu):
    local, features, hidden = wg.shape
    tokens = place.shape[1] // 2
    rows = n * SLOT
    cols = features // CHUNKS
    shapes = [(len(order), tokens, cols) for order in orders]
    types = [jnp.float32] + [jnp.bfloat16] * (len(orders) - 1)
    return pl.pallas_call(
        functools.partial(out_kernel, n, local, orders, chunk),
        out_shape=[jax.ShapeDtypeStruct(s, t) for s, t in zip(shapes, types)],
        scratch_shapes=[pltpu.VMEM((n // 2, cols, 2 * SLOT * local), jnp.bfloat16)],
        compiler_params=params(OUT_MIB * max(1, n // 4)),
        cost_estimate=pl.CostEstimate(
            flops=local * rows * cols * hidden,
            bytes_accessed=local * cols * hidden,
            transcendentals=0,
        ),
    )(place, hg, hu, vmem(wg), vmem(wu))


def sum_kernel(*refs):
    parts, out_ref = refs[:-1], refs[-1]
    each = len(parts) // CHUNKS
    cols = out_ref.shape[1] // CHUNKS
    for c in range(CHUNKS):
        own, *others = parts[c * each : (c + 1) * each]
        total = own[0]
        for other in others:
            total += other[0].astype(jnp.float32)
        out_ref[:, c * cols : (c + 1) * cols] = total.astype(jnp.bfloat16)


def body(axis, saved_input, grad_out, routes, route_gates, gate_proj, up_proj, down_proj):
    n = lax.axis_size(axis)
    local = gate_proj.shape[0]
    experts = n * local
    tokens, features = saved_input.shape

    def swap(array, k):
        return lax.ppermute(array, axis, [(i, i ^ k) for i in range(n)])

    table = rank_table(routes.T, route_gates.T, experts)
    tables = [table] + [swap(table, k) for k in range(1, n)]
    pick, place, gates = slots(axis, n, local, tables)
    gate_proj, up_proj, done = load((gate_proj, up_proj), table)
    if n == 4:
        x_near = [swap(saved_input, 1), swap(saved_input, 2)]
        upper, lower = relay_parts(x_near, [done, place])
        sent = passed(grad_out, upper)
        x_blocks = [[saved_input], *[[x] for x in x_near], [swap(upper, 2), swap(lower, 1)]]
        g_near = [swap(sent, 1), swap(sent, 2)]
    else:
        x_blocks = [[saved_input]] + [[swap(saved_input, k)] for k in range(1, n)]
        sent = grad_out
    x_first = slot_rows(local, pick, x_blocks[:2], 0, sent)
    x_rest = slot_rows(local, pick, x_blocks[2:], 1, sent)
    half = (local + 1) // 2
    factors = [pre(n, range(half), gates, x_first, x_rest, gate_proj, up_proj, table)]
    if n == 4:
        upper, lower = relay_parts(g_near, [factors[0][0]])
        g_blocks = [[sent], *[[g] for g in g_near], [swap(upper, 2), swap(lower, 1)]]
    else:
        g_blocks = [[grad_out]] + [[swap(grad_out, k)] for k in range(1, n)]
        upper = table
    if half < local:
        factors.append(pre(n, range(half, local), gates, x_first, x_rest, gate_proj, up_proj, upper))
    g_first = early_columns(local, place, g_blocks[:2], upper)
    hg, hu = back(n, place, g_first, g_blocks[2:], down_proj, factors, gate_proj, up_proj)
    parts = []
    for chunk in range(CHUNKS):
        if n == 4:
            first, last = (1, 2) if chunk % 2 == 0 else (2, 1)
            orders = ((0,), (first, 3), (last,))
            own, two, one = partial_sums(n, orders, chunk, place, hg, hu, gate_proj, up_proj)
            two = swap(two, first)
            mixed = (two[1:2].astype(jnp.float32) + one.astype(jnp.float32)).astype(jnp.bfloat16)
            parts += [own, two[:1], swap(mixed, last)]
        else:
            orders = tuple((k,) for k in range(n))
            own, *others = partial_sums(n, orders, chunk, place, hg, hu, gate_proj, up_proj)
            parts += [own] + [swap(other, k + 1) for k, other in enumerate(others)]
    return pl.pallas_call(
        sum_kernel,
        out_shape=jax.ShapeDtypeStruct((tokens, features), jnp.bfloat16),
        compiler_params=params(8),
    )(*parts)


def solution(mesh):
    tokens = P(("dp", "expert"), None)
    weights = P("expert", None, None)
    return jax.shard_map(
        functools.partial(body, "expert"),
        mesh=mesh,
        in_specs=(tokens, tokens, tokens, tokens, weights, weights, weights),
        out_specs=tokens,
        check_vma=False,
    )
```

```python
import functools

import jax
import jax.numpy as jnp
from jax import lax
from jax.experimental import pallas as pl
from jax.experimental.pallas import tpu as pltpu
from jax.sharding import PartitionSpec as P

CAP = 56
SLOT = 64
UNUSED = 200.0
MIB = 1 << 20
CHUNKS = 4
RING = 8
COPIES = 4
PRE_MIB = 6
BACK_MIB = 18
OUT_MIB = 12

NT = (((1,), (1,)), ((), ()))


def dot(a, b, dims=(((1,), (0,)), ((), ()))):
    return lax.dot_general(a, b, dims, preferred_element_type=jnp.float32)


def params(limit):
    return pltpu.CompilerParams(vmem_limit_bytes=limit * MIB)


def rank_kernel(experts, routes_ref, gates_ref, out_ref):
    top, tokens = routes_ref.shape
    chosen = routes_ref[...].astype(jnp.float32)
    gates = gates_ref[...].astype(jnp.float32)
    label = lax.broadcasted_iota(jnp.int32, (experts, tokens), 0).astype(jnp.float32)
    hits = [(chosen[k : k + 1, :] == label).astype(jnp.float32) for k in range(top)]
    before = lax.broadcasted_iota(jnp.int32, (tokens, tokens), 0)
    after = lax.broadcasted_iota(jnp.int32, (tokens, tokens), 1)
    earlier = (before < after).astype(jnp.bfloat16)
    base = jnp.zeros((experts, 1), jnp.float32)
    rank = jnp.zeros((experts, tokens), jnp.float32)
    taken = jnp.zeros((experts, tokens), jnp.float32)
    gate = jnp.zeros((experts, tokens), jnp.float32)
    for k in range(top):
        inside = dot(hits[k].astype(jnp.bfloat16), earlier)
        rank += hits[k] * (inside + base)
        taken += hits[k]
        gate += hits[k] * gates[k : k + 1, :]
        base += jnp.sum(hits[k], axis=1, keepdims=True)
    rank = jnp.where((taken > 0.5) & (rank < CAP), rank, UNUSED)
    out_ref[:experts, :] = rank.astype(jnp.bfloat16)
    out_ref[experts:, :] = gate.astype(jnp.bfloat16)


def rank_table(routes, gates, experts):
    tokens = routes.shape[1]
    return pl.pallas_call(
        functools.partial(rank_kernel, experts),
        out_shape=jax.ShapeDtypeStruct((2 * experts, tokens), jnp.bfloat16),
    )(routes, gates)


def slots_kernel(axis, n, local, *refs):
    table_refs, (pick_ref, place_ref, gate_ref) = refs[:n], refs[n:]
    experts = n * local
    tokens = table_refs[0].shape[1]
    wide = 2 * SLOT
    me = lax.axis_index(axis)
    row = lax.broadcasted_iota(jnp.int32, (2 * experts, tokens), 0)
    slot = lax.broadcasted_iota(jnp.int32, (wide, tokens), 0).astype(jnp.float32)
    for p in range(n // 2):
        tables = [table_refs[2 * p + q][...].astype(jnp.float32) for q in range(2)]
        for j in range(local):
            e = me * local + j
            down = slice(j * wide, (j + 1) * wide)
            gates = jnp.zeros((8, wide), jnp.float32)
            for q in range(2):
                rank = jnp.sum(jnp.where(row == e, tables[q], 0.0), axis=0, keepdims=True)
                gate = jnp.sum(jnp.where(row == e + experts, tables[q], 0.0), axis=0, keepdims=True)
                pick = (slot == rank + q * SLOT).astype(jnp.float32)
                place = pick.T.astype(jnp.bfloat16)
                across = slice(q * tokens, (q + 1) * tokens)
                pick_ref[p, down, across] = pick.astype(jnp.bfloat16)
                place_ref[p, across, down] = place
                gates += dot(jnp.broadcast_to(gate, (8, tokens)).astype(jnp.bfloat16), place)
            gate_ref[j, :, p * wide : (p + 1) * wide] = gates


def slots(axis, n, local, tables):
    tokens = tables[0].shape[1]
    across, down = 2 * tokens, 2 * SLOT * local
    return pl.pallas_call(
        functools.partial(slots_kernel, axis, n, local),
        out_shape=[
            jax.ShapeDtypeStruct((n // 2, down, across), jnp.bfloat16),
            jax.ShapeDtypeStruct((n // 2, across, down), jnp.bfloat16),
            jax.ShapeDtypeStruct((local, 8, n * SLOT), jnp.float32),
        ],
        compiler_params=params(4 * max(1, n // 8)),
    )(*tables)


def gather_rows(local, pick_ref, token_refs, first, out):
    wide = 2 * SLOT
    features = out.shape[2]
    cols = features // 4
    for p in range(len(token_refs) // 2):
        refs = [ref for pair in token_refs[2 * p : 2 * p + 2] for ref in pair]
        for d in range(0, features, cols):
            part = slice(d, d + cols)
            tokens = jnp.concatenate([ref[:, part] for ref in refs], axis=0)
            rows = dot(pick_ref[first + p], tokens).astype(jnp.bfloat16)
            for j in range(local):
                out[j, p * wide : (p + 1) * wide, part] = rows[j * wide : (j + 1) * wide, :]


def gather_columns(local, place_ref, token_refs, first, out):
    wide = 2 * SLOT
    features = out.shape[1]
    size = features // 4
    for p in range(len(token_refs) // 2):
        refs = [ref for pair in token_refs[2 * p : 2 * p + 2] for ref in pair]
        for d in range(0, features, size):
            part = slice(d, d + size)
            tokens = jnp.concatenate([ref[:, part] for ref in refs], axis=0)
            columns = dot(tokens.T, place_ref[first + p]).astype(jnp.bfloat16)
            for j in range(local):
                out[j, part, p * wide : (p + 1) * wide] = columns[:, j * wide : (j + 1) * wide]


def split(refs, counts):
    parts, first = [], 0
    for count in counts:
        parts.append(refs[first : first + count])
        first += count
    return parts, refs[first:]


def flat(groups):
    return [block for blocks in groups for block in blocks]


def sizes(groups):
    return [len(blocks) for blocks in groups]


INSIDE = pl.BlockSpec(memory_space=pltpu.VMEM)
OUTSIDE = pl.BlockSpec(memory_space=pltpu.HBM)
ANYWHERE = pl.BlockSpec(memory_space=pl.ANY)


def vmem(array):
    return pltpu.with_memory_space_constraint(array, pltpu.VMEM)


def hbm(array):
    return pltpu.with_memory_space_constraint(array, pltpu.HBM)


def fetches(source, result, sems):
    return [pltpu.make_async_copy(source.at[e], result.at[e], sems.at[e]) for e in range(source.shape[0])]


def load_kernel(count, *refs):
    sources, (*results, done_ref, sems) = refs[:count], refs[count + 1 :]
    copies = [
        pltpu.make_async_copy(source.at[e], result.at[e], sems.at[i, e])
        for i, (source, result) in enumerate(zip(sources, results))
        for e in range(source.shape[0])
    ]
    for copy in copies:
        copy.start()
    for copy in copies:
        copy.wait()
    done_ref[...] = jnp.zeros_like(done_ref)


def load(arrays, after):
    count = len(arrays)
    return pl.pallas_call(
        functools.partial(load_kernel, count),
        in_specs=[OUTSIDE] * count + [pl.BlockSpec(memory_space=pl.ANY)],
        out_specs=[pl.BlockSpec(memory_space=pltpu.VMEM)] * (count + 1),
        out_shape=[pltpu.VMEM(w.shape, w.dtype) for w in arrays]
        + [jax.ShapeDtypeStruct((8, 128), jnp.float32)],
        scratch_shapes=[pltpu.SemaphoreType.DMA((count, arrays[0].shape[0]))],
        compiler_params=params(1),
        cost_estimate=pl.CostEstimate(
            flops=0, bytes_accessed=4 * count * arrays[0].size, transcendentals=0
        ),
    )(*[pltpu.with_memory_space_constraint(w, pltpu.HBM) for w in arrays], after)


def rows_kernel(local, counts, first, pick_ref, *refs):
    token_refs, (_, out_ref) = split(refs, counts)
    gather_rows(local, pick_ref, token_refs, first, out_ref)


def slot_rows(local, pick, tokens, first, after):
    features = tokens[0][0].shape[1]
    return pl.pallas_call(
        functools.partial(rows_kernel, local, sizes(tokens), first),
        in_specs=[INSIDE] * (1 + len(flat(tokens))) + [ANYWHERE],
        out_shape=jax.ShapeDtypeStruct((local, len(tokens) * SLOT, features), jnp.bfloat16),
        compiler_params=params(4),
    )(pick, *flat(tokens), after)


def columns_kernel(local, counts, place_ref, *refs):
    token_refs, (_, out_ref) = split(refs, counts)
    gather_columns(local, place_ref, token_refs, 0, out_ref)


def early_columns(local, place, tokens, after):
    features = tokens[0][0].shape[1]
    return pl.pallas_call(
        functools.partial(columns_kernel, local, sizes(tokens)),
        in_specs=[INSIDE] * (1 + len(flat(tokens))) + [ANYWHERE],
        out_shape=jax.ShapeDtypeStruct((local, features, 2 * SLOT), jnp.bfloat16),
        compiler_params=params(4),
    )(place, *flat(tokens), after)


def relay_kernel(x_ref, y_ref, *refs):
    upper_ref, lower_ref = refs[-2:]
    half = upper_ref.shape[0]
    upper_ref[...] = x_ref[:half, :]
    lower_ref[...] = y_ref[half:, :]


def relay_parts(beside, after):
    tokens, features = beside[0].shape
    inside, anywhere = pl.BlockSpec(memory_space=pltpu.VMEM), pl.BlockSpec(memory_space=pl.ANY)
    half = jax.ShapeDtypeStruct((tokens // 2, features), beside[0].dtype)
    return pl.pallas_call(
        relay_kernel,
        in_specs=[inside] * 2 + [anywhere] * len(after),
        out_shape=[half, half],
        compiler_params=params(4),
    )(*beside, *after)


def pass_kernel(array_ref, _, copy_ref):
    copy_ref[...] = array_ref[...]


def passed(array, after):
    return pl.pallas_call(
        pass_kernel,
        in_specs=[pl.BlockSpec(memory_space=pltpu.VMEM), pl.BlockSpec(memory_space=pl.ANY)],
        out_shape=jax.ShapeDtypeStruct(array.shape, array.dtype),
        compiler_params=params(4),
    )(array, after)


def pre_kernel(experts, gate_ref, first_ref, rest_ref, wg_ref, wu_ref, _, a_ref, b_ref):
    hidden = wg_ref.shape[2]
    cols = hidden // 2
    for i, e in enumerate(experts):
        rows = jnp.concatenate([first_ref[e], rest_ref[e]], axis=0)
        gates = gate_ref[e][:1, :]
        for f in range(0, hidden, cols):
            part = slice(f, f + cols)
            gate_pre = dot(rows, wg_ref[e, :, part])
            up_pre = dot(rows, wu_ref[e, :, part])
            sig = jax.nn.sigmoid(gate_pre)
            a_ref[i, part, :] = (sig * up_pre * (1.0 + gate_pre * (1.0 - sig))).T * gates
            b_ref[i, part, :] = (sig * gate_pre).T * gates


def pre(n, experts, gates, first, rest, wg, wu, after):
    local, features, hidden = wg.shape
    rows, count = n * SLOT, len(experts)
    shape = jax.ShapeDtypeStruct((count, hidden, rows), jnp.float32)
    return pl.pallas_call(
        functools.partial(pre_kernel, experts),
        in_specs=[INSIDE] * 5 + [ANYWHERE],
        out_shape=[shape, shape],
        compiler_params=params(PRE_MIB * max(1, n // 4)),
        cost_estimate=pl.CostEstimate(
            flops=4 * count * rows * features * hidden,
            bytes_accessed=4 * count * features * hidden,
            transcendentals=count * rows * hidden,
        ),
    )(gates, first, rest, vmem(wg), vmem(wu), after)


def back_kernel(local, counts, halves, place_ref, first_ref, *refs):
    token_refs, (wd_ref, *refs) = split(refs, counts)
    factor_refs, (_, hg_ref, hu_ref, gs, weight, sems) = refs[: 2 * halves], refs[2 * halves :]
    factors = [
        (a_ref, b_ref, i)
        for a_ref, b_ref in zip(factor_refs[::2], factor_refs[1::2])
        for i in range(a_ref.shape[0])
    ]
    hidden = wd_ref.shape[1]
    cols = hidden // 2
    ring, rows_each = weight.shape[0], cols // COPIES
    pieces = [(e, i) for e in range(local) for i in range(2)]

    def fetch(piece):
        e, i = pieces[piece]
        at = piece % ring
        return [
            pltpu.make_async_copy(
                wd_ref.at[e, pl.ds(i * cols + c * rows_each, rows_each)],
                weight.at[at, pl.ds(c * rows_each, rows_each)],
                sems.at[at, c],
            )
            for c in range(COPIES)
        ]

    def start(piece):
        if piece < len(pieces):
            for copy in fetch(piece):
                copy.start()

    for piece in range(ring):
        start(piece)
    gather_columns(local, place_ref, token_refs, 1, gs)

    for e, (a_ref, b_ref, at) in enumerate(factors):
        rows = jnp.concatenate([first_ref[e], gs[e]], axis=1)
        for i in range(2):
            part = slice(i * cols, (i + 1) * cols)
            piece = 2 * e + i
            for copy in fetch(piece):
                copy.wait()
            back = dot(weight[piece % ring], rows)
            hg_ref[e, part, :] = (back * a_ref[at, part, :]).astype(jnp.bfloat16)
            hu_ref[e, part, :] = (back * b_ref[at, part, :]).astype(jnp.bfloat16)
            start(piece + ring)


def back(n, place, first, tokens, wd, factors, wg):
    local, hidden, features = wd.shape
    rows = n * SLOT
    shape = jax.ShapeDtypeStruct((local, hidden, rows), jnp.bfloat16)
    return pl.pallas_call(
        functools.partial(back_kernel, local, sizes(tokens), len(factors)),
        in_specs=[INSIDE] * (2 + len(flat(tokens))) + [OUTSIDE] + [INSIDE] * (2 * len(factors) + 1),
        out_shape=[shape, shape],
        scratch_shapes=[
            pltpu.VMEM((local, features, rows - 2 * SLOT), jnp.bfloat16),
            pltpu.VMEM((min(2 * local, RING), hidden // 2, features), jnp.bfloat16),
            pltpu.SemaphoreType.DMA((min(2 * local, RING), COPIES)),
        ],
        compiler_params=params(BACK_MIB),
        cost_estimate=pl.CostEstimate(
            flops=2 * local * rows * features * hidden,
            bytes_accessed=2 * local * features * hidden,
            transcendentals=0,
        ),
    )(place, first, *flat(tokens), hbm(wd), *flat(factors), vmem(wg))


def out_kernel(n, local, orders, chunk, place_ref, hg_ref, hu_ref, wg_ref, wu_ref, *rest):
    outs, (rows_ref, half_ref, weight, sems) = rest[:-4], rest[-4:]
    wide = 2 * SLOT
    cols = wg_ref.shape[1] // CHUNKS
    part = slice(chunk * cols, (chunk + 1) * cols)
    copies = [
        [
            pltpu.make_async_copy(
                wu_ref.at[e, pl.ds(chunk * cols + c * cols // 2, cols // 2)],
                weight.at[e, pl.ds(c * cols // 2, cols // 2)],
                sems.at[e, c],
            )
            for c in range(2)
        ]
        for e in range(local)
    ]
    for copy in flat(copies):
        copy.start()
    for e in range(local):
        half_ref[e] = dot(wg_ref[e, part, :], hg_ref[e])
    for e in range(local):
        for copy in copies[e]:
            copy.wait()
        rows = (half_ref[e] + dot(weight[e], hu_ref[e])).astype(jnp.bfloat16)
        for p in range(n // 2):
            rows_ref[p, :, e * wide : (e + 1) * wide] = rows[:, p * wide : (p + 1) * wide]
    tokens = place_ref.shape[1] // 2
    for p in range(n // 2):
        total = dot(place_ref[p], rows_ref[p], NT)
        for out_ref, order in zip(outs, orders):
            for i, g in enumerate(order):
                if g // 2 == p:
                    mine = total[g % 2 * tokens : (g % 2 + 1) * tokens, :]
                    out_ref[i] = mine.astype(out_ref.dtype)


def partial_sums(n, orders, chunk, place, hg, hu, wg, wu):
    local, features, hidden = wg.shape
    tokens = place.shape[1] // 2
    rows = n * SLOT
    cols = features // CHUNKS
    shapes = [(len(order), tokens, cols) for order in orders]
    types = [jnp.float32] + [jnp.bfloat16] * (len(orders) - 1)
    return pl.pallas_call(
        functools.partial(out_kernel, n, local, orders, chunk),
        in_specs=[INSIDE] * 4 + [OUTSIDE],
        out_shape=[jax.ShapeDtypeStruct(s, t) for s, t in zip(shapes, types)],
        scratch_shapes=[
            pltpu.VMEM((n // 2, cols, 2 * SLOT * local), jnp.bfloat16),
            pltpu.VMEM((local, cols, rows), jnp.float32),
            pltpu.VMEM((local, cols, hidden), jnp.bfloat16),
            pltpu.SemaphoreType.DMA((local, 2)),
        ],
        compiler_params=params(OUT_MIB * max(1, n // 8)),
        cost_estimate=pl.CostEstimate(
            flops=local * rows * cols * hidden,
            bytes_accessed=local * cols * hidden,
            transcendentals=0,
        ),
    )(place, hg, hu, vmem(wg), hbm(wu))


def sum_kernel(*refs):
    parts, out_ref = refs[:-1], refs[-1]
    each = len(parts) // CHUNKS
    cols = out_ref.shape[1] // CHUNKS
    for c in range(CHUNKS):
        own, *others = parts[c * each : (c + 1) * each]
        total = own[0]
        for other in others:
            total += other[0].astype(jnp.float32)
        out_ref[:, c * cols : (c + 1) * cols] = total.astype(jnp.bfloat16)


def body(axis, saved_input, grad_out, routes, route_gates, gate_proj, up_proj, down_proj):
    n = lax.axis_size(axis)
    local = gate_proj.shape[0]
    experts = n * local
    tokens, features = saved_input.shape

    def swap(array, k):
        return lax.ppermute(array, axis, [(i, i ^ k) for i in range(n)])

    table = rank_table(routes.T, route_gates.T, experts)
    tables = [table] + [swap(table, k) for k in range(1, n)]
    pick, place, gates = slots(axis, n, local, tables)
    gate_proj, up_near, done = load((gate_proj, up_proj), table)
    if n == 4:
        x_near = [swap(saved_input, 1), swap(saved_input, 2)]
        upper, lower = relay_parts(x_near, [done, place])
        sent = passed(grad_out, upper)
        x_blocks = [[saved_input], *[[x] for x in x_near], [swap(upper, 2), swap(lower, 1)]]
        g_near = [swap(sent, 1), swap(sent, 2)]
    else:
        x_blocks = [[saved_input]] + [[swap(saved_input, k)] for k in range(1, n)]
        sent = grad_out
    x_first = slot_rows(local, pick, x_blocks[:2], 0, sent)
    x_rest = slot_rows(local, pick, x_blocks[2:], 1, sent)
    half = (local + 1) // 2
    factors = [pre(n, range(half), gates, x_first, x_rest, gate_proj, up_near, table)]
    if n == 4:
        upper, lower = relay_parts(g_near, [factors[0][0]])
        g_blocks = [[sent], *[[g] for g in g_near], [swap(upper, 2), swap(lower, 1)]]
    else:
        g_blocks = [[grad_out]] + [[swap(grad_out, k)] for k in range(1, n)]
        upper = table
    if half < local:
        factors.append(pre(n, range(half, local), gates, x_first, x_rest, gate_proj, up_near, upper))
    g_first = early_columns(local, place, g_blocks[:2], upper)
    hg, hu = back(n, place, g_first, g_blocks[2:], down_proj, factors, gate_proj)
    parts = []
    for chunk in range(CHUNKS):
        if n == 4:
            first, last = (1, 2) if chunk % 2 == 0 else (2, 1)
            orders = ((0,), (first, 3), (last,))
            own, two, one = partial_sums(n, orders, chunk, place, hg, hu, gate_proj, up_proj)
            two = swap(two, first)
            mixed = (two[1:2].astype(jnp.float32) + one.astype(jnp.float32)).astype(jnp.bfloat16)
            parts += [own, two[:1], swap(mixed, last)]
        else:
            orders = tuple((k,) for k in range(n))
            own, *others = partial_sums(n, orders, chunk, place, hg, hu, gate_proj, up_proj)
            parts += [own] + [swap(other, k + 1) for k, other in enumerate(others)]
    return pl.pallas_call(
        sum_kernel,
        out_shape=jax.ShapeDtypeStruct((tokens, features), jnp.bfloat16),
        compiler_params=params(8),
    )(*parts)


def solution(mesh):
    tokens = P(("dp", "expert"), None)
    weights = P("expert", None, None)
    return jax.shard_map(
        functools.partial(body, "expert"),
        mesh=mesh,
        in_specs=(tokens, tokens, tokens, tokens, weights, weights, weights),
        out_specs=tokens,
        check_vma=False,
    )
```

```python
import functools

import jax
import jax.numpy as jnp
from jax import lax
from jax.experimental import pallas as pl
from jax.experimental.pallas import tpu as pltpu
from jax.sharding import PartitionSpec as P

CAP = 56
SLOT = 64
UNUSED = 200.0
MIB = 1 << 20
CHUNKS = 4
PRE_MIB = 6
BACK_MIB = 6
OUT_MIB = 5

NT = (((1,), (1,)), ((), ()))


def dot(a, b, dims=(((1,), (0,)), ((), ()))):
    return lax.dot_general(a, b, dims, preferred_element_type=jnp.float32)


def params(limit):
    return pltpu.CompilerParams(vmem_limit_bytes=limit * MIB)


def rank_kernel(experts, routes_ref, gates_ref, out_ref):
    top, tokens = routes_ref.shape
    chosen = routes_ref[...].astype(jnp.float32)
    gates = gates_ref[...].astype(jnp.float32)
    label = lax.broadcasted_iota(jnp.int32, (experts, tokens), 0).astype(jnp.float32)
    hits = [(chosen[k : k + 1, :] == label).astype(jnp.float32) for k in range(top)]
    before = lax.broadcasted_iota(jnp.int32, (tokens, tokens), 0)
    after = lax.broadcasted_iota(jnp.int32, (tokens, tokens), 1)
    earlier = (before < after).astype(jnp.bfloat16)
    base = jnp.zeros((experts, 1), jnp.float32)
    rank = jnp.zeros((experts, tokens), jnp.float32)
    taken = jnp.zeros((experts, tokens), jnp.float32)
    gate = jnp.zeros((experts, tokens), jnp.float32)
    for k in range(top):
        inside = dot(hits[k].astype(jnp.bfloat16), earlier)
        rank += hits[k] * (inside + base)
        taken += hits[k]
        gate += hits[k] * gates[k : k + 1, :]
        base += jnp.sum(hits[k], axis=1, keepdims=True)
    rank = jnp.where((taken > 0.5) & (rank < CAP), rank, UNUSED)
    out_ref[:experts, :] = rank.astype(jnp.bfloat16)
    out_ref[experts:, :] = gate.astype(jnp.bfloat16)


def rank_table(routes, gates, experts):
    tokens = routes.shape[1]
    return pl.pallas_call(
        functools.partial(rank_kernel, experts),
        out_shape=jax.ShapeDtypeStruct((2 * experts, tokens), jnp.bfloat16),
    )(routes, gates)


def slots_kernel(axis, n, local, *refs):
    table_refs, (pick_ref, place_ref, gate_ref) = refs[:n], refs[n:]
    experts = n * local
    tokens = table_refs[0].shape[1]
    wide = 2 * SLOT
    me = lax.axis_index(axis)
    row = lax.broadcasted_iota(jnp.int32, (2 * experts, tokens), 0)
    slot = lax.broadcasted_iota(jnp.int32, (wide, tokens), 0).astype(jnp.float32)
    for p in range(n // 2):
        tables = [table_refs[2 * p + q][...].astype(jnp.float32) for q in range(2)]
        for j in range(local):
            e = me * local + j
            down = slice(j * wide, (j + 1) * wide)
            gates = jnp.zeros((8, wide), jnp.float32)
            for q in range(2):
                rank = jnp.sum(jnp.where(row == e, tables[q], 0.0), axis=0, keepdims=True)
                gate = jnp.sum(jnp.where(row == e + experts, tables[q], 0.0), axis=0, keepdims=True)
                pick = (slot == rank + q * SLOT).astype(jnp.float32)
                place = pick.T.astype(jnp.bfloat16)
                across = slice(q * tokens, (q + 1) * tokens)
                pick_ref[p, down, across] = pick.astype(jnp.bfloat16)
                place_ref[p, across, down] = place
                gates += dot(jnp.broadcast_to(gate, (8, tokens)).astype(jnp.bfloat16), place)
            gate_ref[j, :, p * wide : (p + 1) * wide] = gates


def slots(axis, n, local, tables):
    tokens = tables[0].shape[1]
    across, down = 2 * tokens, 2 * SLOT * local
    return pl.pallas_call(
        functools.partial(slots_kernel, axis, n, local),
        out_shape=[
            jax.ShapeDtypeStruct((n // 2, down, across), jnp.bfloat16),
            jax.ShapeDtypeStruct((n // 2, across, down), jnp.bfloat16),
            jax.ShapeDtypeStruct((local, 8, n * SLOT), jnp.float32),
        ],
        compiler_params=params(4 * max(1, n // 8)),
    )(*tables)


def gather_rows(local, pick_ref, token_refs, first, out):
    wide = 2 * SLOT
    features = out.shape[2]
    cols = features // 4
    for p in range(len(token_refs) // 2):
        refs = [ref for pair in token_refs[2 * p : 2 * p + 2] for ref in pair]
        for d in range(0, features, cols):
            part = slice(d, d + cols)
            tokens = jnp.concatenate([ref[:, part] for ref in refs], axis=0)
            rows = dot(pick_ref[first + p], tokens).astype(jnp.bfloat16)
            for j in range(local):
                out[j, p * wide : (p + 1) * wide, part] = rows[j * wide : (j + 1) * wide, :]


def gather_columns(local, place_ref, token_refs, first, out):
    wide = 2 * SLOT
    features = out.shape[1]
    size = features // 4
    for p in range(len(token_refs) // 2):
        refs = [ref for pair in token_refs[2 * p : 2 * p + 2] for ref in pair]
        for d in range(0, features, size):
            part = slice(d, d + size)
            tokens = jnp.concatenate([ref[:, part] for ref in refs], axis=0)
            columns = dot(tokens.T, place_ref[first + p]).astype(jnp.bfloat16)
            for j in range(local):
                out[j, part, p * wide : (p + 1) * wide] = columns[:, j * wide : (j + 1) * wide]


def split(refs, counts):
    parts, first = [], 0
    for count in counts:
        parts.append(refs[first : first + count])
        first += count
    return parts, refs[first:]


def flat(groups):
    return [block for blocks in groups for block in blocks]


def sizes(groups):
    return [len(blocks) for blocks in groups]


INSIDE = pl.BlockSpec(memory_space=pltpu.VMEM)
OUTSIDE = pl.BlockSpec(memory_space=pltpu.HBM)
ANYWHERE = pl.BlockSpec(memory_space=pl.ANY)


def vmem(array):
    return pltpu.with_memory_space_constraint(array, pltpu.VMEM)


def hbm(array):
    return pltpu.with_memory_space_constraint(array, pltpu.HBM)


class Ahead:
    def __init__(self, array, first, count, first_row=0, rows=None):
        self.array, self.first, self.count = array, first, count
        self.first_row, self.rows = first_row, rows or array.shape[1]
        self.pieces = 4

    def result(self):
        return pltpu.VMEM((self.count, self.rows, self.array.shape[2]), self.array.dtype)

    def semaphores(self):
        return pltpu.SemaphoreType.DMA((self.count, self.pieces))

    def copies(self, source, result, sems):
        size = self.rows // self.pieces
        return [
            pltpu.make_async_copy(
                source.at[self.first + e, pl.ds(self.first_row + c * size, size)],
                result.at[e, pl.ds(c * size, size)],
                sems.at[e, c],
            )
            for e in range(self.count)
            for c in range(self.pieces)
        ]


def load_kernel(aheads, *refs):
    count = len(aheads)
    sources, results, done_ref, sems = refs[:count], refs[count + 1 : -count - 1], refs[-count - 1], refs[-count:]
    copies = flat(ahead.copies(*each) for ahead, *each in zip(aheads, sources, results, sems))
    for copy in copies:
        copy.start()
    for copy in copies:
        copy.wait()
    done_ref[...] = jnp.zeros_like(done_ref)


def load(aheads, after):
    return pl.pallas_call(
        functools.partial(load_kernel, aheads),
        in_specs=[OUTSIDE] * len(aheads) + [ANYWHERE],
        out_specs=[INSIDE] * (len(aheads) + 1),
        out_shape=[ahead.result() for ahead in aheads] + [jax.ShapeDtypeStruct((8, 128), jnp.float32)],
        scratch_shapes=[ahead.semaphores() for ahead in aheads],
        compiler_params=params(1),
        cost_estimate=pl.CostEstimate(
            flops=0,
            bytes_accessed=4 * sum(ahead.count * ahead.array[0].size for ahead in aheads),
            transcendentals=0,
        ),
    )(*[hbm(ahead.array) for ahead in aheads], after)


def rows_kernel(local, counts, first, pick_ref, *refs):
    token_refs, (_, out_ref) = split(refs, counts)
    gather_rows(local, pick_ref, token_refs, first, out_ref)


def slot_rows(local, pick, tokens, first, after):
    features = tokens[0][0].shape[1]
    return pl.pallas_call(
        functools.partial(rows_kernel, local, sizes(tokens), first),
        in_specs=[INSIDE] * (1 + len(flat(tokens))) + [ANYWHERE],
        out_shape=jax.ShapeDtypeStruct((local, len(tokens) * SLOT, features), jnp.bfloat16),
        compiler_params=params(4),
    )(pick, *flat(tokens), after)


def columns_kernel(local, counts, first, place_ref, *refs):
    token_refs, (_, out_ref) = split(refs, counts)
    gather_columns(local, place_ref, token_refs, first, out_ref)


def slot_columns(local, place, tokens, first, after):
    features = tokens[0][0].shape[1]
    return pl.pallas_call(
        functools.partial(columns_kernel, local, sizes(tokens), first),
        in_specs=[INSIDE] * (1 + len(flat(tokens))) + [ANYWHERE],
        out_shape=jax.ShapeDtypeStruct((local, features, len(tokens) * SLOT), jnp.bfloat16),
        compiler_params=params(4),
    )(place, *flat(tokens), after)


def relay_kernel(x_ref, y_ref, *refs):
    upper_ref, lower_ref = refs[-2:]
    half = upper_ref.shape[0]
    upper_ref[...] = x_ref[:half, :]
    lower_ref[...] = y_ref[half:, :]


def relay_parts(beside, after):
    tokens, features = beside[0].shape
    inside, anywhere = pl.BlockSpec(memory_space=pltpu.VMEM), pl.BlockSpec(memory_space=pl.ANY)
    half = jax.ShapeDtypeStruct((tokens // 2, features), beside[0].dtype)
    return pl.pallas_call(
        relay_kernel,
        in_specs=[inside] * 2 + [anywhere] * len(after),
        out_shape=[half, half],
        compiler_params=params(4),
    )(*beside, *after)


def pass_kernel(array_ref, _, copy_ref):
    copy_ref[...] = array_ref[...]


def passed(array, after):
    return pl.pallas_call(
        pass_kernel,
        in_specs=[pl.BlockSpec(memory_space=pltpu.VMEM), pl.BlockSpec(memory_space=pl.ANY)],
        out_shape=jax.ShapeDtypeStruct(array.shape, array.dtype),
        compiler_params=params(4),
    )(array, after)


def pre_kernel(experts, ahead, gate_ref, first_ref, rest_ref, wg_ref, wu_ref, source, _, a_ref, b_ref, result, sems):
    hidden = wg_ref.shape[2]
    cols = hidden // 2
    copies = ahead.copies(source, result, sems)
    for copy in copies:
        copy.start()
    for i, e in enumerate(experts):
        rows = jnp.concatenate([first_ref[e], rest_ref[e]], axis=0)
        gates = gate_ref[e][:1, :]
        for f in range(0, hidden, cols):
            part = slice(f, f + cols)
            gate_pre = dot(rows, wg_ref[e, :, part])
            up_pre = dot(rows, wu_ref[i, :, part])
            sig = jax.nn.sigmoid(gate_pre)
            a_ref[i, part, :] = (sig * up_pre * (1.0 + gate_pre * (1.0 - sig))).T * gates
            b_ref[i, part, :] = (sig * gate_pre).T * gates
    for copy in copies:
        copy.wait()


def pre(n, experts, ahead, gates, first, rest, wg, wu, after):
    local, features, hidden = wg.shape
    rows, count = n * SLOT, len(experts)
    shape = jax.ShapeDtypeStruct((count, hidden, rows), jnp.float32)
    return pl.pallas_call(
        functools.partial(pre_kernel, experts, ahead),
        in_specs=[INSIDE] * 5 + [OUTSIDE, ANYWHERE],
        out_specs=[INSIDE] * 3,
        out_shape=[shape, shape, ahead.result()],
        scratch_shapes=[ahead.semaphores()],
        compiler_params=params(PRE_MIB * max(1, n // 4)),
        cost_estimate=pl.CostEstimate(
            flops=4 * count * rows * features * hidden,
            bytes_accessed=4 * count * features * hidden,
            transcendentals=count * rows * hidden,
        ),
    )(gates, first, rest, vmem(wg), vmem(wu), hbm(ahead.array), after)


def back_kernel(experts, ahead, first_ref, rest_ref, wd_ref, a_ref, b_ref, _, source, hg_ref, hu_ref, result, sems):
    hidden = wd_ref.shape[1]
    cols = hidden // 2
    copies = ahead.copies(source, result, sems)
    for copy in copies:
        copy.start()
    for i, e in enumerate(experts):
        columns = jnp.concatenate([first_ref[e], rest_ref[e]], axis=1)
        for f in range(0, hidden, cols):
            part = slice(f, f + cols)
            back = dot(wd_ref[i, part, :], columns)
            hg_ref[i, part, :] = (back * a_ref[i, part, :]).astype(jnp.bfloat16)
            hu_ref[i, part, :] = (back * b_ref[i, part, :]).astype(jnp.bfloat16)
    for copy in copies:
        copy.wait()


def back(n, experts, ahead, first, rest, wd, a, b, wg):
    count, hidden, features = wd.shape
    rows = n * SLOT
    shape = jax.ShapeDtypeStruct((count, hidden, rows), jnp.bfloat16)
    return pl.pallas_call(
        functools.partial(back_kernel, experts, ahead),
        in_specs=[INSIDE] * 6 + [OUTSIDE],
        out_specs=[INSIDE] * 3,
        out_shape=[shape, shape, ahead.result()],
        scratch_shapes=[ahead.semaphores()],
        compiler_params=params(BACK_MIB * max(1, n // 4)),
        cost_estimate=pl.CostEstimate(
            flops=2 * count * rows * features * hidden,
            bytes_accessed=2 * count * features * hidden,
            transcendentals=0,
        ),
    )(first, rest, vmem(wd), a, b, vmem(wg), hbm(ahead.array))


def out_kernel(n, local, orders, chunk, ahead, parts, place_ref, *refs):
    h_refs, (wg_ref, wu_ref, *refs) = refs[: 2 * parts], refs[2 * parts :]
    copies = []
    if ahead:
        source, *outs, result, rows_ref, sems = refs
        copies = ahead.copies(source, result, sems)
    else:
        *outs, rows_ref = refs
    for copy in copies:
        copy.start()
    wide = 2 * SLOT
    cols = wu_ref.shape[1]
    part = slice(chunk * cols, (chunk + 1) * cols)
    hidden_refs = [
        (hg_ref.at[i], hu_ref.at[i])
        for hg_ref, hu_ref in zip(h_refs[::2], h_refs[1::2])
        for i in range(hg_ref.shape[0])
    ]
    for e, (hg_ref, hu_ref) in enumerate(hidden_refs):
        rows = dot(wg_ref[e, part, :], hg_ref[...]) + dot(wu_ref[e], hu_ref[...])
        rows = rows.astype(jnp.bfloat16)
        for p in range(n // 2):
            rows_ref[p, :, e * wide : (e + 1) * wide] = rows[:, p * wide : (p + 1) * wide]
    tokens = place_ref.shape[1] // 2
    for p in range(n // 2):
        total = dot(place_ref[p], rows_ref[p], NT)
        for out_ref, order in zip(outs, orders):
            for i, g in enumerate(order):
                if g // 2 == p:
                    mine = total[g % 2 * tokens : (g % 2 + 1) * tokens, :]
                    out_ref[i] = mine.astype(out_ref.dtype)
    for copy in copies:
        copy.wait()


def partial_sums(n, orders, chunk, ahead, place, hidden_grads, wg, wu):
    local, features, hidden = wg.shape
    tokens = place.shape[1] // 2
    rows = n * SLOT
    cols = wu.shape[1]
    shapes = [(len(order), tokens, cols) for order in orders]
    types = [jnp.float32] + [jnp.bfloat16] * (len(orders) - 1)
    more = [ahead] if ahead else []
    return pl.pallas_call(
        functools.partial(out_kernel, n, local, orders, chunk, ahead, len(hidden_grads)),
        in_specs=[INSIDE] * (3 + 2 * len(hidden_grads)) + [OUTSIDE] * len(more),
        out_specs=[INSIDE] * (len(orders) + len(more)),
        out_shape=[jax.ShapeDtypeStruct(s, t) for s, t in zip(shapes, types)] + [m.result() for m in more],
        scratch_shapes=[pltpu.VMEM((n // 2, cols, 2 * SLOT * local), jnp.bfloat16)] + [m.semaphores() for m in more],
        compiler_params=params(OUT_MIB * max(1, n // 4)),
        cost_estimate=pl.CostEstimate(
            flops=local * rows * cols * hidden,
            bytes_accessed=local * cols * hidden,
            transcendentals=0,
        ),
    )(place, *flat(hidden_grads), vmem(wg), vmem(wu), *[hbm(m.array) for m in more])


def sum_kernel(*refs):
    parts, out_ref = refs[:-1], refs[-1]
    each = len(parts) // CHUNKS
    cols = out_ref.shape[1] // CHUNKS
    for c in range(CHUNKS):
        own, *others = parts[c * each : (c + 1) * each]
        total = own[0]
        for other in others:
            total += other[0].astype(jnp.float32)
        out_ref[:, c * cols : (c + 1) * cols] = total.astype(jnp.bfloat16)


def body(axis, saved_input, grad_out, routes, route_gates, gate_proj, up_proj, down_proj):
    n = lax.axis_size(axis)
    local = gate_proj.shape[0]
    experts = n * local
    tokens, features = saved_input.shape

    def swap(array, k):
        return lax.ppermute(array, axis, [(i, i ^ k) for i in range(n)])

    table = rank_table(routes.T, route_gates.T, experts)
    tables = [table] + [swap(table, k) for k in range(1, n)]
    pick, place, gates = slots(axis, n, local, tables)
    half = (local + 1) // 2
    experts_of = [part for part in (range(half), range(half, local)) if len(part)]
    cols = features // CHUNKS
    ups = [Ahead(up_proj, part[0], len(part)) for part in experts_of]
    downs = [Ahead(down_proj, part[0], len(part)) for part in experts_of]
    chunks = [Ahead(up_proj, 0, local, c * cols, cols) for c in range(CHUNKS)]
    gate_proj, near, done = load([Ahead(gate_proj, 0, local), ups[0]], table)
    if n == 4:
        x_near = [swap(saved_input, 1), swap(saved_input, 2)]
        upper, lower = relay_parts(x_near, [done, place])
        sent = passed(grad_out, upper)
        x_blocks = [[saved_input], *[[x] for x in x_near], [swap(upper, 2), swap(lower, 1)]]
        g_near = [swap(sent, 1), swap(sent, 2)]
    else:
        x_blocks = [[saved_input]] + [[swap(saved_input, k)] for k in range(1, n)]
        sent = grad_out
    x_first = slot_rows(local, pick, x_blocks[:2], 0, sent)
    x_rest = slot_rows(local, pick, x_blocks[2:], 1, sent)
    after = table
    factors = []
    for i, part in enumerate(experts_of):
        following = [*ups, downs[0]][i + 1]
        a, b, near = pre(n, part, following, gates, x_first, x_rest, gate_proj, near, after)
        factors.append((a, b))
        if i == 0 and n == 4:
            after, lower = relay_parts(g_near, [a])
            g_blocks = [[sent], *[[g] for g in g_near], [swap(after, 2), swap(lower, 1)]]
        elif i == 0:
            g_blocks = [[grad_out]] + [[swap(grad_out, k)] for k in range(1, n)]
    g_first = slot_columns(local, place, g_blocks[:2], 0, after)
    g_rest = slot_columns(local, place, g_blocks[2:], 1, after)
    hidden_grads = []
    for i, (part, (a, b)) in enumerate(zip(experts_of, factors)):
        following = [*downs, chunks[0]][i + 1]
        hg, hu, near = back(n, part, following, g_first, g_rest, near, a, b, gate_proj)
        hidden_grads.append((hg, hu))
    parts = []
    for chunk in range(CHUNKS):
        following = chunks[chunk + 1] if chunk + 1 < CHUNKS else None
        if n == 4:
            first, last = (1, 2) if chunk % 2 == 0 else (2, 1)
            orders = ((0,), (first, 3), (last,))
        else:
            orders = tuple((k,) for k in range(n))
        own, *others = partial_sums(n, orders, chunk, following, place, hidden_grads, gate_proj, near)
        if following:
            *others, near = others
        if n == 4:
            two, one = others
            two = swap(two, first)
            mixed = (two[1:2].astype(jnp.float32) + one.astype(jnp.float32)).astype(jnp.bfloat16)
            parts += [own, two[:1], swap(mixed, last)]
        else:
            parts += [own] + [swap(other, k + 1) for k, other in enumerate(others)]
    return pl.pallas_call(
        sum_kernel,
        out_shape=jax.ShapeDtypeStruct((tokens, features), jnp.bfloat16),
        compiler_params=params(8),
    )(*parts)


def solution(mesh):
    tokens = P(("dp", "expert"), None)
    weights = P("expert", None, None)
    return jax.shard_map(
        functools.partial(body, "expert"),
        mesh=mesh,
        in_specs=(tokens, tokens, tokens, tokens, weights, weights, weights),
        out_specs=tokens,
        check_vma=False,
    )
```

```python
import functools

import jax
import jax.numpy as jnp
from jax import lax
from jax.experimental import pallas as pl
from jax.experimental.pallas import tpu as pltpu
from jax.sharding import PartitionSpec as P

CAP = 56
SLOT = 64
UNUSED = 200.0
MIB = 1 << 20
CHUNKS = 4
RING = 2
COPIES = 4
PRE_MIB = 5
BACK_MIB = 7
OUT_MIB = 4

NT = (((1,), (1,)), ((), ()))


def dot(a, b, dims=(((1,), (0,)), ((), ()))):
    return lax.dot_general(a, b, dims, preferred_element_type=jnp.float32)


def params(limit):
    return pltpu.CompilerParams(vmem_limit_bytes=limit * MIB)


def rank_kernel(experts, routes_ref, gates_ref, out_ref):
    top, tokens = routes_ref.shape
    chosen = routes_ref[...].astype(jnp.float32)
    gates = gates_ref[...].astype(jnp.float32)
    label = lax.broadcasted_iota(jnp.int32, (experts, tokens), 0).astype(jnp.float32)
    hits = [(chosen[k : k + 1, :] == label).astype(jnp.float32) for k in range(top)]
    before = lax.broadcasted_iota(jnp.int32, (tokens, tokens), 0)
    after = lax.broadcasted_iota(jnp.int32, (tokens, tokens), 1)
    earlier = (before < after).astype(jnp.bfloat16)
    base = jnp.zeros((experts, 1), jnp.float32)
    rank = jnp.zeros((experts, tokens), jnp.float32)
    taken = jnp.zeros((experts, tokens), jnp.float32)
    gate = jnp.zeros((experts, tokens), jnp.float32)
    for k in range(top):
        inside = dot(hits[k].astype(jnp.bfloat16), earlier)
        rank += hits[k] * (inside + base)
        taken += hits[k]
        gate += hits[k] * gates[k : k + 1, :]
        base += jnp.sum(hits[k], axis=1, keepdims=True)
    rank = jnp.where((taken > 0.5) & (rank < CAP), rank, UNUSED)
    out_ref[:experts, :] = rank.astype(jnp.bfloat16)
    out_ref[experts:, :] = gate.astype(jnp.bfloat16)


def rank_table(routes, gates, experts):
    tokens = routes.shape[1]
    return pl.pallas_call(
        functools.partial(rank_kernel, experts),
        out_shape=jax.ShapeDtypeStruct((2 * experts, tokens), jnp.bfloat16),
    )(routes, gates)


def slots_kernel(axis, n, local, *refs):
    table_refs, (pick_ref, place_ref, gate_ref) = refs[:n], refs[n:]
    experts = n * local
    tokens = table_refs[0].shape[1]
    wide = 2 * SLOT
    me = lax.axis_index(axis)
    row = lax.broadcasted_iota(jnp.int32, (2 * experts, tokens), 0)
    slot = lax.broadcasted_iota(jnp.int32, (wide, tokens), 0).astype(jnp.float32)
    for p in range(n // 2):
        tables = [table_refs[2 * p + q][...].astype(jnp.float32) for q in range(2)]
        for j in range(local):
            e = me * local + j
            down = slice(j * wide, (j + 1) * wide)
            gates = jnp.zeros((8, wide), jnp.float32)
            for q in range(2):
                rank = jnp.sum(jnp.where(row == e, tables[q], 0.0), axis=0, keepdims=True)
                gate = jnp.sum(jnp.where(row == e + experts, tables[q], 0.0), axis=0, keepdims=True)
                pick = (slot == rank + q * SLOT).astype(jnp.float32)
                place = pick.T.astype(jnp.bfloat16)
                across = slice(q * tokens, (q + 1) * tokens)
                pick_ref[p, down, across] = pick.astype(jnp.bfloat16)
                place_ref[p, across, down] = place
                gates += dot(jnp.broadcast_to(gate, (8, tokens)).astype(jnp.bfloat16), place)
            gate_ref[j, :, p * wide : (p + 1) * wide] = gates


def slots(axis, n, local, tables):
    tokens = tables[0].shape[1]
    across, down = 2 * tokens, 2 * SLOT * local
    return pl.pallas_call(
        functools.partial(slots_kernel, axis, n, local),
        out_shape=[
            jax.ShapeDtypeStruct((n // 2, down, across), jnp.bfloat16),
            jax.ShapeDtypeStruct((n // 2, across, down), jnp.bfloat16),
            jax.ShapeDtypeStruct((local, 8, n * SLOT), jnp.float32),
        ],
        compiler_params=params(4 * max(1, n // 8)),
    )(*tables)


def gather_rows(local, pick_ref, token_refs, first, out):
    wide = 2 * SLOT
    features = out.shape[2]
    cols = features // 4
    for p in range(len(token_refs) // 2):
        refs = [ref for pair in token_refs[2 * p : 2 * p + 2] for ref in pair]
        for d in range(0, features, cols):
            part = slice(d, d + cols)
            tokens = jnp.concatenate([ref[:, part] for ref in refs], axis=0)
            rows = dot(pick_ref[first + p], tokens).astype(jnp.bfloat16)
            for j in range(local):
                out[j, p * wide : (p + 1) * wide, part] = rows[j * wide : (j + 1) * wide, :]


def gather_columns(local, place_ref, token_refs, first, out):
    wide = 2 * SLOT
    features = out.shape[1]
    size = features // 4
    for p in range(len(token_refs) // 2):
        refs = [ref for pair in token_refs[2 * p : 2 * p + 2] for ref in pair]
        for d in range(0, features, size):
            part = slice(d, d + size)
            tokens = jnp.concatenate([ref[:, part] for ref in refs], axis=0)
            columns = dot(tokens.T, place_ref[first + p]).astype(jnp.bfloat16)
            for j in range(local):
                out[j, part, p * wide : (p + 1) * wide] = columns[:, j * wide : (j + 1) * wide]


def split(refs, counts):
    parts, first = [], 0
    for count in counts:
        parts.append(refs[first : first + count])
        first += count
    return parts, refs[first:]


def flat(groups):
    return [block for blocks in groups for block in blocks]


def sizes(groups):
    return [len(blocks) for blocks in groups]


INSIDE = pl.BlockSpec(memory_space=pltpu.VMEM)
OUTSIDE = pl.BlockSpec(memory_space=pltpu.HBM)
ANYWHERE = pl.BlockSpec(memory_space=pl.ANY)


def vmem(array):
    return pltpu.with_memory_space_constraint(array, pltpu.VMEM)


def hbm(array):
    return pltpu.with_memory_space_constraint(array, pltpu.HBM)


def fetches(source, result, sems):
    return [pltpu.make_async_copy(source.at[e], result.at[e], sems.at[e]) for e in range(source.shape[0])]


def load_kernel(count, *refs):
    sources, (*results, done_ref, sems) = refs[:count], refs[count + 1 :]
    copies = [
        pltpu.make_async_copy(source.at[e], result.at[e], sems.at[i, e])
        for i, (source, result) in enumerate(zip(sources, results))
        for e in range(source.shape[0])
    ]
    for copy in copies:
        copy.start()
    for copy in copies:
        copy.wait()
    done_ref[...] = jnp.zeros_like(done_ref)


def load(arrays, after):
    count = len(arrays)
    return pl.pallas_call(
        functools.partial(load_kernel, count),
        in_specs=[OUTSIDE] * count + [pl.BlockSpec(memory_space=pl.ANY)],
        out_specs=[pl.BlockSpec(memory_space=pltpu.VMEM)] * (count + 1),
        out_shape=[pltpu.VMEM(w.shape, w.dtype) for w in arrays]
        + [jax.ShapeDtypeStruct((8, 128), jnp.float32)],
        scratch_shapes=[pltpu.SemaphoreType.DMA((count, arrays[0].shape[0]))],
        compiler_params=params(1),
        cost_estimate=pl.CostEstimate(
            flops=0, bytes_accessed=4 * count * arrays[0].size, transcendentals=0
        ),
    )(*[pltpu.with_memory_space_constraint(w, pltpu.HBM) for w in arrays], after)


def rows_kernel(local, counts, first, pick_ref, *refs):
    token_refs, (_, out_ref) = split(refs, counts)
    gather_rows(local, pick_ref, token_refs, first, out_ref)


def slot_rows(local, pick, tokens, first, after):
    features = tokens[0][0].shape[1]
    return pl.pallas_call(
        functools.partial(rows_kernel, local, sizes(tokens), first),
        in_specs=[INSIDE] * (1 + len(flat(tokens))) + [ANYWHERE],
        out_shape=jax.ShapeDtypeStruct((local, len(tokens) * SLOT, features), jnp.bfloat16),
        compiler_params=params(4),
    )(pick, *flat(tokens), after)


def columns_kernel(local, counts, place_ref, *refs):
    token_refs, (_, out_ref) = split(refs, counts)
    gather_columns(local, place_ref, token_refs, 0, out_ref)


def early_columns(local, place, tokens, after):
    features = tokens[0][0].shape[1]
    return pl.pallas_call(
        functools.partial(columns_kernel, local, sizes(tokens)),
        in_specs=[INSIDE] * (1 + len(flat(tokens))) + [ANYWHERE],
        out_shape=jax.ShapeDtypeStruct((local, features, 2 * SLOT), jnp.bfloat16),
        compiler_params=params(4),
    )(place, *flat(tokens), after)


def relay_kernel(x_ref, y_ref, *refs):
    upper_ref, lower_ref = refs[-2:]
    half = upper_ref.shape[0]
    upper_ref[...] = x_ref[:half, :]
    lower_ref[...] = y_ref[half:, :]


def relay_parts(beside, after):
    tokens, features = beside[0].shape
    inside, anywhere = pl.BlockSpec(memory_space=pltpu.VMEM), pl.BlockSpec(memory_space=pl.ANY)
    half = jax.ShapeDtypeStruct((tokens // 2, features), beside[0].dtype)
    return pl.pallas_call(
        relay_kernel,
        in_specs=[inside] * 2 + [anywhere] * len(after),
        out_shape=[half, half],
        compiler_params=params(4),
    )(*beside, *after)


def pass_kernel(array_ref, _, copy_ref):
    copy_ref[...] = array_ref[...]


def passed(array, after):
    return pl.pallas_call(
        pass_kernel,
        in_specs=[pl.BlockSpec(memory_space=pltpu.VMEM), pl.BlockSpec(memory_space=pl.ANY)],
        out_shape=jax.ShapeDtypeStruct(array.shape, array.dtype),
        compiler_params=params(4),
    )(array, after)


def pre_kernel(experts, gate_ref, first_ref, rest_ref, wg_ref, wu_ref, _, a_ref, b_ref):
    hidden = wg_ref.shape[2]
    cols = hidden // 2
    for i, e in enumerate(experts):
        rows = jnp.concatenate([first_ref[e], rest_ref[e]], axis=0)
        gates = gate_ref[e][:1, :]
        for f in range(0, hidden, cols):
            part = slice(f, f + cols)
            gate_pre = dot(rows, wg_ref[e, :, part])
            up_pre = dot(rows, wu_ref[e, :, part])
            sig = jax.nn.sigmoid(gate_pre)
            a_ref[i, part, :] = (sig * up_pre * (1.0 + gate_pre * (1.0 - sig))).T * gates
            b_ref[i, part, :] = (sig * gate_pre).T * gates


def pre(n, experts, gates, first, rest, wg, wu, after):
    local, features, hidden = wg.shape
    rows, count = n * SLOT, len(experts)
    shape = jax.ShapeDtypeStruct((count, hidden, rows), jnp.float32)
    return pl.pallas_call(
        functools.partial(pre_kernel, experts),
        in_specs=[INSIDE] * 5 + [ANYWHERE],
        out_shape=[shape, shape],
        compiler_params=params(PRE_MIB * max(1, n // 4)),
        cost_estimate=pl.CostEstimate(
            flops=4 * count * rows * features * hidden,
            bytes_accessed=4 * count * features * hidden,
            transcendentals=count * rows * hidden,
        ),
    )(gates, first, rest, vmem(wg), vmem(wu), after)


def back_kernel(local, counts, halves, place_ref, first_ref, *refs):
    token_refs, (wd_ref, *refs) = split(refs, counts)
    factor_refs, (_, _, hg_ref, hu_ref, gs, weight, sems) = refs[: 2 * halves], refs[2 * halves :]
    factors = [
        (a_ref, b_ref, i)
        for a_ref, b_ref in zip(factor_refs[::2], factor_refs[1::2])
        for i in range(a_ref.shape[0])
    ]
    hidden = wd_ref.shape[1]
    cols = hidden // 2
    ring, rows_each = weight.shape[0], cols // COPIES
    pieces = [(e, i) for e in range(local) for i in range(2)]

    def fetch(piece):
        e, i = pieces[piece]
        at = piece % ring
        return [
            pltpu.make_async_copy(
                wd_ref.at[e, pl.ds(i * cols + c * rows_each, rows_each)],
                weight.at[at, pl.ds(c * rows_each, rows_each)],
                sems.at[at, c],
            )
            for c in range(COPIES)
        ]

    def start(piece):
        if piece < len(pieces):
            for copy in fetch(piece):
                copy.start()

    for piece in range(ring):
        start(piece)
    gather_columns(local, place_ref, token_refs, 1, gs)

    for e, (a_ref, b_ref, at) in enumerate(factors):
        rows = jnp.concatenate([first_ref[e], gs[e]], axis=1)
        for i in range(2):
            part = slice(i * cols, (i + 1) * cols)
            piece = 2 * e + i
            for copy in fetch(piece):
                copy.wait()
            back = dot(weight[piece % ring], rows)
            hg_ref[e, part, :] = (back * a_ref[at, part, :]).astype(jnp.bfloat16)
            hu_ref[e, part, :] = (back * b_ref[at, part, :]).astype(jnp.bfloat16)
            start(piece + ring)


def back(n, place, first, tokens, wd, factors, wg, wu):
    local, hidden, features = wd.shape
    rows = n * SLOT
    shape = jax.ShapeDtypeStruct((local, hidden, rows), jnp.bfloat16)
    return pl.pallas_call(
        functools.partial(back_kernel, local, sizes(tokens), len(factors)),
        in_specs=[INSIDE] * (2 + len(flat(tokens))) + [OUTSIDE] + [INSIDE] * (2 * len(factors) + 2),
        out_shape=[shape, shape],
        scratch_shapes=[
            pltpu.VMEM((local, features, rows - 2 * SLOT), jnp.bfloat16),
            pltpu.VMEM((min(2 * local, RING), hidden // 2, features), jnp.bfloat16),
            pltpu.SemaphoreType.DMA((min(2 * local, RING), COPIES)),
        ],
        compiler_params=params(BACK_MIB * max(1, n // 4)),
        cost_estimate=pl.CostEstimate(
            flops=2 * local * rows * features * hidden,
            bytes_accessed=2 * local * features * hidden,
            transcendentals=0,
        ),
    )(place, first, *flat(tokens), hbm(wd), *flat(factors), vmem(wg), vmem(wu))


def out_kernel(n, local, orders, chunk, place_ref, hg_ref, hu_ref, wg_ref, wu_ref, *rest):
    outs, rows_ref = rest[:-1], rest[-1]
    wide = 2 * SLOT
    cols = wg_ref.shape[1] // CHUNKS
    part = slice(chunk * cols, (chunk + 1) * cols)
    for e in range(local):
        rows = dot(wg_ref[e, part, :], hg_ref[e]) + dot(wu_ref[e, part, :], hu_ref[e])
        rows = rows.astype(jnp.bfloat16)
        for p in range(n // 2):
            rows_ref[p, :, e * wide : (e + 1) * wide] = rows[:, p * wide : (p + 1) * wide]
    tokens = place_ref.shape[1] // 2
    for p in range(n // 2):
        total = dot(place_ref[p], rows_ref[p], NT)
        for out_ref, order in zip(outs, orders):
            for i, g in enumerate(order):
                if g // 2 == p:
                    mine = total[g % 2 * tokens : (g % 2 + 1) * tokens, :]
                    out_ref[i] = mine.astype(out_ref.dtype)


def partial_sums(n, orders, chunk, place, hg, hu, wg, wu):
    local, features, hidden = wg.shape
    tokens = place.shape[1] // 2
    rows = n * SLOT
    cols = features // CHUNKS
    shapes = [(len(order), tokens, cols) for order in orders]
    types = [jnp.float32] + [jnp.bfloat16] * (len(orders) - 1)
    return pl.pallas_call(
        functools.partial(out_kernel, n, local, orders, chunk),
        out_shape=[jax.ShapeDtypeStruct(s, t) for s, t in zip(shapes, types)],
        scratch_shapes=[pltpu.VMEM((n // 2, cols, 2 * SLOT * local), jnp.bfloat16)],
        compiler_params=params(OUT_MIB * max(1, n // 4)),
        cost_estimate=pl.CostEstimate(
            flops=local * rows * cols * hidden,
            bytes_accessed=local * cols * hidden,
            transcendentals=0,
        ),
    )(place, hg, hu, vmem(wg), vmem(wu))


def sum_kernel(*refs):
    parts, out_ref = refs[:-1], refs[-1]
    each = len(parts) // CHUNKS
    cols = out_ref.shape[1] // CHUNKS
    for c in range(CHUNKS):
        own, *others = parts[c * each : (c + 1) * each]
        total = own[0]
        for other in others:
            total += other[0].astype(jnp.float32)
        out_ref[:, c * cols : (c + 1) * cols] = total.astype(jnp.bfloat16)


def body(axis, saved_input, grad_out, routes, route_gates, gate_proj, up_proj, down_proj):
    n = lax.axis_size(axis)
    local = gate_proj.shape[0]
    experts = n * local
    tokens, features = saved_input.shape

    def swap(array, k):
        return lax.ppermute(array, axis, [(i, i ^ k) for i in range(n)])

    table = rank_table(routes.T, route_gates.T, experts)
    tables = [table] + [swap(table, k) for k in range(1, n)]
    pick, place, gates = slots(axis, n, local, tables)
    gate_proj, up_proj, done = load((gate_proj, up_proj), table)
    if n == 4:
        x_near = [swap(saved_input, 1), swap(saved_input, 2)]
        upper, lower = relay_parts(x_near, [done, place])
        sent = passed(grad_out, upper)
        x_blocks = [[saved_input], *[[x] for x in x_near], [swap(upper, 2), swap(lower, 1)]]
        g_near = [swap(sent, 1), swap(sent, 2)]
    else:
        x_blocks = [[saved_input]] + [[swap(saved_input, k)] for k in range(1, n)]
        sent = grad_out
    x_first = slot_rows(local, pick, x_blocks[:2], 0, sent)
    x_rest = slot_rows(local, pick, x_blocks[2:], 1, sent)
    half = (local + 1) // 2
    factors = [pre(n, range(half), gates, x_first, x_rest, gate_proj, up_proj, table)]
    if n == 4:
        upper, lower = relay_parts(g_near, [factors[0][0]])
        g_blocks = [[sent], *[[g] for g in g_near], [swap(upper, 2), swap(lower, 1)]]
    else:
        g_blocks = [[grad_out]] + [[swap(grad_out, k)] for k in range(1, n)]
        upper = table
    if half < local:
        factors.append(pre(n, range(half, local), gates, x_first, x_rest, gate_proj, up_proj, upper))
    g_first = early_columns(local, place, g_blocks[:2], upper)
    hg, hu = back(n, place, g_first, g_blocks[2:], down_proj, factors, gate_proj, up_proj)
    parts = []
    for chunk in range(CHUNKS):
        if n == 4:
            first, last = (1, 2) if chunk % 2 == 0 else (2, 1)
            orders = ((0,), (first, 3), (last,))
            own, two, one = partial_sums(n, orders, chunk, place, hg, hu, gate_proj, up_proj)
            two = swap(two, first)
            mixed = (two[1:2].astype(jnp.float32) + one.astype(jnp.float32)).astype(jnp.bfloat16)
            parts += [own, two[:1], swap(mixed, last)]
        else:
            orders = tuple((k,) for k in range(n))
            own, *others = partial_sums(n, orders, chunk, place, hg, hu, gate_proj, up_proj)
            parts += [own] + [swap(other, k + 1) for k, other in enumerate(others)]
    return pl.pallas_call(
        sum_kernel,
        out_shape=jax.ShapeDtypeStruct((tokens, features), jnp.bfloat16),
        compiler_params=params(8),
    )(*parts)


def solution(mesh):
    tokens = P(("dp", "expert"), None)
    weights = P("expert", None, None)
    return jax.shard_map(
        functools.partial(body, "expert"),
        mesh=mesh,
        in_specs=(tokens, tokens, tokens, tokens, weights, weights, weights),
        out_specs=tokens,
        check_vma=False,
    )
```

```python
import functools

import jax
import jax.numpy as jnp
from jax import lax
from jax.experimental import pallas as pl
from jax.experimental.pallas import tpu as pltpu
from jax.sharding import PartitionSpec as P

CAP = 56
SLOT = 64
UNUSED = 200.0
MIB = 1 << 20
CHUNKS = 4
DIRECT = (0, 1)
RING = 2
COPIES = 4
PRE_MIB = 5
BACK_MIB = 7
OUT_MIB = 4

NT = (((1,), (1,)), ((), ()))


def dot(a, b, dims=(((1,), (0,)), ((), ()))):
    return lax.dot_general(a, b, dims, preferred_element_type=jnp.float32)


def params(limit):
    return pltpu.CompilerParams(vmem_limit_bytes=limit * MIB)


def rank_kernel(experts, routes_ref, gates_ref, out_ref):
    top, tokens = routes_ref.shape
    chosen = routes_ref[...].astype(jnp.float32)
    gates = gates_ref[...].astype(jnp.float32)
    label = lax.broadcasted_iota(jnp.int32, (experts, tokens), 0).astype(jnp.float32)
    hits = [(chosen[k : k + 1, :] == label).astype(jnp.float32) for k in range(top)]
    before = lax.broadcasted_iota(jnp.int32, (tokens, tokens), 0)
    after = lax.broadcasted_iota(jnp.int32, (tokens, tokens), 1)
    earlier = (before < after).astype(jnp.bfloat16)
    base = jnp.zeros((experts, 1), jnp.float32)
    rank = jnp.zeros((experts, tokens), jnp.float32)
    taken = jnp.zeros((experts, tokens), jnp.float32)
    gate = jnp.zeros((experts, tokens), jnp.float32)
    for k in range(top):
        inside = dot(hits[k].astype(jnp.bfloat16), earlier)
        rank += hits[k] * (inside + base)
        taken += hits[k]
        gate += hits[k] * gates[k : k + 1, :]
        base += jnp.sum(hits[k], axis=1, keepdims=True)
    rank = jnp.where((taken > 0.5) & (rank < CAP), rank, UNUSED)
    out_ref[:experts, :] = rank.astype(jnp.bfloat16)
    out_ref[experts:, :] = gate.astype(jnp.bfloat16)


def rank_table(routes, gates, experts):
    tokens = routes.shape[1]
    return pl.pallas_call(
        functools.partial(rank_kernel, experts),
        out_shape=jax.ShapeDtypeStruct((2 * experts, tokens), jnp.bfloat16),
    )(routes, gates)


def slots_kernel(axis, n, local, *refs):
    table_refs, (pick_ref, place_ref, gate_ref) = refs[:n], refs[n:]
    experts = n * local
    tokens = table_refs[0].shape[1]
    wide = 2 * SLOT
    me = lax.axis_index(axis)
    row = lax.broadcasted_iota(jnp.int32, (2 * experts, tokens), 0)
    slot = lax.broadcasted_iota(jnp.int32, (wide, tokens), 0).astype(jnp.float32)
    for p in range(n // 2):
        tables = [table_refs[2 * p + q][...].astype(jnp.float32) for q in range(2)]
        for j in range(local):
            e = me * local + j
            down = slice(j * wide, (j + 1) * wide)
            gates = jnp.zeros((8, wide), jnp.float32)
            for q in range(2):
                rank = jnp.sum(jnp.where(row == e, tables[q], 0.0), axis=0, keepdims=True)
                gate = jnp.sum(jnp.where(row == e + experts, tables[q], 0.0), axis=0, keepdims=True)
                pick = (slot == rank + q * SLOT).astype(jnp.float32)
                place = pick.T.astype(jnp.bfloat16)
                across = slice(q * tokens, (q + 1) * tokens)
                pick_ref[p, down, across] = pick.astype(jnp.bfloat16)
                place_ref[p, across, down] = place
                gates += dot(jnp.broadcast_to(gate, (8, tokens)).astype(jnp.bfloat16), place)
            gate_ref[j, :, p * wide : (p + 1) * wide] = gates


def slots(axis, n, local, tables):
    tokens = tables[0].shape[1]
    across, down = 2 * tokens, 2 * SLOT * local
    return pl.pallas_call(
        functools.partial(slots_kernel, axis, n, local),
        out_shape=[
            jax.ShapeDtypeStruct((n // 2, down, across), jnp.bfloat16),
            jax.ShapeDtypeStruct((n // 2, across, down), jnp.bfloat16),
            jax.ShapeDtypeStruct((local, 8, n * SLOT), jnp.float32),
        ],
        compiler_params=params(4 * max(1, n // 8)),
    )(*tables)


def gather_rows(local, pick_ref, token_refs, first, out):
    wide = 2 * SLOT
    features = out.shape[2]
    cols = features // 4
    for p in range(len(token_refs) // 2):
        refs = [ref for pair in token_refs[2 * p : 2 * p + 2] for ref in pair]
        for d in range(0, features, cols):
            part = slice(d, d + cols)
            tokens = jnp.concatenate([ref[:, part] for ref in refs], axis=0)
            rows = dot(pick_ref[first + p], tokens).astype(jnp.bfloat16)
            for j in range(local):
                out[j, p * wide : (p + 1) * wide, part] = rows[j * wide : (j + 1) * wide, :]


def gather_columns(local, place_ref, token_refs, first, out):
    wide = 2 * SLOT
    features = out.shape[1]
    size = features // 4
    for p in range(len(token_refs) // 2):
        refs = [ref for pair in token_refs[2 * p : 2 * p + 2] for ref in pair]
        for d in range(0, features, size):
            part = slice(d, d + size)
            tokens = jnp.concatenate([ref[:, part] for ref in refs], axis=0)
            columns = dot(tokens.T, place_ref[first + p]).astype(jnp.bfloat16)
            for j in range(local):
                out[j, part, p * wide : (p + 1) * wide] = columns[:, j * wide : (j + 1) * wide]


def split(refs, counts):
    parts, first = [], 0
    for count in counts:
        parts.append(refs[first : first + count])
        first += count
    return parts, refs[first:]


def flat(groups):
    return [block for blocks in groups for block in blocks]


def sizes(groups):
    return [len(blocks) for blocks in groups]


INSIDE = pl.BlockSpec(memory_space=pltpu.VMEM)
OUTSIDE = pl.BlockSpec(memory_space=pltpu.HBM)
ANYWHERE = pl.BlockSpec(memory_space=pl.ANY)


def vmem(array):
    return pltpu.with_memory_space_constraint(array, pltpu.VMEM)


def hbm(array):
    return pltpu.with_memory_space_constraint(array, pltpu.HBM)


def fetches(source, result, sems):
    return [pltpu.make_async_copy(source.at[e], result.at[e], sems.at[e]) for e in range(source.shape[0])]


def load_kernel(count, *refs):
    sources, (*results, done_ref, sems) = refs[:count], refs[count + 1 :]
    copies = [
        pltpu.make_async_copy(source.at[e], result.at[e], sems.at[i, e])
        for i, (source, result) in enumerate(zip(sources, results))
        for e in range(source.shape[0])
    ]
    for copy in copies:
        copy.start()
    for copy in copies:
        copy.wait()
    done_ref[...] = jnp.zeros_like(done_ref)


def load(arrays, after):
    count = len(arrays)
    return pl.pallas_call(
        functools.partial(load_kernel, count),
        in_specs=[OUTSIDE] * count + [pl.BlockSpec(memory_space=pl.ANY)],
        out_specs=[pl.BlockSpec(memory_space=pltpu.VMEM)] * (count + 1),
        out_shape=[pltpu.VMEM(w.shape, w.dtype) for w in arrays]
        + [jax.ShapeDtypeStruct((8, 128), jnp.float32)],
        scratch_shapes=[pltpu.SemaphoreType.DMA((count, arrays[0].shape[0]))],
        compiler_params=params(1),
        cost_estimate=pl.CostEstimate(
            flops=0, bytes_accessed=4 * count * arrays[0].size, transcendentals=0
        ),
    )(*[pltpu.with_memory_space_constraint(w, pltpu.HBM) for w in arrays], after)


def rows_kernel(local, counts, first, pick_ref, *refs):
    token_refs, (_, out_ref) = split(refs, counts)
    gather_rows(local, pick_ref, token_refs, first, out_ref)


def slot_rows(local, pick, tokens, first, after):
    features = tokens[0][0].shape[1]
    return pl.pallas_call(
        functools.partial(rows_kernel, local, sizes(tokens), first),
        in_specs=[INSIDE] * (1 + len(flat(tokens))) + [ANYWHERE],
        out_shape=jax.ShapeDtypeStruct((local, len(tokens) * SLOT, features), jnp.bfloat16),
        compiler_params=params(4),
    )(pick, *flat(tokens), after)


def columns_kernel(local, counts, place_ref, *refs):
    token_refs, (_, out_ref) = split(refs, counts)
    gather_columns(local, place_ref, token_refs, 0, out_ref)


def early_columns(local, place, tokens, after):
    features = tokens[0][0].shape[1]
    return pl.pallas_call(
        functools.partial(columns_kernel, local, sizes(tokens)),
        in_specs=[INSIDE] * (1 + len(flat(tokens))) + [ANYWHERE],
        out_shape=jax.ShapeDtypeStruct((local, features, 2 * SLOT), jnp.bfloat16),
        compiler_params=params(4),
    )(place, *flat(tokens), after)


def relay_kernel(x_ref, y_ref, *refs):
    upper_ref, lower_ref = refs[-2:]
    half = upper_ref.shape[0]
    upper_ref[...] = x_ref[:half, :]
    lower_ref[...] = y_ref[half:, :]


def relay_parts(beside, after):
    tokens, features = beside[0].shape
    inside, anywhere = pl.BlockSpec(memory_space=pltpu.VMEM), pl.BlockSpec(memory_space=pl.ANY)
    half = jax.ShapeDtypeStruct((tokens // 2, features), beside[0].dtype)
    return pl.pallas_call(
        relay_kernel,
        in_specs=[inside] * 2 + [anywhere] * len(after),
        out_shape=[half, half],
        compiler_params=params(4),
    )(*beside, *after)


def pass_kernel(array_ref, _, copy_ref):
    copy_ref[...] = array_ref[...]


def passed(array, after):
    return pl.pallas_call(
        pass_kernel,
        in_specs=[pl.BlockSpec(memory_space=pltpu.VMEM), pl.BlockSpec(memory_space=pl.ANY)],
        out_shape=jax.ShapeDtypeStruct(array.shape, array.dtype),
        compiler_params=params(4),
    )(array, after)


def pre_kernel(experts, gate_ref, first_ref, rest_ref, wg_ref, wu_ref, _, a_ref, b_ref):
    hidden = wg_ref.shape[2]
    cols = hidden // 2
    for i, e in enumerate(experts):
        rows = jnp.concatenate([first_ref[e], rest_ref[e]], axis=0)
        gates = gate_ref[e][:1, :]
        for f in range(0, hidden, cols):
            part = slice(f, f + cols)
            gate_pre = dot(rows, wg_ref[e, :, part])
            up_pre = dot(rows, wu_ref[e, :, part])
            sig = jax.nn.sigmoid(gate_pre)
            a_ref[i, part, :] = (sig * up_pre * (1.0 + gate_pre * (1.0 - sig))).T * gates
            b_ref[i, part, :] = (sig * gate_pre).T * gates


def pre(n, experts, gates, first, rest, wg, wu, after):
    local, features, hidden = wg.shape
    rows, count = n * SLOT, len(experts)
    shape = jax.ShapeDtypeStruct((count, hidden, rows), jnp.float32)
    return pl.pallas_call(
        functools.partial(pre_kernel, experts),
        in_specs=[INSIDE] * 5 + [ANYWHERE],
        out_shape=[shape, shape],
        compiler_params=params(PRE_MIB * max(1, n // 4)),
        cost_estimate=pl.CostEstimate(
            flops=4 * count * rows * features * hidden,
            bytes_accessed=4 * count * features * hidden,
            transcendentals=count * rows * hidden,
        ),
    )(gates, first, rest, vmem(wg), vmem(wu), after)


def back_kernel(local, counts, halves, place_ref, first_ref, *refs):
    token_refs, (wd_ref, *refs) = split(refs, counts)
    factor_refs, (_, _, hg_ref, hu_ref, gs, weight, sems) = refs[: 2 * halves], refs[2 * halves :]
    factors = [
        (a_ref, b_ref, i)
        for a_ref, b_ref in zip(factor_refs[::2], factor_refs[1::2])
        for i in range(a_ref.shape[0])
    ]
    hidden = wd_ref.shape[1]
    cols = hidden // 2
    ring, rows_each = weight.shape[0], cols // COPIES
    pieces = [(e, i) for e in range(local) for i in range(2)]

    def fetch(piece):
        e, i = pieces[piece]
        at = piece % ring
        return [
            pltpu.make_async_copy(
                wd_ref.at[e, pl.ds(i * cols + c * rows_each, rows_each)],
                weight.at[at, pl.ds(c * rows_each, rows_each)],
                sems.at[at, c],
            )
            for c in range(COPIES)
        ]

    def start(piece):
        if piece < len(pieces):
            for copy in fetch(piece):
                copy.start()

    for piece in range(ring):
        start(piece)
    gather_columns(local, place_ref, token_refs, 1, gs)

    for e, (a_ref, b_ref, at) in enumerate(factors):
        rows = jnp.concatenate([first_ref[e], gs[e]], axis=1)
        for i in range(2):
            part = slice(i * cols, (i + 1) * cols)
            piece = 2 * e + i
            for copy in fetch(piece):
                copy.wait()
            back = dot(weight[piece % ring], rows)
            hg_ref[e, part, :] = (back * a_ref[at, part, :]).astype(jnp.bfloat16)
            hu_ref[e, part, :] = (back * b_ref[at, part, :]).astype(jnp.bfloat16)
            start(piece + ring)


def back(n, place, first, tokens, wd, factors, wg, wu):
    local, hidden, features = wd.shape
    rows = n * SLOT
    shape = jax.ShapeDtypeStruct((local, hidden, rows), jnp.bfloat16)
    return pl.pallas_call(
        functools.partial(back_kernel, local, sizes(tokens), len(factors)),
        in_specs=[INSIDE] * (2 + len(flat(tokens))) + [OUTSIDE] + [INSIDE] * (2 * len(factors) + 2),
        out_shape=[shape, shape],
        scratch_shapes=[
            pltpu.VMEM((local, features, rows - 2 * SLOT), jnp.bfloat16),
            pltpu.VMEM((min(2 * local, RING), hidden // 2, features), jnp.bfloat16),
            pltpu.SemaphoreType.DMA((min(2 * local, RING), COPIES)),
        ],
        compiler_params=params(BACK_MIB * max(1, n // 4)),
        cost_estimate=pl.CostEstimate(
            flops=2 * local * rows * features * hidden,
            bytes_accessed=2 * local * features * hidden,
            transcendentals=0,
        ),
    )(place, first, *flat(tokens), hbm(wd), *flat(factors), vmem(wg), vmem(wu))


def out_kernel(n, local, orders, chunk, place_ref, hg_ref, hu_ref, wg_ref, wu_ref, *rest):
    outs, rows_ref = rest[:-1], rest[-1]
    wide = 2 * SLOT
    cols = wg_ref.shape[1] // CHUNKS
    part = slice(chunk * cols, (chunk + 1) * cols)
    for e in range(local):
        rows = dot(wg_ref[e, part, :], hg_ref[e]) + dot(wu_ref[e, part, :], hu_ref[e])
        rows = rows.astype(jnp.bfloat16)
        for p in range(n // 2):
            rows_ref[p, :, e * wide : (e + 1) * wide] = rows[:, p * wide : (p + 1) * wide]
    tokens = place_ref.shape[1] // 2
    for p in range(n // 2):
        total = dot(place_ref[p], rows_ref[p], NT)
        for out_ref, order in zip(outs, orders):
            for i, g in enumerate(order):
                if g // 2 == p:
                    mine = total[g % 2 * tokens : (g % 2 + 1) * tokens, :]
                    out_ref[i] = mine.astype(out_ref.dtype)


def partial_sums(n, orders, chunk, place, hg, hu, wg, wu):
    local, features, hidden = wg.shape
    tokens = place.shape[1] // 2
    rows = n * SLOT
    cols = features // CHUNKS
    shapes = [(len(order), tokens, cols) for order in orders]
    types = [jnp.float32] + [jnp.bfloat16] * (len(orders) - 1)
    return pl.pallas_call(
        functools.partial(out_kernel, n, local, orders, chunk),
        out_shape=[jax.ShapeDtypeStruct(s, t) for s, t in zip(shapes, types)],
        scratch_shapes=[pltpu.VMEM((n // 2, cols, 2 * SLOT * local), jnp.bfloat16)],
        compiler_params=params(OUT_MIB * max(1, n // 4)),
        cost_estimate=pl.CostEstimate(
            flops=local * rows * cols * hidden,
            bytes_accessed=local * cols * hidden,
            transcendentals=0,
        ),
    )(place, hg, hu, vmem(wg), vmem(wu))


def sum_kernel(counts, *refs):
    parts, _ = split(refs, counts)
    out_ref = refs[-1]
    cols = out_ref.shape[1] // CHUNKS
    for c, (own, *others) in enumerate(parts):
        total = own[0]
        for other in others:
            total += other[0].astype(jnp.float32)
        out_ref[:, c * cols : (c + 1) * cols] = total.astype(jnp.bfloat16)


def body(axis, saved_input, grad_out, routes, route_gates, gate_proj, up_proj, down_proj):
    n = lax.axis_size(axis)
    local = gate_proj.shape[0]
    experts = n * local
    tokens, features = saved_input.shape

    def swap(array, k):
        return lax.ppermute(array, axis, [(i, i ^ k) for i in range(n)])

    table = rank_table(routes.T, route_gates.T, experts)
    tables = [table] + [swap(table, k) for k in range(1, n)]
    pick, place, gates = slots(axis, n, local, tables)
    gate_proj, up_proj, done = load((gate_proj, up_proj), table)
    if n == 4:
        x_near = [swap(saved_input, 1), swap(saved_input, 2)]
        upper, lower = relay_parts(x_near, [done, place])
        sent = passed(grad_out, upper)
        x_blocks = [[saved_input], *[[x] for x in x_near], [swap(upper, 2), swap(lower, 1)]]
        g_near = [swap(sent, 1), swap(sent, 2)]
    else:
        x_blocks = [[saved_input]] + [[swap(saved_input, k)] for k in range(1, n)]
        sent = grad_out
    x_first = slot_rows(local, pick, x_blocks[:2], 0, sent)
    x_rest = slot_rows(local, pick, x_blocks[2:], 1, sent)
    half = (local + 1) // 2
    factors = [pre(n, range(half), gates, x_first, x_rest, gate_proj, up_proj, table)]
    if n == 4:
        upper, lower = relay_parts(g_near, [factors[0][0]])
        g_blocks = [[sent], *[[g] for g in g_near], [swap(upper, 2), swap(lower, 1)]]
    else:
        g_blocks = [[grad_out]] + [[swap(grad_out, k)] for k in range(1, n)]
        upper = table
    if half < local:
        factors.append(pre(n, range(half, local), gates, x_first, x_rest, gate_proj, up_proj, upper))
    g_first = early_columns(local, place, g_blocks[:2], upper)
    hg, hu = back(n, place, g_first, g_blocks[2:], down_proj, factors, gate_proj, up_proj)
    parts = []
    for chunk in range(CHUNKS):
        if n == 4 and chunk not in DIRECT:
            first, last = (1, 2) if chunk % 2 == 0 else (2, 1)
            orders = ((0,), (first, 3), (last,))
            own, two, one = partial_sums(n, orders, chunk, place, hg, hu, gate_proj, up_proj)
            two = swap(two, first)
            mixed = (two[1:2].astype(jnp.float32) + one.astype(jnp.float32)).astype(jnp.bfloat16)
            parts.append([own, two[:1], swap(mixed, last)])
        else:
            orders = tuple((k,) for k in range(n))
            own, *others = partial_sums(n, orders, chunk, place, hg, hu, gate_proj, up_proj)
            parts.append([own] + [swap(other, k + 1) for k, other in enumerate(others)])
    return pl.pallas_call(
        functools.partial(sum_kernel, sizes(parts)),
        out_shape=jax.ShapeDtypeStruct((tokens, features), jnp.bfloat16),
        compiler_params=params(8),
    )(*flat(parts))


def solution(mesh):
    tokens = P(("dp", "expert"), None)
    weights = P("expert", None, None)
    return jax.shard_map(
        functools.partial(body, "expert"),
        mesh=mesh,
        in_specs=(tokens, tokens, tokens, tokens, weights, weights, weights),
        out_specs=tokens,
        check_vma=False,
    )
```

```python
import functools

import jax
import jax.numpy as jnp
from jax import lax
from jax.experimental import pallas as pl
from jax.experimental.pallas import tpu as pltpu
from jax.sharding import PartitionSpec as P

CAP = 56
SLOT = 64
UNUSED = 200.0
MIB = 1 << 20
CHUNKS = 4
RING = 2
COPIES = 4
PRE_MIB = 5
BACK_MIB = 7
OUT_MIB = 4

NT = (((1,), (1,)), ((), ()))


def dot(a, b, dims=(((1,), (0,)), ((), ()))):
    return lax.dot_general(a, b, dims, preferred_element_type=jnp.float32)


def params(limit):
    return pltpu.CompilerParams(vmem_limit_bytes=limit * MIB)


def rank_kernel(experts, routes_ref, gates_ref, out_ref):
    top, tokens = routes_ref.shape
    chosen = routes_ref[...].astype(jnp.float32)
    gates = gates_ref[...].astype(jnp.float32)
    label = lax.broadcasted_iota(jnp.int32, (experts, tokens), 0).astype(jnp.float32)
    hits = [(chosen[k : k + 1, :] == label).astype(jnp.float32) for k in range(top)]
    before = lax.broadcasted_iota(jnp.int32, (tokens, tokens), 0)
    after = lax.broadcasted_iota(jnp.int32, (tokens, tokens), 1)
    earlier = (before < after).astype(jnp.bfloat16)
    base = jnp.zeros((experts, 1), jnp.float32)
    rank = jnp.zeros((experts, tokens), jnp.float32)
    taken = jnp.zeros((experts, tokens), jnp.float32)
    gate = jnp.zeros((experts, tokens), jnp.float32)
    for k in range(top):
        inside = dot(hits[k].astype(jnp.bfloat16), earlier)
        rank += hits[k] * (inside + base)
        taken += hits[k]
        gate += hits[k] * gates[k : k + 1, :]
        base += jnp.sum(hits[k], axis=1, keepdims=True)
    rank = jnp.where((taken > 0.5) & (rank < CAP), rank, UNUSED)
    out_ref[:experts, :] = rank.astype(jnp.bfloat16)
    out_ref[experts:, :] = gate.astype(jnp.bfloat16)


def rank_table(routes, gates, experts):
    tokens = routes.shape[1]
    return pl.pallas_call(
        functools.partial(rank_kernel, experts),
        out_shape=jax.ShapeDtypeStruct((2 * experts, tokens), jnp.bfloat16),
    )(routes, gates)


def slots_kernel(axis, n, local, *refs):
    table_refs, (pick_ref, place_ref, gate_ref) = refs[:n], refs[n:]
    experts = n * local
    tokens = table_refs[0].shape[1]
    wide = 2 * SLOT
    me = lax.axis_index(axis)
    row = lax.broadcasted_iota(jnp.int32, (2 * experts, tokens), 0)
    slot = lax.broadcasted_iota(jnp.int32, (wide, tokens), 0).astype(jnp.float32)
    for p in range(n // 2):
        tables = [table_refs[2 * p + q][...].astype(jnp.float32) for q in range(2)]
        for j in range(local):
            e = me * local + j
            down = slice(j * wide, (j + 1) * wide)
            gates = jnp.zeros((8, wide), jnp.float32)
            for q in range(2):
                rank = jnp.sum(jnp.where(row == e, tables[q], 0.0), axis=0, keepdims=True)
                gate = jnp.sum(jnp.where(row == e + experts, tables[q], 0.0), axis=0, keepdims=True)
                pick = (slot == rank + q * SLOT).astype(jnp.float32)
                place = pick.T.astype(jnp.bfloat16)
                across = slice(q * tokens, (q + 1) * tokens)
                pick_ref[p, down, across] = pick.astype(jnp.bfloat16)
                place_ref[p, across, down] = place
                gates += dot(jnp.broadcast_to(gate, (8, tokens)).astype(jnp.bfloat16), place)
            gate_ref[j, :, p * wide : (p + 1) * wide] = gates


def slots(axis, n, local, tables):
    tokens = tables[0].shape[1]
    across, down = 2 * tokens, 2 * SLOT * local
    return pl.pallas_call(
        functools.partial(slots_kernel, axis, n, local),
        out_shape=[
            jax.ShapeDtypeStruct((n // 2, down, across), jnp.bfloat16),
            jax.ShapeDtypeStruct((n // 2, across, down), jnp.bfloat16),
            jax.ShapeDtypeStruct((local, 8, n * SLOT), jnp.float32),
        ],
        compiler_params=params(4 * max(1, n // 8)),
    )(*tables)


def gather_rows(local, pick_ref, token_refs, first, out):
    wide = 2 * SLOT
    features = out.shape[2]
    cols = features // 4
    for p in range(len(token_refs) // 2):
        refs = [ref for pair in token_refs[2 * p : 2 * p + 2] for ref in pair]
        for d in range(0, features, cols):
            part = slice(d, d + cols)
            tokens = jnp.concatenate([ref[:, part] for ref in refs], axis=0)
            rows = dot(pick_ref[first + p], tokens).astype(jnp.bfloat16)
            for j in range(local):
                out[j, p * wide : (p + 1) * wide, part] = rows[j * wide : (j + 1) * wide, :]


def gather_columns(local, place_ref, token_refs, first, out):
    wide = 2 * SLOT
    features = out.shape[1]
    size = features // 4
    for p in range(len(token_refs) // 2):
        refs = [ref for pair in token_refs[2 * p : 2 * p + 2] for ref in pair]
        for d in range(0, features, size):
            part = slice(d, d + size)
            tokens = jnp.concatenate([ref[:, part] for ref in refs], axis=0)
            columns = dot(tokens.T, place_ref[first + p]).astype(jnp.bfloat16)
            for j in range(local):
                out[j, part, p * wide : (p + 1) * wide] = columns[:, j * wide : (j + 1) * wide]


def split(refs, counts):
    parts, first = [], 0
    for count in counts:
        parts.append(refs[first : first + count])
        first += count
    return parts, refs[first:]


def flat(groups):
    return [block for blocks in groups for block in blocks]


def sizes(groups):
    return [len(blocks) for blocks in groups]


INSIDE = pl.BlockSpec(memory_space=pltpu.VMEM)
OUTSIDE = pl.BlockSpec(memory_space=pltpu.HBM)
ANYWHERE = pl.BlockSpec(memory_space=pl.ANY)


def vmem(array):
    return pltpu.with_memory_space_constraint(array, pltpu.VMEM)


def hbm(array):
    return pltpu.with_memory_space_constraint(array, pltpu.HBM)


def fetches(source, result, sems):
    return [pltpu.make_async_copy(source.at[e], result.at[e], sems.at[e]) for e in range(source.shape[0])]


def load_kernel(count, *refs):
    sources, (*results, done_ref, sems) = refs[:count], refs[count + 1 :]
    copies = [
        pltpu.make_async_copy(source.at[e], result.at[e], sems.at[i, e])
        for i, (source, result) in enumerate(zip(sources, results))
        for e in range(source.shape[0])
    ]
    for copy in copies:
        copy.start()
    for copy in copies:
        copy.wait()
    done_ref[...] = jnp.zeros_like(done_ref)


def load(arrays, after):
    count = len(arrays)
    return pl.pallas_call(
        functools.partial(load_kernel, count),
        in_specs=[OUTSIDE] * count + [pl.BlockSpec(memory_space=pl.ANY)],
        out_specs=[pl.BlockSpec(memory_space=pltpu.VMEM)] * (count + 1),
        out_shape=[pltpu.VMEM(w.shape, w.dtype) for w in arrays]
        + [jax.ShapeDtypeStruct((8, 128), jnp.float32)],
        scratch_shapes=[pltpu.SemaphoreType.DMA((count, arrays[0].shape[0]))],
        compiler_params=params(1),
        cost_estimate=pl.CostEstimate(
            flops=0, bytes_accessed=4 * count * arrays[0].size, transcendentals=0
        ),
    )(*[pltpu.with_memory_space_constraint(w, pltpu.HBM) for w in arrays], after)


def rows_kernel(local, counts, first, pick_ref, *refs):
    token_refs, (_, out_ref) = split(refs, counts)
    gather_rows(local, pick_ref, token_refs, first, out_ref)


def slot_rows(local, pick, tokens, first, after):
    features = tokens[0][0].shape[1]
    return pl.pallas_call(
        functools.partial(rows_kernel, local, sizes(tokens), first),
        in_specs=[INSIDE] * (1 + len(flat(tokens))) + [ANYWHERE],
        out_shape=jax.ShapeDtypeStruct((local, len(tokens) * SLOT, features), jnp.bfloat16),
        compiler_params=params(4),
    )(pick, *flat(tokens), after)


def columns_kernel(local, counts, place_ref, *refs):
    token_refs, (_, out_ref) = split(refs, counts)
    gather_columns(local, place_ref, token_refs, 0, out_ref)


def early_columns(local, place, tokens, after):
    features = tokens[0][0].shape[1]
    return pl.pallas_call(
        functools.partial(columns_kernel, local, sizes(tokens)),
        in_specs=[INSIDE] * (1 + len(flat(tokens))) + [ANYWHERE],
        out_shape=jax.ShapeDtypeStruct((local, features, 2 * SLOT), jnp.bfloat16),
        compiler_params=params(4),
    )(place, *flat(tokens), after)


def relay_kernel(x_ref, y_ref, *refs):
    upper_ref, lower_ref = refs[-2:]
    half = upper_ref.shape[0]
    upper_ref[...] = x_ref[:half, :]
    lower_ref[...] = y_ref[half:, :]


def relay_parts(beside, after):
    tokens, features = beside[0].shape
    inside, anywhere = pl.BlockSpec(memory_space=pltpu.VMEM), pl.BlockSpec(memory_space=pl.ANY)
    half = jax.ShapeDtypeStruct((tokens // 2, features), beside[0].dtype)
    return pl.pallas_call(
        relay_kernel,
        in_specs=[inside] * 2 + [anywhere] * len(after),
        out_shape=[half, half],
        compiler_params=params(4),
    )(*beside, *after)


def pass_kernel(array_ref, _, copy_ref):
    copy_ref[...] = array_ref[...]


def passed(array, after):
    return pl.pallas_call(
        pass_kernel,
        in_specs=[pl.BlockSpec(memory_space=pltpu.VMEM), pl.BlockSpec(memory_space=pl.ANY)],
        out_shape=jax.ShapeDtypeStruct(array.shape, array.dtype),
        compiler_params=params(4),
    )(array, after)


def pre_kernel(experts, gate_ref, first_ref, rest_ref, wg_ref, wu_ref, _, a_ref, b_ref):
    hidden = wg_ref.shape[2]
    cols = hidden // 2
    for i, e in enumerate(experts):
        rows = jnp.concatenate([first_ref[e], rest_ref[e]], axis=0)
        gates = gate_ref[e][:1, :]
        for f in range(0, hidden, cols):
            part = slice(f, f + cols)
            gate_pre = dot(rows, wg_ref[e, :, part])
            up_pre = dot(rows, wu_ref[e, :, part])
            sig = jax.nn.sigmoid(gate_pre)
            a_ref[i, part, :] = (sig * up_pre * (1.0 + gate_pre * (1.0 - sig))).T * gates
            b_ref[i, part, :] = (sig * gate_pre).T * gates


def pre(n, experts, gates, first, rest, wg, wu, after):
    local, features, hidden = wg.shape
    rows, count = n * SLOT, len(experts)
    shape = jax.ShapeDtypeStruct((count, hidden, rows), jnp.float32)
    return pl.pallas_call(
        functools.partial(pre_kernel, experts),
        in_specs=[INSIDE] * 5 + [ANYWHERE],
        out_shape=[shape, shape],
        compiler_params=params(PRE_MIB * max(1, n // 4)),
        cost_estimate=pl.CostEstimate(
            flops=4 * count * rows * features * hidden,
            bytes_accessed=4 * count * features * hidden,
            transcendentals=count * rows * hidden,
        ),
    )(gates, first, rest, vmem(wg), vmem(wu), after)


def back_kernel(local, counts, halves, place_ref, first_ref, *refs):
    token_refs, (wd_ref, *refs) = split(refs, counts)
    factor_refs, (_, _, hg_ref, hu_ref, gs, weight, sems) = refs[: 2 * halves], refs[2 * halves :]
    factors = [
        (a_ref, b_ref, i)
        for a_ref, b_ref in zip(factor_refs[::2], factor_refs[1::2])
        for i in range(a_ref.shape[0])
    ]
    hidden = wd_ref.shape[1]
    cols = hidden // 2
    ring, rows_each = weight.shape[0], cols // COPIES
    pieces = [(e, i) for e in range(local) for i in range(2)]

    def fetch(piece):
        e, i = pieces[piece]
        at = piece % ring
        return [
            pltpu.make_async_copy(
                wd_ref.at[e, pl.ds(i * cols + c * rows_each, rows_each)],
                weight.at[at, pl.ds(c * rows_each, rows_each)],
                sems.at[at, c],
            )
            for c in range(COPIES)
        ]

    def start(piece):
        if piece < len(pieces):
            for copy in fetch(piece):
                copy.start()

    for piece in range(ring):
        start(piece)
    gather_columns(local, place_ref, token_refs, 1, gs)

    for e, (a_ref, b_ref, at) in enumerate(factors):
        rows = jnp.concatenate([first_ref[e], gs[e]], axis=1)
        for i in range(2):
            part = slice(i * cols, (i + 1) * cols)
            piece = 2 * e + i
            for copy in fetch(piece):
                copy.wait()
            back = dot(weight[piece % ring], rows)
            hg_ref[e, part, :] = (back * a_ref[at, part, :]).astype(jnp.bfloat16)
            hu_ref[e, part, :] = (back * b_ref[at, part, :]).astype(jnp.bfloat16)
            start(piece + ring)


def back(n, place, first, tokens, wd, factors, wg, wu):
    local, hidden, features = wd.shape
    rows = n * SLOT
    shape = jax.ShapeDtypeStruct((local, hidden, rows), jnp.bfloat16)
    return pl.pallas_call(
        functools.partial(back_kernel, local, sizes(tokens), len(factors)),
        in_specs=[INSIDE] * (2 + len(flat(tokens))) + [OUTSIDE] + [INSIDE] * (2 * len(factors) + 2),
        out_shape=[shape, shape],
        scratch_shapes=[
            pltpu.VMEM((local, features, rows - 2 * SLOT), jnp.bfloat16),
            pltpu.VMEM((min(2 * local, RING), hidden // 2, features), jnp.bfloat16),
            pltpu.SemaphoreType.DMA((min(2 * local, RING), COPIES)),
        ],
        compiler_params=params(BACK_MIB * max(1, n // 4)),
        cost_estimate=pl.CostEstimate(
            flops=2 * local * rows * features * hidden,
            bytes_accessed=2 * local * features * hidden,
            transcendentals=0,
        ),
    )(place, first, *flat(tokens), hbm(wd), *flat(factors), vmem(wg), vmem(wu))


def out_kernel(n, local, orders, chunk, place_ref, hg_ref, hu_ref, wg_ref, wu_ref, *rest):
    outs, rows_ref = rest[:-1], rest[-1]
    wide = 2 * SLOT
    cols = wg_ref.shape[1] // CHUNKS
    part = slice(chunk * cols, (chunk + 1) * cols)
    for e in range(local):
        rows = dot(wg_ref[e, part, :], hg_ref[e]) + dot(wu_ref[e, part, :], hu_ref[e])
        rows = rows.astype(jnp.bfloat16)
        for p in range(n // 2):
            rows_ref[p, :, e * wide : (e + 1) * wide] = rows[:, p * wide : (p + 1) * wide]
    tokens = place_ref.shape[1] // 2
    for p in range(n // 2):
        total = dot(place_ref[p], rows_ref[p], NT)
        for out_ref, order in zip(outs, orders):
            for i, g in enumerate(order):
                if g // 2 == p:
                    mine = total[g % 2 * tokens : (g % 2 + 1) * tokens, :]
                    out_ref[i] = mine.astype(out_ref.dtype)


def partial_sums(n, orders, chunk, place, hg, hu, wg, wu):
    local, features, hidden = wg.shape
    tokens = place.shape[1] // 2
    rows = n * SLOT
    cols = features // CHUNKS
    shapes = [(len(order), tokens, cols) for order in orders]
    types = [jnp.float32] + [jnp.bfloat16] * (len(orders) - 1)
    return pl.pallas_call(
        functools.partial(out_kernel, n, local, orders, chunk),
        out_shape=[jax.ShapeDtypeStruct(s, t) for s, t in zip(shapes, types)],
        scratch_shapes=[pltpu.VMEM((n // 2, cols, 2 * SLOT * local), jnp.bfloat16)],
        compiler_params=params(OUT_MIB * max(1, n // 4)),
        cost_estimate=pl.CostEstimate(
            flops=local * rows * cols * hidden,
            bytes_accessed=local * cols * hidden,
            transcendentals=0,
        ),
    )(place, hg, hu, vmem(wg), vmem(wu))


def sum_kernel(*refs):
    parts, out_ref = refs[:-1], refs[-1]
    each = len(parts) // CHUNKS
    cols = out_ref.shape[1] // CHUNKS
    for c in range(CHUNKS):
        own, *others = parts[c * each : (c + 1) * each]
        total = own[0]
        for other in others:
            total += other[0].astype(jnp.float32)
        out_ref[:, c * cols : (c + 1) * cols] = total.astype(jnp.bfloat16)


def body(axis, saved_input, grad_out, routes, route_gates, gate_proj, up_proj, down_proj):
    n = lax.axis_size(axis)
    local = gate_proj.shape[0]
    experts = n * local
    tokens, features = saved_input.shape

    def swap(array, k):
        return lax.ppermute(array, axis, [(i, i ^ k) for i in range(n)])

    table = rank_table(routes.T, route_gates.T, experts)
    tables = [table] + [swap(table, k) for k in range(1, n)]
    pick, place, gates = slots(axis, n, local, tables)
    if n == 4:
        x_near = [swap(saved_input, 1), swap(saved_input, 2)]
        upper, lower = relay_parts(x_near, [place])
        sent = passed(grad_out, upper)
        x_blocks = [[saved_input], *[[x] for x in x_near], [swap(upper, 2), swap(lower, 1)]]
        g_near = [swap(sent, 1), swap(sent, 2)]
    else:
        x_blocks = [[saved_input]] + [[swap(saved_input, k)] for k in range(1, n)]
        sent = grad_out
    gate_proj, up_proj, _ = load((gate_proj, up_proj), sent)
    x_first = slot_rows(local, pick, x_blocks[:2], 0, sent)
    x_rest = slot_rows(local, pick, x_blocks[2:], 1, sent)
    half = (local + 1) // 2
    factors = [pre(n, range(half), gates, x_first, x_rest, gate_proj, up_proj, table)]
    if n == 4:
        upper, lower = relay_parts(g_near, [factors[0][0]])
        g_blocks = [[sent], *[[g] for g in g_near], [swap(upper, 2), swap(lower, 1)]]
    else:
        g_blocks = [[grad_out]] + [[swap(grad_out, k)] for k in range(1, n)]
        upper = table
    if half < local:
        factors.append(pre(n, range(half, local), gates, x_first, x_rest, gate_proj, up_proj, upper))
    g_first = early_columns(local, place, g_blocks[:2], upper)
    hg, hu = back(n, place, g_first, g_blocks[2:], down_proj, factors, gate_proj, up_proj)
    parts = []
    for chunk in range(CHUNKS):
        if n == 4:
            first, last = (1, 2) if chunk % 2 == 0 else (2, 1)
            orders = ((0,), (first, 3), (last,))
            own, two, one = partial_sums(n, orders, chunk, place, hg, hu, gate_proj, up_proj)
            two = swap(two, first)
            mixed = (two[1:2].astype(jnp.float32) + one.astype(jnp.float32)).astype(jnp.bfloat16)
            parts += [own, two[:1], swap(mixed, last)]
        else:
            orders = tuple((k,) for k in range(n))
            own, *others = partial_sums(n, orders, chunk, place, hg, hu, gate_proj, up_proj)
            parts += [own] + [swap(other, k + 1) for k, other in enumerate(others)]
    return pl.pallas_call(
        sum_kernel,
        out_shape=jax.ShapeDtypeStruct((tokens, features), jnp.bfloat16),
        compiler_params=params(8),
    )(*parts)


def solution(mesh):
    tokens = P(("dp", "expert"), None)
    weights = P("expert", None, None)
    return jax.shard_map(
        functools.partial(body, "expert"),
        mesh=mesh,
        in_specs=(tokens, tokens, tokens, tokens, weights, weights, weights),
        out_specs=tokens,
        check_vma=False,
    )
```

```python
import functools

import jax
import jax.numpy as jnp
from jax import lax
from jax.experimental import pallas as pl
from jax.experimental.pallas import tpu as pltpu
from jax.sharding import PartitionSpec as P

CAP = 56
SLOT = 64
UNUSED = 200.0
MIB = 1 << 20
CHUNKS = 4
PRE_MIB = 6
BACK_MIB = 10
OUT_MIB = 4

NT = (((1,), (1,)), ((), ()))


def dot(a, b, dims=(((1,), (0,)), ((), ()))):
    return lax.dot_general(a, b, dims, preferred_element_type=jnp.float32)


def params(limit):
    return pltpu.CompilerParams(vmem_limit_bytes=limit * MIB)


def rank_kernel(experts, routes_ref, gates_ref, out_ref):
    top, tokens = routes_ref.shape
    chosen = routes_ref[...].astype(jnp.float32)
    gates = gates_ref[...].astype(jnp.float32)
    label = lax.broadcasted_iota(jnp.int32, (experts, tokens), 0).astype(jnp.float32)
    hits = [(chosen[k : k + 1, :] == label).astype(jnp.float32) for k in range(top)]
    before = lax.broadcasted_iota(jnp.int32, (tokens, tokens), 0)
    after = lax.broadcasted_iota(jnp.int32, (tokens, tokens), 1)
    earlier = (before < after).astype(jnp.bfloat16)
    base = jnp.zeros((experts, 1), jnp.float32)
    rank = jnp.zeros((experts, tokens), jnp.float32)
    taken = jnp.zeros((experts, tokens), jnp.float32)
    gate = jnp.zeros((experts, tokens), jnp.float32)
    for k in range(top):
        inside = dot(hits[k].astype(jnp.bfloat16), earlier)
        rank += hits[k] * (inside + base)
        taken += hits[k]
        gate += hits[k] * gates[k : k + 1, :]
        base += jnp.sum(hits[k], axis=1, keepdims=True)
    rank = jnp.where((taken > 0.5) & (rank < CAP), rank, UNUSED)
    out_ref[:experts, :] = rank.astype(jnp.bfloat16)
    out_ref[experts:, :] = gate.astype(jnp.bfloat16)


def rank_table(routes, gates, experts):
    tokens = routes.shape[1]
    return pl.pallas_call(
        functools.partial(rank_kernel, experts),
        out_shape=jax.ShapeDtypeStruct((2 * experts, tokens), jnp.bfloat16),
    )(routes, gates)


def slots_kernel(axis, n, local, *refs):
    table_refs, (pick_ref, place_ref, gate_ref) = refs[:n], refs[n:]
    experts = n * local
    tokens = table_refs[0].shape[1]
    wide = 2 * SLOT
    me = lax.axis_index(axis)
    row = lax.broadcasted_iota(jnp.int32, (2 * experts, tokens), 0)
    slot = lax.broadcasted_iota(jnp.int32, (wide, tokens), 0).astype(jnp.float32)
    for p in range(n // 2):
        tables = [table_refs[2 * p + q][...].astype(jnp.float32) for q in range(2)]
        for j in range(local):
            e = me * local + j
            down = slice(j * wide, (j + 1) * wide)
            gates = jnp.zeros((8, wide), jnp.float32)
            for q in range(2):
                rank = jnp.sum(jnp.where(row == e, tables[q], 0.0), axis=0, keepdims=True)
                gate = jnp.sum(jnp.where(row == e + experts, tables[q], 0.0), axis=0, keepdims=True)
                pick = (slot == rank + q * SLOT).astype(jnp.float32)
                place = pick.T.astype(jnp.bfloat16)
                across = slice(q * tokens, (q + 1) * tokens)
                pick_ref[p, down, across] = pick.astype(jnp.bfloat16)
                place_ref[p, across, down] = place
                gates += dot(jnp.broadcast_to(gate, (8, tokens)).astype(jnp.bfloat16), place)
            gate_ref[j, :, p * wide : (p + 1) * wide] = gates


def slots(axis, n, local, tables):
    tokens = tables[0].shape[1]
    across, down = 2 * tokens, 2 * SLOT * local
    return pl.pallas_call(
        functools.partial(slots_kernel, axis, n, local),
        out_shape=[
            jax.ShapeDtypeStruct((n // 2, down, across), jnp.bfloat16),
            jax.ShapeDtypeStruct((n // 2, across, down), jnp.bfloat16),
            jax.ShapeDtypeStruct((local, 8, n * SLOT), jnp.float32),
        ],
        compiler_params=params(4 * max(1, n // 8)),
    )(*tables)


def gather_rows(local, pick_ref, token_refs, first, out):
    wide = 2 * SLOT
    features = out.shape[2]
    cols = features // 4
    for p in range(len(token_refs) // 2):
        refs = [ref for pair in token_refs[2 * p : 2 * p + 2] for ref in pair]
        for d in range(0, features, cols):
            part = slice(d, d + cols)
            tokens = jnp.concatenate([ref[:, part] for ref in refs], axis=0)
            rows = dot(pick_ref[first + p], tokens).astype(jnp.bfloat16)
            for j in range(local):
                out[j, p * wide : (p + 1) * wide, part] = rows[j * wide : (j + 1) * wide, :]


def gather_columns(local, place_ref, token_refs, first, out):
    wide = 2 * SLOT
    features = out.shape[1]
    size = features // 4
    for p in range(len(token_refs) // 2):
        refs = [ref for pair in token_refs[2 * p : 2 * p + 2] for ref in pair]
        for d in range(0, features, size):
            part = slice(d, d + size)
            tokens = jnp.concatenate([ref[:, part] for ref in refs], axis=0)
            columns = dot(tokens.T, place_ref[first + p]).astype(jnp.bfloat16)
            for j in range(local):
                out[j, part, p * wide : (p + 1) * wide] = columns[:, j * wide : (j + 1) * wide]


def split(refs, counts):
    parts, first = [], 0
    for count in counts:
        parts.append(refs[first : first + count])
        first += count
    return parts, refs[first:]


def flat(groups):
    return [block for blocks in groups for block in blocks]


def sizes(groups):
    return [len(blocks) for blocks in groups]


INSIDE = pl.BlockSpec(memory_space=pltpu.VMEM)
OUTSIDE = pl.BlockSpec(memory_space=pltpu.HBM)
ANYWHERE = pl.BlockSpec(memory_space=pl.ANY)


def vmem(array):
    return pltpu.with_memory_space_constraint(array, pltpu.VMEM)


def hbm(array):
    return pltpu.with_memory_space_constraint(array, pltpu.HBM)


def fetches(source, result, sems):
    return [pltpu.make_async_copy(source.at[e], result.at[e], sems.at[e]) for e in range(source.shape[0])]


def load_kernel(count, *refs):
    sources, (*results, done_ref, sems) = refs[:count], refs[count + 1 :]
    copies = [
        pltpu.make_async_copy(source.at[e], result.at[e], sems.at[i, e])
        for i, (source, result) in enumerate(zip(sources, results))
        for e in range(source.shape[0])
    ]
    for copy in copies:
        copy.start()
    for copy in copies:
        copy.wait()
    done_ref[...] = jnp.zeros_like(done_ref)


def load(arrays, after):
    count = len(arrays)
    return pl.pallas_call(
        functools.partial(load_kernel, count),
        in_specs=[OUTSIDE] * count + [pl.BlockSpec(memory_space=pl.ANY)],
        out_specs=[pl.BlockSpec(memory_space=pltpu.VMEM)] * (count + 1),
        out_shape=[pltpu.VMEM(w.shape, w.dtype) for w in arrays]
        + [jax.ShapeDtypeStruct((8, 128), jnp.float32)],
        scratch_shapes=[pltpu.SemaphoreType.DMA((count, arrays[0].shape[0]))],
        compiler_params=params(1),
        cost_estimate=pl.CostEstimate(
            flops=0, bytes_accessed=4 * count * arrays[0].size, transcendentals=0
        ),
    )(*[pltpu.with_memory_space_constraint(w, pltpu.HBM) for w in arrays], after)


def rows_kernel(local, counts, pick_ref, *refs):
    token_refs, (_, out_ref) = split(refs, counts)
    gather_rows(local, pick_ref, token_refs, 0, out_ref)


def early_rows(local, pick, tokens, after):
    features = tokens[0][0].shape[1]
    return pl.pallas_call(
        functools.partial(rows_kernel, local, sizes(tokens)),
        in_specs=[INSIDE] * (1 + len(flat(tokens))) + [ANYWHERE],
        out_shape=jax.ShapeDtypeStruct((local, 2 * SLOT, features), jnp.bfloat16),
        compiler_params=params(4),
    )(pick, *flat(tokens), after)


def columns_kernel(local, counts, place_ref, *refs):
    token_refs, (_, out_ref) = split(refs, counts)
    gather_columns(local, place_ref, token_refs, 0, out_ref)


def early_columns(local, place, tokens, after):
    features = tokens[0][0].shape[1]
    return pl.pallas_call(
        functools.partial(columns_kernel, local, sizes(tokens)),
        in_specs=[INSIDE] * (1 + len(flat(tokens))) + [ANYWHERE],
        out_shape=jax.ShapeDtypeStruct((local, features, 2 * SLOT), jnp.bfloat16),
        compiler_params=params(4),
    )(place, *flat(tokens), after)


def relay_kernel(x_ref, y_ref, *refs):
    upper_ref, lower_ref = refs[-2:]
    half = upper_ref.shape[0]
    upper_ref[...] = x_ref[:half, :]
    lower_ref[...] = y_ref[half:, :]


def relay_parts(beside, after):
    tokens, features = beside[0].shape
    inside, anywhere = pl.BlockSpec(memory_space=pltpu.VMEM), pl.BlockSpec(memory_space=pl.ANY)
    half = jax.ShapeDtypeStruct((tokens // 2, features), beside[0].dtype)
    return pl.pallas_call(
        relay_kernel,
        in_specs=[inside] * 2 + [anywhere] * len(after),
        out_shape=[half, half],
        compiler_params=params(4),
    )(*beside, *after)


def pass_kernel(array_ref, _, copy_ref):
    copy_ref[...] = array_ref[...]


def passed(array, after):
    return pl.pallas_call(
        pass_kernel,
        in_specs=[pl.BlockSpec(memory_space=pltpu.VMEM), pl.BlockSpec(memory_space=pl.ANY)],
        out_shape=jax.ShapeDtypeStruct(array.shape, array.dtype),
        compiler_params=params(4),
    )(array, after)


def pre_kernel(local, counts, pick_ref, gate_ref, first_ref, *refs):
    token_refs, refs = split(refs, counts)
    wg_ref, wu_ref, a_ref, b_ref, xs = refs
    hidden = wg_ref.shape[2]
    cols = hidden // 2
    gather_rows(local, pick_ref, token_refs, 1, xs)

    for e in range(local):
        rows = jnp.concatenate([first_ref[e], xs[e]], axis=0)
        gates = gate_ref[e][:1, :]
        for f in range(0, hidden, cols):
            part = slice(f, f + cols)
            gate_pre = dot(rows, wg_ref[e, :, part])
            up_pre = dot(rows, wu_ref[e, :, part])
            sig = jax.nn.sigmoid(gate_pre)
            a_ref[e, part, :] = (sig * up_pre * (1.0 + gate_pre * (1.0 - sig))).T * gates
            b_ref[e, part, :] = (sig * gate_pre).T * gates


def pre(n, pick, gates, first, tokens, wg, wu):
    local, features, hidden = wg.shape
    rows = n * SLOT
    return pl.pallas_call(
        functools.partial(pre_kernel, local, sizes(tokens)),
        in_specs=[INSIDE] * (5 + len(flat(tokens))),
        out_shape=[
            jax.ShapeDtypeStruct((local, hidden, rows), jnp.float32),
            jax.ShapeDtypeStruct((local, hidden, rows), jnp.float32),
        ],
        scratch_shapes=[pltpu.VMEM((local, rows - 2 * SLOT, features), jnp.bfloat16)],
        compiler_params=params(PRE_MIB * max(1, n // 4)),
        cost_estimate=pl.CostEstimate(
            flops=4 * local * rows * features * hidden,
            bytes_accessed=4 * local * features * hidden,
            transcendentals=local * rows * hidden,
        ),
    )(pick, gates, first, *flat(tokens), vmem(wg), vmem(wu))


def back_kernel(local, counts, place_ref, first_ref, *refs):
    token_refs, refs = split(refs, counts)
    wd_ref, a_ref, b_ref, _, _, hg_ref, hu_ref, gs, weight, sems = refs
    hidden = wd_ref.shape[1]
    cols = hidden // 2
    held = weight.shape[0]

    def fetch(e, i):
        part = pl.ds(i * cols, cols)
        slot = lax.rem(e, held)
        return pltpu.make_async_copy(wd_ref.at[e, part], weight.at[slot, part], sems.at[slot, i])

    for e in range(held):
        for i in range(2):
            fetch(e, i).start()
    gather_columns(local, place_ref, token_refs, 1, gs)

    @pl.loop(0, local)
    def _(e):
        rows = jnp.concatenate([first_ref[e], gs[e]], axis=1)
        for i in range(2):
            part = slice(i * cols, (i + 1) * cols)
            fetch(e, i).wait()
            back = dot(weight[lax.rem(e, held), part, :], rows)
            hg_ref[e, part, :] = (back * a_ref[e, part, :]).astype(jnp.bfloat16)
            hu_ref[e, part, :] = (back * b_ref[e, part, :]).astype(jnp.bfloat16)

            @pl.when(e + held < local)
            def _():
                fetch(e + held, i).start()


def back(n, place, first, tokens, wd, a, b, wg, wu):
    local, hidden, features = wd.shape
    rows = n * SLOT
    shape = jax.ShapeDtypeStruct((local, hidden, rows), jnp.bfloat16)
    return pl.pallas_call(
        functools.partial(back_kernel, local, sizes(tokens)),
        in_specs=[INSIDE] * (2 + len(flat(tokens))) + [OUTSIDE] + [INSIDE] * 4,
        out_shape=[shape, shape],
        scratch_shapes=[
            pltpu.VMEM((local, features, rows - 2 * SLOT), jnp.bfloat16),
            pltpu.VMEM((min(local, 2), hidden, features), jnp.bfloat16),
            pltpu.SemaphoreType.DMA((min(local, 2), 2)),
        ],
        compiler_params=params(BACK_MIB * max(1, n // 4)),
        cost_estimate=pl.CostEstimate(
            flops=2 * local * rows * features * hidden,
            bytes_accessed=2 * local * features * hidden,
            transcendentals=0,
        ),
    )(place, first, *flat(tokens), hbm(wd), a, b, vmem(wg), vmem(wu))


def out_kernel(n, local, orders, chunk, place_ref, hg_ref, hu_ref, wg_ref, wu_ref, *rest):
    outs, rows_ref = rest[:-1], rest[-1]
    wide = 2 * SLOT
    cols = wg_ref.shape[1] // CHUNKS
    part = slice(chunk * cols, (chunk + 1) * cols)
    for e in range(local):
        rows = dot(wg_ref[e, part, :], hg_ref[e]) + dot(wu_ref[e, part, :], hu_ref[e])
        rows = rows.astype(jnp.bfloat16)
        for p in range(n // 2):
            rows_ref[p, :, e * wide : (e + 1) * wide] = rows[:, p * wide : (p + 1) * wide]
    tokens = place_ref.shape[1] // 2
    for p in range(n // 2):
        total = dot(place_ref[p], rows_ref[p], NT)
        for out_ref, order in zip(outs, orders):
            for i, g in enumerate(order):
                if g // 2 == p:
                    mine = total[g % 2 * tokens : (g % 2 + 1) * tokens, :]
                    out_ref[i] = mine.astype(out_ref.dtype)


def partial_sums(n, orders, chunk, place, hg, hu, wg, wu):
    local, features, hidden = wg.shape
    tokens = place.shape[1] // 2
    rows = n * SLOT
    cols = features // CHUNKS
    shapes = [(len(order), tokens, cols) for order in orders]
    types = [jnp.float32] + [jnp.bfloat16] * (len(orders) - 1)
    return pl.pallas_call(
        functools.partial(out_kernel, n, local, orders, chunk),
        out_shape=[jax.ShapeDtypeStruct(s, t) for s, t in zip(shapes, types)],
        scratch_shapes=[pltpu.VMEM((n // 2, cols, 2 * SLOT * local), jnp.bfloat16)],
        compiler_params=params(OUT_MIB * max(1, n // 4)),
        cost_estimate=pl.CostEstimate(
            flops=local * rows * cols * hidden,
            bytes_accessed=local * cols * hidden,
            transcendentals=0,
        ),
    )(place, hg, hu, vmem(wg), vmem(wu))


def sum_kernel(*refs):
    parts, out_ref = refs[:-1], refs[-1]
    each = len(parts) // CHUNKS
    cols = out_ref.shape[1] // CHUNKS
    for c in range(CHUNKS):
        own, *others = parts[c * each : (c + 1) * each]
        total = own[0]
        for other in others:
            total += other[0].astype(jnp.float32)
        out_ref[:, c * cols : (c + 1) * cols] = total.astype(jnp.bfloat16)


def body(axis, saved_input, grad_out, routes, route_gates, gate_proj, up_proj, down_proj):
    n = lax.axis_size(axis)
    local = gate_proj.shape[0]
    experts = n * local
    tokens, features = saved_input.shape

    def swap(array, k):
        return lax.ppermute(array, axis, [(i, i ^ k) for i in range(n)])

    table = rank_table(routes.T, route_gates.T, experts)
    tables = [table] + [swap(table, k) for k in range(1, n)]
    pick, place, gates = slots(axis, n, local, tables)
    gate_proj, up_proj, done = load((gate_proj, up_proj), table)
    if n == 4:
        x_near = [swap(saved_input, 1), swap(saved_input, 2)]
        upper, lower = relay_parts(x_near, [done, place])
        sent = passed(grad_out, upper)
        x_blocks = [[saved_input], *[[x] for x in x_near], [swap(upper, 2), swap(lower, 1)]]
        g_near = [swap(sent, 1), swap(sent, 2)]
    else:
        x_blocks = [[saved_input]] + [[swap(saved_input, k)] for k in range(1, n)]
        sent = grad_out
    x_first = early_rows(local, pick, x_blocks[:2], sent)
    a, b = pre(n, pick, gates, x_first, x_blocks[2:], gate_proj, up_proj)
    if n == 4:
        upper, lower = relay_parts(g_near, [a])
        g_blocks = [[sent], *[[g] for g in g_near], [swap(upper, 2), swap(lower, 1)]]
    else:
        g_blocks = [[grad_out]] + [[swap(grad_out, k)] for k in range(1, n)]
        upper = a
    g_first = early_columns(local, place, g_blocks[:2], upper)
    hg, hu = back(n, place, g_first, g_blocks[2:], down_proj, a, b, gate_proj, up_proj)
    parts = []
    for chunk in range(CHUNKS):
        if n == 4:
            first, last = (1, 2) if chunk % 2 == 0 else (2, 1)
            orders = ((0,), (first, 3), (last,))
            own, two, one = partial_sums(n, orders, chunk, place, hg, hu, gate_proj, up_proj)
            two = swap(two, first)
            mixed = (two[1:2].astype(jnp.float32) + one.astype(jnp.float32)).astype(jnp.bfloat16)
            parts += [own, two[:1], swap(mixed, last)]
        else:
            orders = tuple((k,) for k in range(n))
            own, *others = partial_sums(n, orders, chunk, place, hg, hu, gate_proj, up_proj)
            parts += [own] + [swap(other, k + 1) for k, other in enumerate(others)]
    return pl.pallas_call(
        sum_kernel,
        out_shape=jax.ShapeDtypeStruct((tokens, features), jnp.bfloat16),
        compiler_params=params(8),
    )(*parts)


def solution(mesh):
    tokens = P(("dp", "expert"), None)
    weights = P("expert", None, None)
    return jax.shard_map(
        functools.partial(body, "expert"),
        mesh=mesh,
        in_specs=(tokens, tokens, tokens, tokens, weights, weights, weights),
        out_specs=tokens,
        check_vma=False,
    )
```

```python
import functools

import jax
import jax.numpy as jnp
from jax import lax
from jax.experimental import pallas as pl
from jax.experimental.pallas import tpu as pltpu
from jax.sharding import PartitionSpec as P

CAP = 56
SLOT = 64
UNUSED = 200.0
MIB = 1 << 20
CHUNKS = 4
PRE_MIB = 6
BACK_MIB = 10
OUT_MIB = 4

NT = (((1,), (1,)), ((), ()))


def dot(a, b, dims=(((1,), (0,)), ((), ()))):
    return lax.dot_general(a, b, dims, preferred_element_type=jnp.float32)


def params(limit):
    return pltpu.CompilerParams(vmem_limit_bytes=limit * MIB)


def rank_kernel(experts, routes_ref, gates_ref, out_ref):
    top, tokens = routes_ref.shape
    chosen = routes_ref[...].astype(jnp.float32)
    gates = gates_ref[...].astype(jnp.float32)
    label = lax.broadcasted_iota(jnp.int32, (experts, tokens), 0).astype(jnp.float32)
    hits = [(chosen[k : k + 1, :] == label).astype(jnp.float32) for k in range(top)]
    before = lax.broadcasted_iota(jnp.int32, (tokens, tokens), 0)
    after = lax.broadcasted_iota(jnp.int32, (tokens, tokens), 1)
    earlier = (before < after).astype(jnp.bfloat16)
    base = jnp.zeros((experts, 1), jnp.float32)
    rank = jnp.zeros((experts, tokens), jnp.float32)
    taken = jnp.zeros((experts, tokens), jnp.float32)
    gate = jnp.zeros((experts, tokens), jnp.float32)
    for k in range(top):
        inside = dot(hits[k].astype(jnp.bfloat16), earlier)
        rank += hits[k] * (inside + base)
        taken += hits[k]
        gate += hits[k] * gates[k : k + 1, :]
        base += jnp.sum(hits[k], axis=1, keepdims=True)
    rank = jnp.where((taken > 0.5) & (rank < CAP), rank, UNUSED)
    out_ref[:experts, :] = rank.astype(jnp.bfloat16)
    out_ref[experts:, :] = gate.astype(jnp.bfloat16)


def rank_table(routes, gates, experts):
    tokens = routes.shape[1]
    return pl.pallas_call(
        functools.partial(rank_kernel, experts),
        out_shape=jax.ShapeDtypeStruct((2 * experts, tokens), jnp.bfloat16),
    )(routes, gates)


def slots_kernel(axis, n, local, *refs):
    table_refs, (pick_ref, place_ref, gate_ref) = refs[:n], refs[n:]
    experts = n * local
    tokens = table_refs[0].shape[1]
    wide = 2 * SLOT
    me = lax.axis_index(axis)
    row = lax.broadcasted_iota(jnp.int32, (2 * experts, tokens), 0)
    slot = lax.broadcasted_iota(jnp.int32, (wide, tokens), 0).astype(jnp.float32)
    for p in range(n // 2):
        tables = [table_refs[2 * p + q][...].astype(jnp.float32) for q in range(2)]
        for j in range(local):
            e = me * local + j
            down = slice(j * wide, (j + 1) * wide)
            gates = jnp.zeros((8, wide), jnp.float32)
            for q in range(2):
                rank = jnp.sum(jnp.where(row == e, tables[q], 0.0), axis=0, keepdims=True)
                gate = jnp.sum(jnp.where(row == e + experts, tables[q], 0.0), axis=0, keepdims=True)
                pick = (slot == rank + q * SLOT).astype(jnp.float32)
                place = pick.T.astype(jnp.bfloat16)
                across = slice(q * tokens, (q + 1) * tokens)
                pick_ref[p, down, across] = pick.astype(jnp.bfloat16)
                place_ref[p, across, down] = place
                gates += dot(jnp.broadcast_to(gate, (8, tokens)).astype(jnp.bfloat16), place)
            gate_ref[j, :, p * wide : (p + 1) * wide] = gates


def slots(axis, n, local, tables):
    tokens = tables[0].shape[1]
    across, down = 2 * tokens, 2 * SLOT * local
    return pl.pallas_call(
        functools.partial(slots_kernel, axis, n, local),
        out_shape=[
            jax.ShapeDtypeStruct((n // 2, down, across), jnp.bfloat16),
            jax.ShapeDtypeStruct((n // 2, across, down), jnp.bfloat16),
            jax.ShapeDtypeStruct((local, 8, n * SLOT), jnp.float32),
        ],
        compiler_params=params(4 * max(1, n // 8)),
    )(*tables)


def gather_rows(local, pick_ref, token_refs, first, out):
    wide = 2 * SLOT
    features = out.shape[2]
    cols = features // 4
    for p in range(len(token_refs) // 2):
        refs = [ref for pair in token_refs[2 * p : 2 * p + 2] for ref in pair]
        for d in range(0, features, cols):
            part = slice(d, d + cols)
            tokens = jnp.concatenate([ref[:, part] for ref in refs], axis=0)
            rows = dot(pick_ref[first + p], tokens).astype(jnp.bfloat16)
            for j in range(local):
                out[j, p * wide : (p + 1) * wide, part] = rows[j * wide : (j + 1) * wide, :]


def gather_columns(local, place_ref, token_refs, first, out):
    wide = 2 * SLOT
    features = out.shape[1]
    size = features // 4
    for p in range(len(token_refs) // 2):
        refs = [ref for pair in token_refs[2 * p : 2 * p + 2] for ref in pair]
        for d in range(0, features, size):
            part = slice(d, d + size)
            tokens = jnp.concatenate([ref[:, part] for ref in refs], axis=0)
            columns = dot(tokens.T, place_ref[first + p]).astype(jnp.bfloat16)
            for j in range(local):
                out[j, part, p * wide : (p + 1) * wide] = columns[:, j * wide : (j + 1) * wide]


def split(refs, counts):
    parts, first = [], 0
    for count in counts:
        parts.append(refs[first : first + count])
        first += count
    return parts, refs[first:]


def flat(groups):
    return [block for blocks in groups for block in blocks]


def sizes(groups):
    return [len(blocks) for blocks in groups]


INSIDE = pl.BlockSpec(memory_space=pltpu.VMEM)
OUTSIDE = pl.BlockSpec(memory_space=pltpu.HBM)
ANYWHERE = pl.BlockSpec(memory_space=pl.ANY)


def vmem(array):
    return pltpu.with_memory_space_constraint(array, pltpu.VMEM)


def hbm(array):
    return pltpu.with_memory_space_constraint(array, pltpu.HBM)


def fetches(source, result, sems):
    return [pltpu.make_async_copy(source.at[e], result.at[e], sems.at[e]) for e in range(source.shape[0])]


def load_kernel(count, *refs):
    sources, (*results, done_ref, sems) = refs[:count], refs[count + 1 :]
    copies = [
        pltpu.make_async_copy(source.at[e], result.at[e], sems.at[i, e])
        for i, (source, result) in enumerate(zip(sources, results))
        for e in range(source.shape[0])
    ]
    for copy in copies:
        copy.start()
    for copy in copies:
        copy.wait()
    done_ref[...] = jnp.zeros_like(done_ref)


def load(arrays, after):
    count = len(arrays)
    return pl.pallas_call(
        functools.partial(load_kernel, count),
        in_specs=[OUTSIDE] * count + [pl.BlockSpec(memory_space=pl.ANY)],
        out_specs=[pl.BlockSpec(memory_space=pltpu.VMEM)] * (count + 1),
        out_shape=[pltpu.VMEM(w.shape, w.dtype) for w in arrays]
        + [jax.ShapeDtypeStruct((8, 128), jnp.float32)],
        scratch_shapes=[pltpu.SemaphoreType.DMA((count, arrays[0].shape[0]))],
        compiler_params=params(1),
        cost_estimate=pl.CostEstimate(
            flops=0, bytes_accessed=4 * count * arrays[0].size, transcendentals=0
        ),
    )(*[pltpu.with_memory_space_constraint(w, pltpu.HBM) for w in arrays], after)


def rows_kernel(local, counts, pick_ref, *refs):
    token_refs, (_, out_ref) = split(refs, counts)
    gather_rows(local, pick_ref, token_refs, 0, out_ref)


def early_rows(local, pick, tokens, after):
    features = tokens[0][0].shape[1]
    return pl.pallas_call(
        functools.partial(rows_kernel, local, sizes(tokens)),
        in_specs=[INSIDE] * (1 + len(flat(tokens))) + [ANYWHERE],
        out_shape=jax.ShapeDtypeStruct((local, 2 * SLOT, features), jnp.bfloat16),
        compiler_params=params(4),
    )(pick, *flat(tokens), after)


def columns_kernel(local, counts, place_ref, *refs):
    token_refs, (_, out_ref) = split(refs, counts)
    gather_columns(local, place_ref, token_refs, 0, out_ref)


def early_columns(local, place, tokens, after):
    features = tokens[0][0].shape[1]
    return pl.pallas_call(
        functools.partial(columns_kernel, local, sizes(tokens)),
        in_specs=[INSIDE] * (1 + len(flat(tokens))) + [ANYWHERE],
        out_shape=jax.ShapeDtypeStruct((local, features, 2 * SLOT), jnp.bfloat16),
        compiler_params=params(4),
    )(place, *flat(tokens), after)


def relay_kernel(x_ref, y_ref, *refs):
    upper_ref, lower_ref = refs[-2:]
    half = upper_ref.shape[0]
    upper_ref[...] = x_ref[:half, :]
    lower_ref[...] = y_ref[half:, :]


def relay_parts(beside, after):
    tokens, features = beside[0].shape
    inside, anywhere = pl.BlockSpec(memory_space=pltpu.VMEM), pl.BlockSpec(memory_space=pl.ANY)
    half = jax.ShapeDtypeStruct((tokens // 2, features), beside[0].dtype)
    return pl.pallas_call(
        relay_kernel,
        in_specs=[inside] * 2 + [anywhere] * len(after),
        out_shape=[half, half],
        compiler_params=params(4),
    )(*beside, *after)


def pass_kernel(array_ref, _, copy_ref):
    copy_ref[...] = array_ref[...]


def passed(array, after):
    return pl.pallas_call(
        pass_kernel,
        in_specs=[pl.BlockSpec(memory_space=pltpu.VMEM), pl.BlockSpec(memory_space=pl.ANY)],
        out_shape=jax.ShapeDtypeStruct(array.shape, array.dtype),
        compiler_params=params(4),
    )(array, after)


def pre_kernel(local, counts, pick_ref, gate_ref, first_ref, *refs):
    token_refs, refs = split(refs, counts)
    wg_ref, wu_ref, a_ref, b_ref, xs = refs
    hidden = wg_ref.shape[2]
    cols = hidden // 2
    gather_rows(local, pick_ref, token_refs, 1, xs)

    for e in range(local):
        rows = jnp.concatenate([first_ref[e], xs[e]], axis=0)
        gates = gate_ref[e][:1, :]
        for f in range(0, hidden, cols):
            part = slice(f, f + cols)
            gate_pre = dot(rows, wg_ref[e, :, part])
            up_pre = dot(rows, wu_ref[e, :, part])
            sig = jax.nn.sigmoid(gate_pre)
            a_ref[e, part, :] = (sig * up_pre * (1.0 + gate_pre * (1.0 - sig))).T * gates
            b_ref[e, part, :] = (sig * gate_pre).T * gates


def pre(n, pick, gates, first, tokens, wg, wu):
    local, features, hidden = wg.shape
    rows = n * SLOT
    return pl.pallas_call(
        functools.partial(pre_kernel, local, sizes(tokens)),
        in_specs=[INSIDE] * (5 + len(flat(tokens))),
        out_shape=[
            jax.ShapeDtypeStruct((local, hidden, rows), jnp.float32),
            jax.ShapeDtypeStruct((local, hidden, rows), jnp.float32),
        ],
        scratch_shapes=[pltpu.VMEM((local, rows - 2 * SLOT, features), jnp.bfloat16)],
        compiler_params=params(PRE_MIB * max(1, n // 4)),
        cost_estimate=pl.CostEstimate(
            flops=4 * local * rows * features * hidden,
            bytes_accessed=4 * local * features * hidden,
            transcendentals=local * rows * hidden,
        ),
    )(pick, gates, first, *flat(tokens), vmem(wg), vmem(wu))


def back_kernel(local, counts, place_ref, first_ref, *refs):
    token_refs, refs = split(refs, counts)
    wd_ref, a_ref, b_ref, _, _, hg_ref, hu_ref, gs, weight, sems = refs
    hidden = wd_ref.shape[1]
    cols = hidden // 2
    held = weight.shape[0]

    def fetch(e, i):
        part = pl.ds(i * cols, cols)
        slot = e % held
        return pltpu.make_async_copy(wd_ref.at[e, part], weight.at[slot, part], sems.at[slot, i])

    for e in range(held):
        for i in range(2):
            fetch(e, i).start()
    gather_columns(local, place_ref, token_refs, 1, gs)

    for e in range(local):
        rows = jnp.concatenate([first_ref[e], gs[e]], axis=1)
        for i in range(2):
            part = slice(i * cols, (i + 1) * cols)
            fetch(e, i).wait()
            back = dot(weight[e % held, part, :], rows)
            hg_ref[e, part, :] = (back * a_ref[e, part, :]).astype(jnp.bfloat16)
            hu_ref[e, part, :] = (back * b_ref[e, part, :]).astype(jnp.bfloat16)

            if e + held < local:
                fetch(e + held, i).start()


def back(n, place, first, tokens, wd, a, b, wg, wu):
    local, hidden, features = wd.shape
    rows = n * SLOT
    shape = jax.ShapeDtypeStruct((local, hidden, rows), jnp.bfloat16)
    return pl.pallas_call(
        functools.partial(back_kernel, local, sizes(tokens)),
        in_specs=[INSIDE] * (2 + len(flat(tokens))) + [OUTSIDE] + [INSIDE] * 4,
        out_shape=[shape, shape],
        scratch_shapes=[
            pltpu.VMEM((local, features, rows - 2 * SLOT), jnp.bfloat16),
            pltpu.VMEM((min(local, 2), hidden, features), jnp.bfloat16),
            pltpu.SemaphoreType.DMA((min(local, 2), 2)),
        ],
        compiler_params=params(BACK_MIB * max(1, n // 4)),
        cost_estimate=pl.CostEstimate(
            flops=2 * local * rows * features * hidden,
            bytes_accessed=2 * local * features * hidden,
            transcendentals=0,
        ),
    )(place, first, *flat(tokens), hbm(wd), a, b, vmem(wg), vmem(wu))


def out_kernel(n, local, orders, chunk, place_ref, hg_ref, hu_ref, wg_ref, wu_ref, *rest):
    outs, rows_ref = rest[:-1], rest[-1]
    wide = 2 * SLOT
    cols = wg_ref.shape[1] // CHUNKS
    part = slice(chunk * cols, (chunk + 1) * cols)
    for e in range(local):
        rows = dot(wg_ref[e, part, :], hg_ref[e]) + dot(wu_ref[e, part, :], hu_ref[e])
        rows = rows.astype(jnp.bfloat16)
        for p in range(n // 2):
            rows_ref[p, :, e * wide : (e + 1) * wide] = rows[:, p * wide : (p + 1) * wide]
    tokens = place_ref.shape[1] // 2
    for p in range(n // 2):
        total = dot(place_ref[p], rows_ref[p], NT)
        for out_ref, order in zip(outs, orders):
            for i, g in enumerate(order):
                if g // 2 == p:
                    mine = total[g % 2 * tokens : (g % 2 + 1) * tokens, :]
                    out_ref[i] = mine.astype(out_ref.dtype)


def partial_sums(n, orders, chunk, place, hg, hu, wg, wu):
    local, features, hidden = wg.shape
    tokens = place.shape[1] // 2
    rows = n * SLOT
    cols = features // CHUNKS
    shapes = [(len(order), tokens, cols) for order in orders]
    types = [jnp.float32] + [jnp.bfloat16] * (len(orders) - 1)
    return pl.pallas_call(
        functools.partial(out_kernel, n, local, orders, chunk),
        out_shape=[jax.ShapeDtypeStruct(s, t) for s, t in zip(shapes, types)],
        scratch_shapes=[pltpu.VMEM((n // 2, cols, 2 * SLOT * local), jnp.bfloat16)],
        compiler_params=params(OUT_MIB * max(1, n // 4)),
        cost_estimate=pl.CostEstimate(
            flops=local * rows * cols * hidden,
            bytes_accessed=local * cols * hidden,
            transcendentals=0,
        ),
    )(place, hg, hu, vmem(wg), vmem(wu))


def sum_kernel(*refs):
    parts, out_ref = refs[:-1], refs[-1]
    each = len(parts) // CHUNKS
    cols = out_ref.shape[1] // CHUNKS
    for c in range(CHUNKS):
        own, *others = parts[c * each : (c + 1) * each]
        total = own[0]
        for other in others:
            total += other[0].astype(jnp.float32)
        out_ref[:, c * cols : (c + 1) * cols] = total.astype(jnp.bfloat16)


def body(axis, saved_input, grad_out, routes, route_gates, gate_proj, up_proj, down_proj):
    n = lax.axis_size(axis)
    local = gate_proj.shape[0]
    experts = n * local
    tokens, features = saved_input.shape

    def swap(array, k):
        return lax.ppermute(array, axis, [(i, i ^ k) for i in range(n)])

    table = rank_table(routes.T, route_gates.T, experts)
    tables = [table] + [swap(table, k) for k in range(1, n)]
    pick, place, gates = slots(axis, n, local, tables)
    gate_proj, up_proj, done = load((gate_proj, up_proj), table)
    if n == 4:
        x_near = [swap(saved_input, 1), swap(saved_input, 2)]
        upper, lower = relay_parts(x_near, [done, place])
        sent = passed(grad_out, upper)
        x_blocks = [[saved_input], *[[x] for x in x_near], [swap(upper, 2), swap(lower, 1)]]
        g_near = [swap(sent, 1), swap(sent, 2)]
    else:
        x_blocks = [[saved_input]] + [[swap(saved_input, k)] for k in range(1, n)]
        sent = grad_out
    x_first = early_rows(local, pick, x_blocks[:2], sent)
    a, b = pre(n, pick, gates, x_first, x_blocks[2:], gate_proj, up_proj)
    if n == 4:
        upper, lower = relay_parts(g_near, [a])
        g_blocks = [[sent], *[[g] for g in g_near], [swap(upper, 2), swap(lower, 1)]]
    else:
        g_blocks = [[grad_out]] + [[swap(grad_out, k)] for k in range(1, n)]
        upper = a
    g_first = early_columns(local, place, g_blocks[:2], upper)
    hg, hu = back(n, place, g_first, g_blocks[2:], down_proj, a, b, gate_proj, up_proj)
    parts = []
    for chunk in range(CHUNKS):
        if n == 4:
            first, last = (1, 2) if chunk % 2 == 0 else (2, 1)
            orders = ((0,), (first, 3), (last,))
            own, two, one = partial_sums(n, orders, chunk, place, hg, hu, gate_proj, up_proj)
            two = swap(two, first)
            mixed = (two[1:2].astype(jnp.float32) + one.astype(jnp.float32)).astype(jnp.bfloat16)
            parts += [own, two[:1], swap(mixed, last)]
        else:
            orders = tuple((k,) for k in range(n))
            own, *others = partial_sums(n, orders, chunk, place, hg, hu, gate_proj, up_proj)
            parts += [own] + [swap(other, k + 1) for k, other in enumerate(others)]
    return pl.pallas_call(
        sum_kernel,
        out_shape=jax.ShapeDtypeStruct((tokens, features), jnp.bfloat16),
        compiler_params=params(8),
    )(*parts)


def solution(mesh):
    tokens = P(("dp", "expert"), None)
    weights = P("expert", None, None)
    return jax.shard_map(
        functools.partial(body, "expert"),
        mesh=mesh,
        in_specs=(tokens, tokens, tokens, tokens, weights, weights, weights),
        out_specs=tokens,
        check_vma=False,
    )
```
